32 devices in a mesh: rep: 4 (over x, core), shard: 8 (over z, y).
Axes of the slice: x: 2, y: 2, z: 4, core: 2. Of those that a mesh axis runs over, the one named last changes fastest.
Arguments:
- tokens: bfloat16 [8192, 1536], P(('rep', 'shard')), may hold values from -6 to 6
- segments: int32 [32, 256], P(('rep', 'shard')), may hold values from 0 to 2, never falling along the last dimension, each value on 1 to 128 neighbouring positions
- routes: int32 [8192, 8], P(('rep', 'shard')), may hold values from 0 to 15, all different within a row; in each aligned block of 256 rows (0 to 255, 256 to 511, ...) at most 160 rows name the same one
- cotangent: bfloat16 [8192, 1536], P(('rep', 'shard')), may hold values from -6 to 6
- wqkv: float32 [1536, 2560], P('shard'), may hold values from -0.15625 to 0.15625
- wqkv_first: float32 [1536, 2560], P('shard')
- wqkv_second: float32 [1536, 2560], P('shard'), may hold values from 1720.32 to 6881.28
- wo: float32 [1536, 1536], P('shard'), may hold values from -1.25 to 1.25
- wo_first: float32 [1536, 1536], P('shard')
- wo_second: float32 [1536, 1536], P('shard'), may hold values from 6.22592 to 24.576
- router: float32 [1536, 16], P('shard'), may hold values from -0.078125 to 0.078125
- router_first: float32 [1536, 16], P('shard')
- router_second: float32 [1536, 16], P('shard'), may hold values from 27607.04 to 110592
- w_in: float32 [16, 1536, 1024], P(None, 'shard'), may hold values from -0.15625 to 0.15625
- w_in_first: float32 [16, 1536, 1024], P(None, 'shard')
- w_in_second: float32 [16, 1536, 1024], P(None, 'shard'), may hold values from 52.4288 to 212.992
- w_out: float32 [16, 512, 1536], P(None, 'shard'), may hold values from -1 to 1
- w_out_first: float32 [16, 512, 1536], P(None, 'shard')
- w_out_second: float32 [16, 512, 1536], P(None, 'shard'), may hold values from 1.212416 to 4.83328
- gains: float32 [2, 1536], P(None, 'shard'), may hold values from 0.5 to 1.5
- gains_first: float32 [2, 1536], P(None, 'shard')
- gains_second: float32 [2, 1536], P(None, 'shard'), may hold values from 1720.32 to 6881.28
Outputs:
- mixed: bfloat16 [8192, 1536], P(('rep', 'shard'))
- tokens_grad: float32 [8192, 1536], P(('rep', 'shard'))
- wqkv_first_new: float32 [1536, 2560], P('shard')
- wqkv_second_new: float32 [1536, 2560], P('shard')
- wqkv_new: float32 [1536, 2560], P('shard')
- wo_first_new: float32 [1536, 1536], P('shard')
- wo_second_new: float32 [1536, 1536], P('shard')
- wo_new: float32 [1536, 1536], P('shard')
- router_first_new: float32 [1536, 16], P('shard')
- router_second_new: float32 [1536, 16], P('shard')
- router_new: float32 [1536, 16], P('shard')
- w_in_first_new: float32 [16, 1536, 1024], P(None, 'shard')
- w_in_second_new: float32 [16, 1536, 1024], P(None, 'shard')
- w_in_new: float32 [16, 1536, 1024], P(None, 'shard')
- w_out_first_new: float32 [16, 512, 1536], P(None, 'shard')
- w_out_second_new: float32 [16, 512, 1536], P(None, 'shard')
- w_out_new: float32 [16, 512, 1536], P(None, 'shard')
- gains_first_new: float32 [2, 1536], P(None, 'shard')
- gains_second_new: float32 [2, 1536], P(None, 'shard')
- gains_new: float32 [2, 1536], P(None, 'shard')
The draws below stay inside these ranges and needn't reach their ends.
Inputs may be any that keep to these rules, and one draw needn't show every extreme that they name: `segments`: numbers never fall along a sequence; a document holds 1 to half of 256 positions, and some document of each draw holds exactly half. `routes`: each token names 8 different experts; among the tokens of one sequence no expert is named more than 160 times, and in every draw some expert is named exactly 160 times in some sequence.
All inputs are finite; a program needn't handle non-finite values.
Results may differ from the reference program's by a relative error of at most 0.024.
Values may be sent and summed in bfloat16 or wider, within the bound.
A program may use at most 256 MiB of HBM per device.

```python
import math
import jax
import jax.numpy as jnp
import numpy as np
from jax import lax

D = 1536
H = 512
HEADS = 24
KV_HEADS = 8
HD = 64
E = 16
TOP = 8
STEP = 10
SEQ = 256
QD = 1536
KVD = 512
CAP = 160
SEQS = 32
TOKENS = 8192


def first_moment(key, shape, factor):
    return factor * jnp.sqrt(TOKENS * 1.0) * jax.random.normal(key, shape, jnp.float32)


def draw_wqkv_first(key, part):
    key = jax.random.fold_in(key, 11)
    return first_moment(key, (D, QD + 2 * KVD), 0.222)


def draw_wo_first(key, part):
    key = jax.random.fold_in(key, 12)
    return first_moment(key, (QD, D), 0.0133)


def draw_router_first(key, part):
    key = jax.random.fold_in(key, 13)
    return first_moment(key, (D, E), 0.888)


def draw_w_in_first(key, part):
    key = jax.random.fold_in(key, 14)
    return first_moment(key, (E, D, 2 * H), 0.039)


def draw_w_out_first(key, part):
    key = jax.random.fold_in(key, 15)
    return first_moment(key, (E, H, D), 0.0059)


def draw_gains_first(key, part):
    key = jax.random.fold_in(key, 16)
    return first_moment(key, (2, D), 0.222)


def level_of(own_key, dims, cuts, smallest, top_value):
    level, own = 1.0, jax.random.fold_in(own_key, 6)
    for position, blocks in cuts:
        draws = jnp.exp(jax.random.uniform(jax.random.fold_in(own, position), (blocks,), jnp.float32, smallest / len(cuts), top_value / len(cuts)))
        level = level * jnp.repeat(draws, dims[position] // blocks).reshape([-1 if axis == position else 1 for axis in range(len(dims))])
    return level


def split_up(number_of, total, most, skew):
    weights = [(1 << 20) // math.isqrt(grade ** skew) + 1 for grade in range(2, number_of + 1)]
    surplus, counts = total - most - (number_of - 1), [1] * (number_of - 1)
    while surplus > 0:
        free = [i for i in range(number_of - 1) if counts[i] < most]
        mass, left = sum([weights[i] for i in free]), surplus
        for i in free:
            extra = min(most - counts[i], max(1, left * weights[i] // mass), surplus)
            counts[i] = counts[i] + extra
            surplus = surplus - extra
    return np.array([most] + counts)


def uneven_parts(key, amount, total, limit, lean):
    if amount == 2:
        one = jax.random.randint(key, (), max(1, total - limit), min(limit, total - 1) + 1)
        return jnp.stack([one, total - one])
    lengths = jnp.asarray(split_up(amount, total, limit, lean), jnp.int32)
    twos = (amount - 1) // 2
    donor, taker = lengths[1:1 + 2 * twos:2], lengths[2:2 + 2 * twos:2]
    slack = jnp.minimum(donor - 1, limit - taker)
    moved = jax.random.randint(jax.random.fold_in(key, 1), (twos,), 0, 1 << 20) % (slack + 1)
    lengths = lengths.at[1:1 + 2 * twos:2].set(donor - moved).at[2:2 + 2 * twos:2].set(taker + moved)
    return lengths[jax.random.permutation(jax.random.fold_in(key, 2), amount)]


def assign_block(key, own, number, rows, amount, top, limit, skew):
    sequence = jax.random.permutation(key, amount)
    heavy_load, usual = load_shares(amount, rows * top, limit, skew, True), load_shares(amount, rows * top, limit, skew, False)
    places = jnp.arange(amount)

    def named(tallies, turn):
        used = int((tallies > 0).sum())
        fixed = max(1, used // 4)
        moved = fixed + (places - fixed + turn * (used - fixed)) % max(1, amount - fixed)
        return jnp.zeros((amount,), jnp.int32).at[sequence[jnp.where(places < fixed, places, moved)]].set(jnp.asarray(tallies, jnp.int32))

    tallies = jnp.where(number % 4 == 0, named(heavy_load, number // 4), named(usual, number - number // 4 - 1))
    mixed = jax.random.permutation(jax.random.fold_in(own, 3), amount)
    giver, receiver = mixed[0:amount // 2 * 2:2], mixed[1:amount // 2 * 2:2]
    slack = jnp.minimum(tallies[giver] - 1, limit - tallies[receiver]) // 2
    slack = jnp.where((giver == sequence[0]) | (receiver == sequence[0]) | (tallies[receiver] == 0), 0, jnp.maximum(slack, 0))
    moved = jax.random.randint(jax.random.fold_in(own, 4), (amount // 2,), 0, 1 << 20) % (slack + 1)
    tallies = tallies.at[giver].add(-moved).at[receiver].add(moved)
    labels = jnp.searchsorted(jnp.cumsum(tallies), jnp.arange(rows * top), side="right").astype(jnp.int32)
    grid = labels.reshape(top, rows).T
    grid = grid[jax.random.permutation(jax.random.fold_in(own, 1), rows)]
    turn = jax.random.randint(jax.random.fold_in(own, 2), (rows, 1), 0, top)
    return jnp.take_along_axis(grid, (jnp.arange(top)[None, :] + turn) % top, axis=1)


def load_shares(amount, total, most, lean, full):
    portions = [(1 << 20) // math.isqrt(standing ** lean) + 1 for standing in range(1, amount + 1)]
    largest = most if full else min(most, max(-(-total // amount), total * portions[0] // sum(portions)))
    least = 1 if total - largest >= amount - 1 else 0
    counts, spare = [largest] + [least] * (amount - 1), total - largest - least * (amount - 1)
    while spare > 0:
        free = [i for i in range(1, amount) if counts[i] < largest] or [i for i in range(1, amount) if counts[i] < most]
        whole, remaining = sum([portions[i] for i in free]), spare
        for i in free:
            more = min(most - counts[i], max(1, remaining * portions[i] // whole), spare)
            counts[i] = counts[i] + more
            spare = spare - more
    return np.array(counts)


def noise(key, extent, width, most, shards=(), kind=jnp.bfloat16):
    level = level_of(key, extent, shards, -0.22, 0.18) if shards else 1.0
    array = jax.random.normal(key, extent, jnp.float32) * width * level
    return jnp.minimum(jnp.maximum(array, -most), most).astype(kind)


def setup_inputs(seed: int = 0) -> dict:
    key_of = jax.random.split(jax.random.key(seed), 23)
    tokens = noise(key_of[0], (TOKENS, D), 1.0, 6.0, ((0, 32),))
    segments = jax.vmap(lambda own: jnp.searchsorted(jnp.cumsum(uneven_parts(own, 3, SEQ, SEQ // 2, 0)), jnp.arange(SEQ), side="right"))(jax.random.split(key_of[1], SEQS)).reshape((SEQS, SEQ)).astype(jnp.int32)
    routes_keys = jax.random.split(jax.random.fold_in(key_of[2], 1), TOKENS // SEQ)
    routes_turns = jax.random.permutation(jax.random.fold_in(key_of[2], 3), TOKENS // SEQ)
    routes = jax.vmap(lambda own, number: assign_block(jax.random.fold_in(key_of[2], 2), own, number, SEQ, E, TOP, CAP, 1))(routes_keys, routes_turns).reshape((TOKENS, TOP))
    cotangent = noise(key_of[3], (TOKENS, D), 1.0, 6.0, ((0, 32),))
    wqkv = noise(key_of[4], (D, QD + 2 * KVD), D ** -0.5, 0.15625, ((0, 8),), jnp.float32)
    wqkv_first = draw_wqkv_first(jax.random.fold_in(key_of[22], 71), 0)
    wqkv_second = jnp.clip(jnp.exp(math.log(6881.28) - 1.3862944 * jax.random.uniform(key_of[6], (D, QD + 2 * KVD), jnp.float32) ** level_of(key_of[6], (D, QD + 2 * KVD), ((0, 8),), -0.2, 0.2)), 1720.32, 6881.28)
    wo = noise(key_of[7], (QD, D), (QD // 64) ** -0.5, 1.25, ((0, 8),), jnp.float32)
    wo_first = draw_wo_first(jax.random.fold_in(key_of[22], 71), 0)
    wo_second = jnp.clip(jnp.exp(math.log(24.576) - 1.3730491 * jax.random.uniform(key_of[9], (QD, D), jnp.float32) ** level_of(key_of[9], (QD, D), ((0, 8),), -0.2, 0.2)), 6.22592, 24.576)
    router = noise(key_of[10], (D, E), (4 * D) ** -0.5, 0.078125, ((0, 8),), jnp.float32)
    router_first = draw_router_first(jax.random.fold_in(key_of[22], 71), 0)
    router_second = jnp.clip(jnp.exp(math.log(110592.0) - 1.387777 * jax.random.uniform(key_of[12], (D, E), jnp.float32) ** level_of(key_of[12], (D, E), ((0, 8),), -0.2, 0.2)), 27607.04, 110592.0)
    w_in = noise(key_of[13], (E, D, 2 * H), D ** -0.5, 0.15625, ((1, 8),), jnp.float32)
    w_in_first = draw_w_in_first(jax.random.fold_in(key_of[22], 71), 0)
    w_in_second = jnp.clip(jnp.exp(math.log(212.992) - 1.4017986 * jax.random.uniform(key_of[15], (E, D, 2 * H), jnp.float32) ** level_of(key_of[15], (E, D, 2 * H), ((1, 8),), -0.2, 0.2)), 52.4288, 212.992)
    w_out = noise(key_of[16], (E, H, D), (H // 16) ** -0.5, 1.0, ((1, 8),), jnp.float32)
    w_out_first = draw_w_out_first(jax.random.fold_in(key_of[22], 71), 0)
    w_out_second = jnp.clip(jnp.exp(math.log(4.83328) - 1.3829102 * jax.random.uniform(key_of[18], (E, H, D), jnp.float32) ** level_of(key_of[18], (E, H, D), ((1, 8),), -0.2, 0.2)), 1.212416, 4.83328)
    gains = jnp.clip(1.0 + 0.1 * jax.random.normal(key_of[19], (2, D), jnp.float32), 0.5, 1.5)
    gains_first = draw_gains_first(jax.random.fold_in(key_of[22], 71), 0)
    gains_second = jnp.clip(jnp.exp(math.log(6881.28) - 1.3862944 * jax.random.uniform(key_of[21], (2, D), jnp.float32) ** level_of(key_of[21], (2, D), ((1, 8),), -0.2, 0.2)), 1720.32, 6881.28)
    return dict(tokens=tokens, segments=segments, routes=routes, cotangent=cotangent, wqkv=wqkv, wqkv_first=wqkv_first, wqkv_second=wqkv_second, wo=wo, wo_first=wo_first, wo_second=wo_second, router=router, router_first=router_first, router_second=router_second, w_in=w_in, w_in_first=w_in_first, w_in_second=w_in_second, w_out=w_out, w_out_first=w_out_first, w_out_second=w_out_second, gains=gains, gains_first=gains_first, gains_second=gains_second)


@jax.custom_vjp
def low(v):
    return lax.optimization_barrier(v.astype(jnp.bfloat16)).astype(jnp.float32)

@jax.custom_vjp
def low_back(v):
    return v

def low_keep(v):
    return (low(v), None)

def low_pass(kept, grad):
    return (grad,)

def back_keep(v):
    return (v, None)

def back_low(kept, grad):
    return (low(grad),)
low.defvjp(low_keep, low_pass)
low_back.defvjp(back_keep, back_low)
HIGH = lax.Precision.HIGHEST
norm_eps = 1e-06
beta_one = 0.9
beta_two = 0.95
adam_eps = 1e-08
decay_rate = 0.1

def rms_norm(value, gain):
    scale = lax.rsqrt(lax.optimization_barrier(jnp.mean(value * value, axis=-1, keepdims=True)) + norm_eps)
    return value * scale * gain

def rotary(value):
    length = value.shape[0]
    halfway = value.shape[-1] // 2
    freqs = 10000.0 ** (-jnp.arange(halfway, dtype=jnp.float32) / halfway)
    angles = jnp.arange(length, dtype=jnp.float32)[:, None] * freqs[None, :]
    cosine = jnp.cos(angles)[:, None, :]
    sine = jnp.sin(angles)[:, None, :]
    first = value[..., :halfway]
    second = value[..., halfway:]
    return jnp.concatenate([first * cosine - second * sine, second * cosine + first * sine], axis=-1)

def forward_seq(x, wqkv, wo, router, w_in, w_out, gains, segs, rows):
    length = x.shape[0]
    group = HEADS // KV_HEADS
    qkv_low = low(wqkv)
    out_low = low(wo)
    router_low = low(router)
    in_low = low(w_in)
    down_low = low(w_out)
    gains_low = low(gains)
    normed = low(rms_norm(x, gains_low[0]))
    qkv = low_back(jnp.dot(normed, qkv_low, precision=HIGH))
    query = low(rotary(qkv[:, :QD].reshape(length, HEADS, HD))).reshape(length, KV_HEADS, group, HD)
    keys = low(rotary(qkv[:, QD:QD + KVD].reshape(length, KV_HEADS, HD)))
    values = low(qkv[:, QD + KVD:].reshape(length, KV_HEADS, HD))
    scores = jnp.einsum('sgrd,tgd->grst', query, keys, precision=HIGH) * HD ** (-0.5)
    places = jnp.arange(length, dtype=jnp.int32)
    allowed = (places[:, None] >= places[None, :]) & (segs[:, None] == segs[None, :])
    scores = low_back(jnp.where(allowed, scores, -1e+30))
    probs = low(jax.nn.softmax(scores, axis=-1))
    attention = jnp.einsum('grst,tgd->sgrd', probs, values, precision=HIGH).reshape(length, QD)
    attention = low_back(low(attention))
    branch = low_back(jnp.dot(attention, out_low, precision=HIGH))
    mid = x + branch
    normed2 = low(rms_norm(mid, gains_low[1]))
    logits = jnp.dot(normed2, router_low, precision=HIGH)
    gates = jax.nn.softmax(jnp.take_along_axis(logits, rows, axis=1), axis=-1)
    picks = (rows[:, :, None] == jnp.arange(E, dtype=jnp.int32)[None, None, :]).astype(gates.dtype)
    combine = lax.optimization_barrier(jnp.sum(gates[:, :, None] * picks, axis=1))
    moe = jnp.zeros_like(x)
    for expert in range(E):
        hidden_in = low_back(jnp.dot(normed2, in_low[expert], precision=HIGH))
        hidden = low(jax.nn.silu(hidden_in[:, :H]) * hidden_in[:, H:])
        result = low_back(jnp.dot(hidden, down_low[expert], precision=HIGH))
        moe = moe + combine[:, expert:expert + 1] * result
    return mid + moe

def adamw(weight, first, second, grad, rate, decay):
    first_new = beta_one * first + (1.0 - beta_one) * grad
    second_new = beta_two * second + (1.0 - beta_two) * grad * grad
    first_fix = 1.0 - beta_one ** STEP
    second_fix = 1.0 - beta_two ** STEP
    update = first_new / first_fix / (jnp.sqrt(second_new / second_fix) + adam_eps)
    return (first_new, second_new, weight - rate * (update + decay * weight))

def reference(tokens, segments, routes, cotangent, wqkv, wqkv_first, wqkv_second, wo, wo_first, wo_second, router, router_first, router_second, w_in, w_in_first, w_in_second, w_out, w_out_first, w_out_second, gains, gains_first, gains_second):
    weights = (wqkv, wo, router, w_in, w_out, gains)
    inputs = tokens.astype(jnp.float32).reshape(SEQS, SEQ, D)
    backs = cotangent.astype(jnp.float32).reshape(SEQS, SEQ, D)
    route_rows = routes.reshape(SEQS, SEQ, TOP)

    def per_sequence(totals, item):
        x, segs, rows, back = item

        def closed(xv, p_qkv, p_out, p_router, p_in, p_down, p_gains):
            return forward_seq(xv, p_qkv, p_out, p_router, p_in, p_down, p_gains, segs, rows)
        out, pullback = jax.vjp(closed, x, wqkv, wo, router, w_in, w_out, gains)
        grads = pullback(back)
        summed = tuple((total + grad for total, grad in zip(totals, grads[1:])))
        return (summed, (out.astype(jnp.bfloat16), grads[0]))
    zeros = tuple((jnp.zeros_like(weight) for weight in weights))
    totals, (mixed, tokens_grad) = lax.scan(per_sequence, zeros, (inputs, segments, route_rows, backs))
    g_qkv, g_out, g_router, g_in, g_down, g_gains = totals
    qkv_m, qkv_v, qkv_w = adamw(wqkv, wqkv_first, wqkv_second, g_qkv, 3.0 * D ** (-0.5), decay_rate)
    out_m, out_v, out_w = adamw(wo, wo_first, wo_second, g_out, 3.0 * (QD // 64) ** (-0.5), decay_rate)
    rout_m, rout_v, rout_w = adamw(router, router_first, router_second, g_router, 1.5 * D ** (-0.5), decay_rate)
    in_m, in_v, in_w = adamw(w_in, w_in_first, w_in_second, g_in, 3.0 * D ** (-0.5), decay_rate)
    down_m, down_v, down_w = adamw(w_out, w_out_first, w_out_second, g_down, 3.0 * (H // 16) ** (-0.5), decay_rate)
    gain_m, gain_v, gain_w = adamw(gains, gains_first, gains_second, g_gains, 0.6, 0.0)
    return (mixed.reshape(TOKENS, D), tokens_grad.reshape(TOKENS, D), qkv_m, qkv_v, qkv_w, out_m, out_v, out_w, rout_m, rout_v, rout_w, in_m, in_v, in_w, down_m, down_v, down_w, gain_m, gain_v, gain_w)
```

```python
import functools

import jax
import jax.numpy as jnp
from jax import lax
from jax.experimental import pallas as pl
from jax.experimental.pallas import tpu as pltpu
from jax.sharding import PartitionSpec as P

D = 1536
H = 512
HEADS = 24
KV_HEADS = 8
HD = 64
E = 16
TOP = 8
STEP = 10
QD = 1536
KVD = 512
GROUP = 4

HIGH = lax.Precision.HIGHEST
MESH = pl.DeviceIdType.MESH
norm_eps = 1e-06
beta_one = 0.9
beta_two = 0.95
adam_eps = 1e-08
decay_rate = 0.1
masked_score = -1e30
VMEM_BYTES = 56 * 2**20


def flip(index, bit):
    step = 2**bit
    return index + (1 - 2 * ((index // step) % 2)) * step


def moved(place, bits):
    rep, shard = place
    for axis, bit in bits:
        if axis == "r":
            rep = flip(rep, bit)
        else:
            shard = flip(shard, bit)
    return (rep, shard)


def subsets(bits):
    result = [()]
    for bit in bits:
        result = result + [item + (bit,) for item in result]
    return result


def here():
    return (lax.axis_index("rep"), lax.axis_index("shard"))


def meet(places):
    barrier = pltpu.get_barrier_semaphore()
    for place in places:
        pl.semaphore_signal(barrier, inc=1, device_id=place, device_id_type=MESH)
    pl.semaphore_wait(barrier, len(places))


def start_copy(source, target, sems, index, place):
    copy = pltpu.make_async_remote_copy(
        src_ref=source,
        dst_ref=target,
        send_sem=sems[0].at[index],
        recv_sem=sems[1].at[index],
        device_id=place,
        device_id_type=MESH,
    )
    copy.start()
    return copy


class Counter:
    def __init__(self):
        self.value = 0

    def next(self):
        self.value += 1
        return self.value - 1


def gather_flows(flows, me, sems, count):
    sends = []
    plans = []
    for order, source, target, local in flows:
        index = {}
        for level, bit in enumerate(order):
            for bits in subsets(order[:level]):
                if not (bit[0] == "r" and local(bits) and local(bits + (bit,))):
                    index[(level, bits)] = count.next()
        plans.append(index)
    deepest = max(len(order) for order, _, _, _ in flows)

    def push(flow, number, level, bits, ready):
        order, source, target, local = flow
        if (level, bits) not in plans[number]:
            return
        place = moved(me, bits)
        origin = source(place) if ready else target(place)
        sends.append(
            start_copy(origin, target(place), sems, plans[number][(level, bits)], moved(me, (order[level],)))
        )

    for level in range(deepest):
        for number, flow in enumerate(flows):
            order, source, target, local = flow
            if level < len(order):
                for bits in subsets(order[:level]):
                    if local(bits):
                        push(flow, number, level, bits, True)
    for level in range(deepest):
        for turn in range(2**level):
            for number, flow in enumerate(flows):
                order, source, target, local = flow
                if level >= len(order):
                    continue
                bits = subsets(order[:level])[turn]
                key = (level, bits)
                if key not in plans[number]:
                    continue
                full = bits + (order[level],)
                place = moved(me, full)
                slot = plans[number][key]
                pltpu.make_async_remote_copy(
                    src_ref=target(place),
                    dst_ref=target(place),
                    send_sem=sems[0].at[slot],
                    recv_sem=sems[1].at[slot],
                    device_id=moved(me, (order[level],)),
                    device_id_type=MESH,
                ).wait_recv()
                for later in range(level + 1, len(order)):
                    push(flow, number, later, full, False)
    return sends


def gather_slots(orders):
    return sum(2 ** len(order) - 1 for order in orders)


def add_into(target, first, second, block):
    rows = first.shape[0]

    def body(index, carry):
        window = pl.ds(pl.multiple_of(index * block, block), block)
        total = first[window].astype(jnp.float32) + second[window].astype(jnp.float32)
        target[window] = total.astype(target.dtype)
        return carry

    lax.fori_loop(0, rows // block, body, 0)


def halving_slots(length):
    return 2 ** (length - 1) + 2**length - 1


def sum_flows(flows, me, sems, local_sems, count, local_count):
    sends = []
    loads = []
    plans = []
    for order, source, buffer, block in flows:
        size = len(order)
        held = subsets(order[1:][::-1])
        place_of = {frozenset(bits): i for i, bits in enumerate(held)}
        index, slots, base = {}, {}, len(held)
        for level in range(size):
            for bits in subsets(order[level + 1 :][::-1]):
                index[(level, frozenset(bits))] = count.next()
                slots[(level, frozenset(bits))] = base
                base += 1
        plans.append((place_of, index, slots))
    deepest = max(len(order) for order, _, _, _ in flows)

    def turns(order, level):
        names = subsets(order[level + 1 :][::-1])
        return names[::-1]

    for turn in range(2 ** (deepest - 1)):
        for number, (order, source, buffer, block) in enumerate(flows):
            names = turns(order, 0)
            if turn >= len(names):
                continue
            bits = names[turn]
            key = frozenset(bits)
            place_of, index, slots = plans[number]
            sends.append(
                start_copy(
                    source(moved(me, bits + (order[0],))),
                    buffer.at[slots[(0, key)]],
                    sems,
                    index[(0, key)],
                    moved(me, (order[0],)),
                )
            )
            load = pltpu.make_async_copy(
                source(moved(me, bits)), buffer.at[place_of[key]], local_sems.at[local_count.next()]
            )
            load.start()
            loads.append(((number, key), load))
    waiting = dict(loads)
    for level in range(deepest):
        for turn in range(2 ** (deepest - 1 - level)):
            for number, (order, source, buffer, block) in enumerate(flows):
                if level >= len(order):
                    continue
                names = turns(order, level)
                if turn >= len(names):
                    continue
                bits = names[turn]
                key = frozenset(bits)
                place_of, index, slots = plans[number]
                slot = index[(level, key)]
                landed = buffer.at[slots[(level, key)]]
                pltpu.make_async_remote_copy(
                    src_ref=landed,
                    dst_ref=landed,
                    send_sem=sems[0].at[slot],
                    recv_sem=sems[1].at[slot],
                    device_id=moved(me, (order[level],)),
                    device_id_type=MESH,
                ).wait_recv()
                if level == 0:
                    waiting[(number, key)].wait()
                kept = buffer.at[place_of[key]]
                add_into(kept, kept, landed, block)
                if level + 1 < len(order) and order[level + 1] in key:
                    after = key - {order[level + 1]}
                    sends.append(
                        start_copy(
                            kept,
                            buffer.at[slots[(level + 1, after)]],
                            sems,
                            index[(level + 1, after)],
                            moved(me, (order[level + 1],)),
                        )
                    )
    return sends


def rms_norm(value, gain):
    scale = lax.rsqrt(jnp.mean(value * value, axis=-1, keepdims=True) + norm_eps)
    return value * scale * gain


def norm_back(value, gain, grad):
    scale = lax.rsqrt(jnp.mean(value * value, axis=-1, keepdims=True) + norm_eps)
    normal = value * scale
    grad_gain = jnp.sum(grad * normal, axis=0)
    inner = grad * gain
    grad_value = scale * (inner - normal * jnp.mean(inner * normal, axis=-1, keepdims=True))
    return (grad_value, grad_gain)


def angle_tables(length, width):
    halfway = width // 2
    freqs = 10000.0 ** (-jnp.arange(halfway, dtype=jnp.float32) / halfway)
    angles = jnp.arange(length, dtype=jnp.float32)[:, None] * freqs[None, :]
    return (jnp.cos(angles)[:, None, :], jnp.sin(angles)[:, None, :], halfway)


def rotary(value):
    cosine, sine, halfway = angle_tables(value.shape[0], value.shape[-1])
    first = value[..., :halfway]
    second = value[..., halfway:]
    return jnp.concatenate(
        [first * cosine - second * sine, second * cosine + first * sine], axis=-1
    )


def rotary_back(grad):
    cosine, sine, halfway = angle_tables(grad.shape[0], grad.shape[-1])
    first = grad[..., :halfway]
    second = grad[..., halfway:]
    return jnp.concatenate(
        [first * cosine + second * sine, second * cosine - first * sine], axis=-1
    )


def block_scores(rows, keys, segs):
    places = jnp.arange(keys.shape[0], dtype=jnp.int32)
    scores = jnp.einsum(
        "sgrd,tgd->grst", rows, keys, preferred_element_type=jnp.float32
    ) * rows.shape[-1] ** (-0.5)
    allowed = (places[:, None] >= places[None, :]) & (segs[:, None] == segs[None, :])
    return jnp.where(allowed, scores, masked_score)


def attend_forward(query, keys, values, segs):
    length = query.shape[0]
    block = min(length, 512)

    def one_block(index):
        scores = block_scores(query, keys, segs)
        top = jnp.max(scores, axis=-1, keepdims=True)
        lse = top + jnp.log(jnp.sum(jnp.exp(scores - top), axis=-1, keepdims=True))
        probs = jnp.exp(scores - lse).astype(jnp.bfloat16)
        output = jnp.einsum("grst,tgd->sgrd", probs, values, preferred_element_type=jnp.float32)
        return (output.astype(jnp.bfloat16), lse)

    outputs, lses = lax.map(one_block, jnp.arange(length // block))
    return (outputs.reshape(query.shape), lses)


def attend_backward(query, keys, values, segs, lses, grad_out):
    length = query.shape[0]
    block = min(length, 512)
    scale = query.shape[-1] ** (-0.5)

    def step(carry, item):
        grad_key, grad_value = carry
        index, lse = item
        probs = jnp.exp(block_scores(query, keys, segs) - lse)
        grad_value = grad_value + jnp.einsum(
            "grst,sgrd->tgd",
            probs.astype(jnp.bfloat16),
            grad_out,
            preferred_element_type=jnp.float32,
        )
        grad_probs = jnp.einsum(
            "sgrd,tgd->grst", grad_out, values, preferred_element_type=jnp.float32
        )
        grad_scores = (
            probs * (grad_probs - jnp.sum(grad_probs * probs, axis=-1, keepdims=True))
        ).astype(jnp.bfloat16)
        grad_rows = (
            jnp.einsum("grst,tgd->sgrd", grad_scores, keys, preferred_element_type=jnp.float32)
            * scale
        )
        grad_key = (
            grad_key
            + jnp.einsum("grst,sgrd->tgd", grad_scores, query, preferred_element_type=jnp.float32)
            * scale
        )
        return ((grad_key, grad_value), grad_rows)

    zeros = jnp.zeros(keys.shape, jnp.float32)
    (grad_key, grad_value), grad_query = lax.scan(
        step, (zeros, zeros), (jnp.arange(length // block), lses)
    )
    return (grad_query.reshape(query.shape), grad_key, grad_value)


def adamw(weight, first, second, grad, rate, decay):
    first_new = beta_one * first + (1.0 - beta_one) * grad
    second_new = beta_two * second + (1.0 - beta_two) * grad * grad
    first_fix = 1.0 - beta_one**STEP
    second_fix = 1.0 - beta_two**STEP
    update = first_new / first_fix / (jnp.sqrt(second_new / second_fix) + adam_eps)
    return (first_new, second_new, weight - rate * (update + decay * weight))


X_BIT, C_BIT, Y_BIT, Z_BIT = ("r", 1), ("r", 0), ("s", 0), ("s", 1)
TURNED = (
    (X_BIT, Y_BIT, Z_BIT),
    (Y_BIT, Z_BIT, X_BIT),
    (Z_BIT, X_BIT, Y_BIT),
)
X_LAST = (
    (Z_BIT, Y_BIT, X_BIT),
    (Y_BIT, Z_BIT, X_BIT),
    (Z_BIT, Y_BIT, X_BIT),
)


def far_bits(shards):
    return tuple(("s", i) for i in range(2, shards.bit_length() - 1))


def only_self(bits):
    return not bits


def same_shard(bits):
    return all(axis == "r" for axis, _ in bits)


def token_flows(source, target, orders):
    width = source.shape[-1] // len(orders)
    flows = []
    for number, order in enumerate(orders):
        columns = pl.ds(number * width, width)
        flows.append(
            (
                order + (C_BIT,),
                lambda place, columns=columns: source.at[:, columns],
                lambda place, columns=columns: target.at[place[0], place[1] % GROUP, :, columns],
                only_self,
            )
        )
    return flows


def share_flows(source, target, orders, reps):
    height = source.shape[0] // len(orders)
    width = source.shape[1] // reps
    flows = []

    def columns_of(place):
        return pl.ds(pl.multiple_of(place[0] * width, 128), width)

    for number, order in enumerate(orders):
        rows = pl.ds(number * height, height)
        flows.append(
            (
                order,
                lambda place, rows=rows: source.at[rows, columns_of(place)],
                lambda place, rows=rows: target.at[place[1], rows, columns_of(place)],
                same_shard,
            )
        )
    return flows


def neighbours(me, bits):
    return [moved(me, (bit,)) for bit in bits]


def open_kernel(shards, reps, *refs):
    qkv, out, small, w_in, w_out, cot = refs[:6]
    qkv_all, out_all, small_all, in_all, down_all, cot_all = refs[6:12]
    send, recv, local = refs[12:]
    me = here()
    sems = (send, recv)
    far = far_bits(shards)
    bits = (Y_BIT, Z_BIT) + far
    partners = [moved(me, item) for item in subsets(bits)[1:]][::-1]
    meet(neighbours(me, (X_BIT, C_BIT)) + partners)
    count = Counter()
    own = me[1]
    here_copies = [
        (qkv, qkv_all.at[own]),
        (out, out_all.at[own]),
        (small, small_all.at[own]),
        (w_in.at[own % GROUP], in_all.at[own]),
        (w_out.at[own % GROUP], down_all.at[own]),
        (cot, cot_all.at[me[0], own % GROUP]),
    ]
    for number, (source, target) in enumerate(here_copies):
        pltpu.make_async_copy(source, target, local.at[number]).start()
    sends = []
    orders = [far + order + (C_BIT,) for order in X_LAST]
    flows = share_flows(qkv, qkv_all, orders, reps) + share_flows(out, out_all, orders, reps)
    flows.append(
        (far + (Y_BIT, Z_BIT), lambda place: small, lambda place: small_all.at[place[1]], only_self)
    )
    sends += gather_flows(flows, me, sems, count)
    direct = []
    for place in partners:
        for source, target in ((w_in, in_all), (w_out, down_all)):
            slot = count.next()
            sends.append(
                start_copy(source.at[place[1] % GROUP], target.at[own], sems, slot, place)
            )
            direct.append((target.at[place[1]], slot, place))
    sends += gather_flows(token_flows(cot, cot_all, X_LAST), me, sems, count)
    for landed, slot, place in direct:
        pltpu.make_async_remote_copy(
            src_ref=landed,
            dst_ref=landed,
            send_sem=send.at[slot],
            recv_sem=recv.at[slot],
            device_id=place,
            device_id_type=MESH,
        ).wait_recv()
    for copy in sends:
        copy.wait_send()
    for number, (source, target) in enumerate(here_copies):
        pltpu.make_async_copy(source, target, local.at[number]).wait()


def anywhere(count):
    return [pl.BlockSpec(memory_space=pl.ANY)] * count


def open_call(qkv, out, small, w_in, w_out, cot, shards, reps):
    def grown(array):
        return jax.ShapeDtypeStruct((shards,) + array.shape[-2:], array.dtype)

    shapes = [grown(array) for array in (qkv, out, small, w_in, w_out)]
    shapes.append(jax.ShapeDtypeStruct((reps, GROUP) + cot.shape, cot.dtype))
    slots = 6 * (shards * reps - 1) + shards + 2 * shards + 3 * 15
    return pl.pallas_call(
        functools.partial(open_kernel, shards, reps),
        out_shape=shapes,
        in_specs=anywhere(6),
        out_specs=anywhere(6),
        scratch_shapes=[
            pltpu.SemaphoreType.DMA((slots,)),
            pltpu.SemaphoreType.DMA((slots,)),
            pltpu.SemaphoreType.DMA((6,)),
        ],
        compiler_params=pltpu.CompilerParams(
            collective_id=0, has_side_effects=True, vmem_limit_bytes=VMEM_BYTES
        ),
        name="open_gather",
    )(qkv, out, small, w_in, w_out, cot)


def spread_kernel(reps, *refs):
    rows, gate, rows_all, gate_all, send, recv, local = refs
    me = here()
    sems = (send, recv)
    meet(neighbours(me, (X_BIT, C_BIT, Y_BIT, Z_BIT)))
    count = Counter()
    copies = [
        (rows, rows_all.at[me[0], me[1] % GROUP]),
        (gate, gate_all.at[me[0], me[1] % GROUP]),
    ]
    for number, (source, target) in enumerate(copies):
        pltpu.make_async_copy(source, target, local.at[number]).start()
    flows = token_flows(rows, rows_all, TURNED)
    flows.append(
        (
            TURNED[0] + (C_BIT,),
            lambda place: gate,
            lambda place: gate_all.at[place[0], place[1] % GROUP],
            only_self,
        )
    )
    for copy in gather_flows(flows, me, sems, count):
        copy.wait_send()
    for number, (source, target) in enumerate(copies):
        pltpu.make_async_copy(source, target, local.at[number]).wait()


def spread_call(rows, gate, reps):
    slots = 4 * 15
    return pl.pallas_call(
        functools.partial(spread_kernel, reps),
        out_shape=[
            jax.ShapeDtypeStruct((reps, GROUP) + array.shape, array.dtype) for array in (rows, gate)
        ],
        in_specs=anywhere(2),
        out_specs=anywhere(2),
        scratch_shapes=[
            pltpu.SemaphoreType.DMA((slots,)),
            pltpu.SemaphoreType.DMA((slots,)),
            pltpu.SemaphoreType.DMA((2,)),
        ],
        compiler_params=pltpu.CompilerParams(
            collective_id=1, has_side_effects=True, vmem_limit_bytes=VMEM_BYTES
        ),
        name="spread_tokens",
    )(rows, gate)


def collect_kernel(reps, *refs):
    moe, grad, gate, moe_sum, grad_sum, gate_sum = refs[:6]
    buffers = refs[6:13]
    send, recv, local = refs[13:]
    me = here()
    sems = (send, recv)
    meet(neighbours(me, (X_BIT, C_BIT, Y_BIT, Z_BIT)))
    count, local_count = Counter(), Counter()
    flows = []
    results = []
    for which, (source, target) in enumerate(((grad, grad_sum), (moe, moe_sum))):
        width = source.shape[-1] // len(TURNED)
        for number, order in enumerate(TURNED):
            columns = pl.ds(number * width, width)
            flows.append(
                (
                    (C_BIT,) + order[::-1],
                    lambda place, source=source, columns=columns: source.at[
                        place[0], place[1] % GROUP, :, columns
                    ],
                    buffers[which * 3 + number],
                    32,
                )
            )
            results.append((buffers[which * 3 + number].at[0], target.at[:, columns]))
    flows.append(
        (
            (C_BIT,) + TURNED[0][::-1],
            lambda place: gate.at[place[0], place[1] % GROUP],
            buffers[6],
            16,
        )
    )
    results.append((buffers[6].at[0], gate_sum))
    sends = sum_flows(flows, me, sems, local, count, local_count)
    stores = []
    for source, target in results:
        copy = pltpu.make_async_copy(source, target, local.at[local_count.next()])
        copy.start()
        stores.append(copy)
    for copy in sends:
        copy.wait_send()
    for copy in stores:
        copy.wait()


def collect_call(moe, grad, gate, reps):
    _, _, length, width = moe.shape
    pieces = halving_slots(4)
    third = pltpu.VMEM((pieces, length, width // 3), moe.dtype)
    slots = 7 * 15
    return pl.pallas_call(
        functools.partial(collect_kernel, reps),
        out_shape=[jax.ShapeDtypeStruct(array.shape[2:], array.dtype) for array in (moe, grad, gate)],
        in_specs=anywhere(3),
        out_specs=anywhere(3),
        scratch_shapes=[third] * 6
        + [
            pltpu.VMEM((pieces,) + gate.shape[2:], gate.dtype),
            pltpu.SemaphoreType.DMA((slots,)),
            pltpu.SemaphoreType.DMA((slots,)),
            pltpu.SemaphoreType.DMA((7 * 8 + 7,)),
        ],
        compiler_params=pltpu.CompilerParams(
            collective_id=2, has_side_effects=True, vmem_limit_bytes=VMEM_BYTES
        ),
        name="collect_tokens",
    )(moe, grad, gate)


def close_kernel(shards, reps, *refs):
    qkv, out, small, g_in, g_down = refs[:5]
    qkv_sum, out_sum, small_sum, in_sum, down_sum = refs[5:10]
    dense = refs[10:16]
    tiny, in_land, down_land, in_own, down_own, send, recv, local = refs[16:]
    me = here()
    sems = (send, recv)
    far = far_bits(shards)
    partners = [moved(me, item) for item in subsets((Y_BIT, Z_BIT) + far)[1:]][::-1]
    meet(neighbours(me, (X_BIT, C_BIT)) + partners)
    count, local_count = Counter(), Counter()
    own = me[1]
    sends = []
    direct = {}
    for place in partners:
        for which, (source, landed) in enumerate(((g_in, in_land), (g_down, down_land))):
            slot = count.next()
            sends.append(start_copy(source.at[place[1]], landed.at[own], sems, slot, place))
            direct[(which, len(direct) // 2)] = (landed.at[place[1]], slot, place)
    loads = []
    for source, landed in ((g_in, in_land), (g_down, down_land)):
        load = pltpu.make_async_copy(source.at[own], landed.at[own], local.at[local_count.next()])
        load.start()
        loads.append(load)
    flows = []
    results = []
    for which, (source, target) in enumerate(((qkv, qkv_sum), (out, out_sum))):
        height = source.shape[1] // len(TURNED)
        width = source.shape[2] // reps
        for number, order in enumerate(TURNED):
            rows = pl.ds(number * height, height)
            buffer = dense[which * 3 + number]

            def piece(place, source=source, rows=rows, width=width):
                return source.at[place[1], rows, pl.ds(pl.multiple_of(place[0] * width, 128), width)]

            def goal(place, target=target, rows=rows, width=width):
                return target.at[rows, pl.ds(pl.multiple_of(place[0] * width, 128), width)]

            flows.append(((C_BIT,) + order[::-1] + far, piece, buffer, 16))
            results.append((buffer, goal))
    tiny_order = (Y_BIT, Z_BIT) + far
    flows.append((tiny_order, lambda place: small.at[place[1]], tiny, 16))
    sends += sum_flows(flows, me, sems, local, count, local_count)
    tail = []
    for buffer, goal in results:
        store = pltpu.make_async_copy(buffer.at[0], goal(me), local.at[local_count.next()])
        store.start()
        tail.append(store)
    flows = [
        ((X_BIT, C_BIT), lambda place, buffer=buffer: buffer.at[0], goal, only_self)
        for buffer, goal in results
    ]
    sends += gather_flows(flows, me, sems, count)
    base = halving_slots(len(tiny_order))
    current = 0
    for bit in (X_BIT, C_BIT):
        slot = count.next()
        landed = tiny.at[base]
        copy = start_copy(tiny.at[current], landed, sems, slot, moved(me, (bit,)))
        copy.wait()
        add_into(tiny.at[base + 1], tiny.at[current], landed, 16)
        current = base + 1
        base += 2
    store = pltpu.make_async_copy(tiny.at[current], small_sum, local.at[local_count.next()])
    store.start()
    tail.append(store)
    for load in loads:
        load.wait()
    for landed, slot, place in direct.values():
        pltpu.make_async_remote_copy(
            src_ref=landed,
            dst_ref=landed,
            send_sem=send.at[slot],
            recv_sem=recv.at[slot],
            device_id=place,
            device_id_type=MESH,
        ).wait_recv()
    flows = []
    for landed, held, target in ((in_land, in_own, in_sum), (down_land, down_own, down_sum)):
        for expert in range(GROUP):
            total = landed.at[expert]
            for copy_of in range(1, shards // GROUP):
                add_into(held.at[expert], total, landed.at[expert + GROUP * copy_of], 16)
                total = held.at[expert]

            def goal(place, target=target, expert=expert):
                return target.at[place[0] * GROUP + expert]

            store = pltpu.make_async_copy(
                held.at[expert], goal(me), local.at[local_count.next()]
            )
            store.start()
            tail.append(store)
            flows.append(
                (
                    (X_BIT, C_BIT),
                    lambda place, held=held, expert=expert: held.at[expert],
                    goal,
                    only_self,
                )
            )
    sends += gather_flows(flows, me, sems, count)
    for copy in sends:
        copy.wait_send()
    for copy in tail:
        copy.wait()


def close_call(qkv, out, small, g_in, g_down, shards, reps):
    far = far_bits(shards)
    size = 4 + len(far)
    pieces = halving_slots(size)

    def dense_buffer(array):
        return [
            pltpu.VMEM((pieces, array.shape[1] // 3, array.shape[2] // reps), array.dtype)
        ] * 3

    tiny_pieces = halving_slots(2 + len(far)) + 4
    slots = 7 * (2**size - 1) + 2 * shards + 14 * 3 + 4
    return pl.pallas_call(
        functools.partial(close_kernel, shards, reps),
        out_shape=[jax.ShapeDtypeStruct(array.shape[1:], array.dtype) for array in (qkv, out, small)]
        + [
            jax.ShapeDtypeStruct((reps * GROUP,) + array.shape[1:], array.dtype)
            for array in (g_in, g_down)
        ],
        in_specs=anywhere(5),
        out_specs=anywhere(5),
        scratch_shapes=dense_buffer(qkv)
        + dense_buffer(out)
        + [
            pltpu.VMEM((tiny_pieces,) + small.shape[1:], small.dtype),
            pltpu.VMEM(g_in.shape, g_in.dtype),
            pltpu.VMEM(g_down.shape, g_down.dtype),
            pltpu.VMEM((GROUP,) + g_in.shape[1:], g_in.dtype),
            pltpu.VMEM((GROUP,) + g_down.shape[1:], g_down.dtype),
            pltpu.SemaphoreType.DMA((slots,)),
            pltpu.SemaphoreType.DMA((slots,)),
            pltpu.SemaphoreType.DMA((7 * 2 ** (size - 1) + 32,)),
        ],
        compiler_params=pltpu.CompilerParams(
            collective_id=3, has_side_effects=True, vmem_limit_bytes=VMEM_BYTES
        ),
        name="close_sums",
    )(qkv, out, small, g_in, g_down)


def on_device(
    shards,
    reps,
    tokens,
    segments,
    routes,
    cotangent,
    wqkv,
    wqkv_first,
    wqkv_second,
    wo,
    wo_first,
    wo_second,
    router,
    router_first,
    router_second,
    w_in,
    w_in_first,
    w_in_second,
    w_out,
    w_out_first,
    w_out_second,
    gains,
    gains_first,
    gains_second,
):
    length, width = tokens.shape
    group = HEADS // KV_HEADS
    members = reps * GROUP
    segs = segments[0]
    rep, shard = here()
    expert = rep * GROUP + shard % GROUP
    low = jnp.bfloat16

    small = jnp.concatenate(
        [router, gains.T, jnp.zeros((router.shape[0], 128 - E - 2), jnp.float32)], axis=1
    ).astype(low)
    mine_in = lax.dynamic_slice_in_dim(w_in, rep * GROUP, GROUP, 0).astype(low)
    mine_out = lax.dynamic_slice_in_dim(w_out, rep * GROUP, GROUP, 0).astype(low)
    qkv_w, out_w, small_w, full_in, full_out, cot_all = open_call(
        wqkv.astype(low), wo.astype(low), small, mine_in, mine_out, cotangent, shards, reps
    )
    qkv_w = qkv_w.reshape(D, -1)
    out_w = out_w.reshape(QD, D)
    small_w = small_w.reshape(D, 128)
    full_in = full_in.reshape(D, 2 * H)
    full_out = full_out.reshape(H, D)
    router_w = small_w[:, :E]
    gain_f = small_w[:, E : E + 2].astype(jnp.float32).T

    x = tokens.astype(jnp.float32)
    normed = rms_norm(x, gain_f[0]).astype(low)
    qkv = jnp.dot(normed, qkv_w, preferred_element_type=jnp.float32)
    query = (
        rotary(qkv[:, :QD].reshape(length, HEADS, HD))
        .astype(low)
        .reshape(length, KV_HEADS, group, HD)
    )
    keys = rotary(qkv[:, QD : QD + KVD].reshape(length, KV_HEADS, HD)).astype(low)
    values = qkv[:, QD + KVD :].reshape(length, KV_HEADS, HD).astype(low)
    attended, lses = attend_forward(query, keys, values, segs)
    attention = attended.reshape(length, QD)
    branch = jnp.dot(attention, out_w, preferred_element_type=jnp.float32)
    mid = x + branch
    normed2 = rms_norm(mid, gain_f[1]).astype(low)
    logits = jnp.dot(normed2, router_w, preferred_element_type=jnp.float32)
    picks = (routes[:, :, None] == jnp.arange(E, dtype=jnp.int32)[None, None, :]).any(axis=1)
    gates = jax.nn.softmax(jnp.where(picks, logits, -jnp.inf), axis=-1)

    rows, gates_all = spread_call(normed2, gates.T, reps)
    rows = rows.reshape(members * length, width)
    back = cot_all.reshape(members * length, width)
    gate = lax.dynamic_index_in_dim(
        gates_all.reshape(members, E, length), expert, axis=1, keepdims=False
    ).reshape(members * length, 1)
    hidden_in = jnp.dot(rows, full_in, preferred_element_type=jnp.float32)
    gate_part = hidden_in[:, :H]
    up_part = hidden_in[:, H:]
    sigma = jax.nn.sigmoid(gate_part)
    active = gate_part * sigma
    hidden = (active * up_part).astype(low)
    result = jnp.dot(hidden, full_out, preferred_element_type=jnp.float32)
    back_f = back.astype(jnp.float32)
    grad_gate = jnp.sum(back_f * result, axis=1)
    moe_part = (gate * result).astype(low)
    grad_result = (gate * back_f).astype(low)
    grad_down = jnp.einsum("ch,cd->hd", hidden, grad_result, preferred_element_type=jnp.float32)
    grad_hidden = jnp.einsum("cd,hd->ch", grad_result, full_out, preferred_element_type=jnp.float32)
    grad_gate_part = grad_hidden * up_part * sigma * (1.0 + gate_part * (1.0 - sigma))
    grad_up_part = grad_hidden * active
    grad_in_rows = jnp.concatenate([grad_gate_part, grad_up_part], axis=1).astype(low)
    grad_in = jnp.einsum("cd,ch->dh", rows, grad_in_rows, preferred_element_type=jnp.float32)
    grad_rows = jnp.einsum(
        "ch,dh->cd", grad_in_rows, full_in, preferred_element_type=jnp.float32
    ).astype(low)
    shape = (reps, GROUP, length, width)
    is_mine = (jnp.arange(E, dtype=jnp.int32) == expert).astype(jnp.float32)
    grad_gate_all = grad_gate.reshape(reps, GROUP, 1, length) * is_mine[:, None]
    moe, grad_normed2, grad_gates = collect_call(
        moe_part.reshape(shape), grad_rows.reshape(shape), grad_gate_all, reps
    )
    mixed = (mid + moe.astype(jnp.float32)).astype(low)

    grad_gates = grad_gates.T
    grad_logits = gates * (grad_gates - jnp.sum(grad_gates * gates, axis=-1, keepdims=True))
    grad_router = jnp.dot(normed2.astype(jnp.float32).T, grad_logits, precision=HIGH)
    grad_normed2 = grad_normed2.astype(jnp.float32) + jnp.dot(
        grad_logits, router_w.astype(jnp.float32).T, precision=HIGH
    )
    cot = cotangent.astype(jnp.float32)
    grad_mid_norm, grad_gain2 = norm_back(mid, gain_f[1], grad_normed2)
    grad_mid = cot + grad_mid_norm
    grad_branch = grad_mid.astype(low)
    grad_out_w = jnp.einsum("sq,sd->qd", attention, grad_branch, preferred_element_type=jnp.float32)
    grad_attention = jnp.einsum(
        "sd,qd->sq", grad_branch, out_w, preferred_element_type=jnp.float32
    ).astype(low)
    grad_query, grad_key, grad_value = attend_backward(
        query, keys, values, segs, lses, grad_attention.reshape(length, KV_HEADS, group, HD)
    )
    grad_query = rotary_back(grad_query.reshape(length, HEADS, HD))
    grad_key = rotary_back(grad_key)
    grad_qkv = jnp.concatenate(
        [
            grad_query.reshape(length, QD),
            grad_key.reshape(length, KVD),
            grad_value.reshape(length, KVD),
        ],
        axis=1,
    ).astype(low)
    grad_qkv_w = jnp.einsum("sd,sq->dq", normed, grad_qkv, preferred_element_type=jnp.float32)
    grad_normed = jnp.einsum("sq,dq->sd", grad_qkv, qkv_w, preferred_element_type=jnp.float32)
    grad_x_norm, grad_gain1 = norm_back(x, gain_f[0], grad_normed)
    tokens_grad = grad_mid + grad_x_norm

    grad_small = jnp.concatenate(
        [
            grad_router,
            jnp.stack([grad_gain1, grad_gain2], axis=1),
            jnp.zeros((D, 128 - E - 2), jnp.float32),
        ],
        axis=1,
    )

    def cut(array):
        return array.astype(low).reshape((shards, array.shape[0] // shards) + array.shape[1:])

    grad_qkv_w, grad_out_w, grad_small, grad_in_all, grad_down_all = close_call(
        cut(grad_qkv_w), cut(grad_out_w), cut(grad_small), cut(grad_in), cut(grad_down), shards, reps
    )
    grad_small = grad_small.astype(jnp.float32)
    grad_router = grad_small[:, :E]
    grad_gains = grad_small[:, E : E + 2].T
    qkv_m, qkv_v, qkv_new = adamw(
        wqkv, wqkv_first, wqkv_second, grad_qkv_w.astype(jnp.float32), 3.0 * D ** (-0.5), decay_rate
    )
    out_m, out_v, out_new = adamw(
        wo, wo_first, wo_second, grad_out_w.astype(jnp.float32), 3.0 * (QD // 64) ** (-0.5), decay_rate
    )
    rout_m, rout_v, rout_new = adamw(
        router, router_first, router_second, grad_router, 1.5 * D ** (-0.5), decay_rate
    )
    in_m, in_v, in_new = adamw(
        w_in, w_in_first, w_in_second, grad_in_all.astype(jnp.float32), 3.0 * D ** (-0.5), decay_rate
    )
    down_m, down_v, down_new = adamw(
        w_out,
        w_out_first,
        w_out_second,
        grad_down_all.astype(jnp.float32),
        3.0 * (H // 16) ** (-0.5),
        decay_rate,
    )
    gain_m, gain_v, gain_new = adamw(gains, gains_first, gains_second, grad_gains, 0.6, 0.0)
    return (
        mixed,
        tokens_grad,
        qkv_m,
        qkv_v,
        qkv_new,
        out_m,
        out_v,
        out_new,
        rout_m,
        rout_v,
        rout_new,
        in_m,
        in_v,
        in_new,
        down_m,
        down_v,
        down_new,
        gain_m,
        gain_v,
        gain_new,
    )


def solution(mesh):
    in_specs = (
        P(("rep", "shard"), None),
        P(("rep", "shard"), None),
        P(("rep", "shard"), None),
        P(("rep", "shard"), None),
        P("shard", None),
        P("shard", None),
        P("shard", None),
        P("shard", None),
        P("shard", None),
        P("shard", None),
        P("shard", None),
        P("shard", None),
        P("shard", None),
        P(None, "shard", None),
        P(None, "shard", None),
        P(None, "shard", None),
        P(None, "shard", None),
        P(None, "shard", None),
        P(None, "shard", None),
        P(None, "shard"),
        P(None, "shard"),
        P(None, "shard"),
    )
    out_specs = (
        P(("rep", "shard"), None),
        P(("rep", "shard"), None),
        P("shard", None),
        P("shard", None),
        P("shard", None),
        P("shard", None),
        P("shard", None),
        P("shard", None),
        P("shard", None),
        P("shard", None),
        P("shard", None),
        P(None, "shard", None),
        P(None, "shard", None),
        P(None, "shard", None),
        P(None, "shard", None),
        P(None, "shard", None),
        P(None, "shard", None),
        P(None, "shard"),
        P(None, "shard"),
        P(None, "shard"),
    )
    return jax.shard_map(
        functools.partial(on_device, mesh.shape["shard"], mesh.shape["rep"]), mesh=mesh, in_specs=in_specs, out_specs=out_specs, check_vma=False
    )
```

```python
import functools

import jax
import jax.numpy as jnp
from jax import lax
from jax.experimental import pallas as pl
from jax.experimental.pallas import tpu as pltpu
from jax.sharding import PartitionSpec as P

D = 1536
H = 512
HEADS = 24
KV_HEADS = 8
HD = 64
E = 16
TOP = 8
STEP = 10
QD = 1536
KVD = 512
GROUP = 4

HIGH = lax.Precision.HIGHEST
MESH = pl.DeviceIdType.MESH
norm_eps = 1e-06
beta_one = 0.9
beta_two = 0.95
adam_eps = 1e-08
decay_rate = 0.1
masked_score = -1e30
HOOK = 0
VMEM_BYTES = 56 * 2**20


def flip(index, bit):
    step = 2**bit
    return index + (1 - 2 * ((index // step) % 2)) * step


def moved(place, bits):
    rep, shard = place
    for axis, bit in bits:
        if axis == "r":
            rep = flip(rep, bit)
        else:
            shard = flip(shard, bit)
    return (rep, shard)


def subsets(bits):
    result = [()]
    for bit in bits:
        result = result + [item + (bit,) for item in result]
    return result


def here():
    return (lax.axis_index("rep"), lax.axis_index("shard"))


def meet(places):
    barrier = pltpu.get_barrier_semaphore()
    for place in places:
        pl.semaphore_signal(barrier, inc=1, device_id=place, device_id_type=MESH)
    pl.semaphore_wait(barrier, len(places))


def start_copy(source, target, sems, index, place):
    copy = pltpu.make_async_remote_copy(
        src_ref=source,
        dst_ref=target,
        send_sem=sems[0].at[index],
        recv_sem=sems[1].at[index],
        device_id=place,
        device_id_type=MESH,
    )
    copy.start()
    return copy


class Counter:
    def __init__(self):
        self.value = 0

    def next(self):
        self.value += 1
        return self.value - 1


def gather_flows(flows, me, sems, count, hooks=()):
    sends = []
    for _ in gather_steps(flows, me, sems, count, sends, hooks):
        pass
    return sends


def gather_steps(flows, me, sems, count, sends, hooks=()):
    plans = []
    for order, source, target, local in flows:
        index = {}
        for level, bit in enumerate(order):
            for bits in subsets(order[:level]):
                if not (bit[0] == "r" and local(bits) and local(bits + (bit,))):
                    index[(level, bits)] = count.next()
        plans.append(index)
    deepest = max(len(order) for order, _, _, _ in flows)

    def push(flow, number, level, bits, ready):
        order, source, target, local = flow
        if (level, bits) not in plans[number]:
            return
        place = moved(me, bits)
        origin = source(place) if ready else target(place)
        sends.append(
            start_copy(origin, target(place), sems, plans[number][(level, bits)], moved(me, (order[level],)))
        )

    for level in range(deepest):
        for number, flow in enumerate(flows):
            order, source, target, local = flow
            if level < len(order):
                for bits in subsets(order[:level]):
                    if local(bits):
                        push(flow, number, level, bits, True)
    yield
    hooks = dict(hooks)
    if -1 in hooks:
        hooks[-1]()
    for level in range(deepest):
        for turn in range(2**level):
            for number, flow in enumerate(flows):
                order, source, target, local = flow
                if level >= len(order):
                    continue
                bits = subsets(order[:level])[turn]
                key = (level, bits)
                if key not in plans[number]:
                    continue
                full = bits + (order[level],)
                place = moved(me, full)
                slot = plans[number][key]
                pltpu.make_async_remote_copy(
                    src_ref=target(place),
                    dst_ref=target(place),
                    send_sem=sems[0].at[slot],
                    recv_sem=sems[1].at[slot],
                    device_id=moved(me, (order[level],)),
                    device_id_type=MESH,
                ).wait_recv()
                for later in range(level + 1, len(order)):
                    push(flow, number, later, full, False)
                yield
        if level in hooks:
            hooks[level]()


def gather_slots(orders):
    return sum(2 ** len(order) - 1 for order in orders)


def add_into(target, first, second, block):
    rows = first.shape[0]

    def body(index, carry):
        window = pl.ds(pl.multiple_of(index * block, block), block)
        target[window] = first[window] + second[window]
        return carry

    if rows == block:
        target[...] = first[...] + second[...]
    else:
        lax.fori_loop(0, rows // block, body, 0)


def halving_slots(length):
    return 2 ** (length - 1) + 2**length - 1


def sum_flows(flows, me, sems, local_sems, count, local_count):
    sends = []
    for _ in sum_steps(flows, me, sems, local_sems, count, local_count, sends):
        pass
    return sends


def sum_steps(flows, me, sems, local_sems, count, local_count, sends):
    loads = []
    plans = []
    for order, source, buffer, block in flows:
        size = len(order)
        held = subsets(order[1:][::-1])
        place_of = {frozenset(bits): i for i, bits in enumerate(held)}
        index, slots, base = {}, {}, len(held)
        for level in range(size):
            for bits in subsets(order[level + 1 :][::-1]):
                index[(level, frozenset(bits))] = count.next()
                slots[(level, frozenset(bits))] = base
                base += 1
        plans.append((place_of, index, slots))
    deepest = max(len(order) for order, _, _, _ in flows)

    def turns(order, level):
        names = subsets(order[level + 1 :][::-1])
        return names[::-1]

    for turn in range(2 ** (deepest - 1)):
        for number, (order, source, buffer, block) in enumerate(flows):
            names = turns(order, 0)
            if turn >= len(names):
                continue
            bits = names[turn]
            key = frozenset(bits)
            place_of, index, slots = plans[number]
            sends.append(
                start_copy(
                    source(moved(me, bits + (order[0],))),
                    buffer.at[slots[(0, key)]],
                    sems,
                    index[(0, key)],
                    moved(me, (order[0],)),
                )
            )
            load = pltpu.make_async_copy(
                source(moved(me, bits)), buffer.at[place_of[key]], local_sems.at[local_count.next()]
            )
            load.start()
            loads.append(((number, key), load))
    waiting = dict(loads)
    yield
    for level in range(deepest):
        for turn in range(2 ** (deepest - 1 - level)):
            for number, (order, source, buffer, block) in enumerate(flows):
                if level >= len(order):
                    continue
                names = turns(order, level)
                if turn >= len(names):
                    continue
                bits = names[turn]
                key = frozenset(bits)
                place_of, index, slots = plans[number]
                slot = index[(level, key)]
                landed = buffer.at[slots[(level, key)]]
                pltpu.make_async_remote_copy(
                    src_ref=landed,
                    dst_ref=landed,
                    send_sem=sems[0].at[slot],
                    recv_sem=sems[1].at[slot],
                    device_id=moved(me, (order[level],)),
                    device_id_type=MESH,
                ).wait_recv()
                if level == 0:
                    waiting[(number, key)].wait()
                kept = buffer.at[place_of[key]]
                add_into(kept, kept, landed, block)
                if level + 1 < len(order) and order[level + 1] in key:
                    after = key - {order[level + 1]}
                    sends.append(
                        start_copy(
                            kept,
                            buffer.at[slots[(level + 1, after)]],
                            sems,
                            index[(level + 1, after)],
                            moved(me, (order[level + 1],)),
                        )
                    )
                yield


def rms_norm(value, gain):
    scale = lax.rsqrt(jnp.mean(value * value, axis=-1, keepdims=True) + norm_eps)
    return value * scale * gain


def norm_back(value, gain, grad):
    scale = lax.rsqrt(jnp.mean(value * value, axis=-1, keepdims=True) + norm_eps)
    normal = value * scale
    grad_gain = jnp.sum(grad * normal, axis=0)
    inner = grad * gain
    grad_value = scale * (inner - normal * jnp.mean(inner * normal, axis=-1, keepdims=True))
    return (grad_value, grad_gain)


def angle_tables(length, width):
    halfway = width // 2
    freqs = 10000.0 ** (-jnp.arange(halfway, dtype=jnp.float32) / halfway)
    angles = jnp.arange(length, dtype=jnp.float32)[:, None] * freqs[None, :]
    return (jnp.cos(angles)[:, None, :], jnp.sin(angles)[:, None, :], halfway)


def rotary(value):
    cosine, sine, halfway = angle_tables(value.shape[0], value.shape[-1])
    first = value[..., :halfway]
    second = value[..., halfway:]
    return jnp.concatenate(
        [first * cosine - second * sine, second * cosine + first * sine], axis=-1
    )


def rotary_back(grad):
    cosine, sine, halfway = angle_tables(grad.shape[0], grad.shape[-1])
    first = grad[..., :halfway]
    second = grad[..., halfway:]
    return jnp.concatenate(
        [first * cosine + second * sine, second * cosine - first * sine], axis=-1
    )


def block_scores(rows, keys, segs):
    places = jnp.arange(keys.shape[0], dtype=jnp.int32)
    scores = jnp.einsum(
        "sgrd,tgd->grst", rows, keys, preferred_element_type=jnp.float32
    ) * rows.shape[-1] ** (-0.5)
    allowed = (places[:, None] >= places[None, :]) & (segs[:, None] == segs[None, :])
    return jnp.where(allowed, scores, masked_score)


def attend_forward(query, keys, values, segs):
    length = query.shape[0]
    block = min(length, 512)

    def one_block(index):
        scores = block_scores(query, keys, segs)
        top = jnp.max(scores, axis=-1, keepdims=True)
        lse = top + jnp.log(jnp.sum(jnp.exp(scores - top), axis=-1, keepdims=True))
        probs = jnp.exp(scores - lse).astype(jnp.bfloat16)
        output = jnp.einsum("grst,tgd->sgrd", probs, values, preferred_element_type=jnp.float32)
        return (output.astype(jnp.bfloat16), lse)

    outputs, lses = lax.map(one_block, jnp.arange(length // block))
    return (outputs.reshape(query.shape), lses)


def attend_backward(query, keys, values, segs, lses, grad_out):
    length = query.shape[0]
    block = min(length, 512)
    scale = query.shape[-1] ** (-0.5)

    def step(carry, item):
        grad_key, grad_value = carry
        index, lse = item
        probs = jnp.exp(block_scores(query, keys, segs) - lse)
        grad_value = grad_value + jnp.einsum(
            "grst,sgrd->tgd",
            probs.astype(jnp.bfloat16),
            grad_out,
            preferred_element_type=jnp.float32,
        )
        grad_probs = jnp.einsum(
            "sgrd,tgd->grst", grad_out, values, preferred_element_type=jnp.float32
        )
        grad_scores = (
            probs * (grad_probs - jnp.sum(grad_probs * probs, axis=-1, keepdims=True))
        ).astype(jnp.bfloat16)
        grad_rows = (
            jnp.einsum("grst,tgd->sgrd", grad_scores, keys, preferred_element_type=jnp.float32)
            * scale
        )
        grad_key = (
            grad_key
            + jnp.einsum("grst,sgrd->tgd", grad_scores, query, preferred_element_type=jnp.float32)
            * scale
        )
        return ((grad_key, grad_value), grad_rows)

    zeros = jnp.zeros(keys.shape, jnp.float32)
    (grad_key, grad_value), grad_query = lax.scan(
        step, (zeros, zeros), (jnp.arange(length // block), lses)
    )
    return (grad_query.reshape(query.shape), grad_key, grad_value)


def adamw(weight, first, second, grad, rate, decay):
    first_new = beta_one * first + (1.0 - beta_one) * grad
    second_new = beta_two * second + (1.0 - beta_two) * grad * grad
    first_fix = 1.0 - beta_one**STEP
    second_fix = 1.0 - beta_two**STEP
    update = first_new / first_fix / (jnp.sqrt(second_new / second_fix) + adam_eps)
    return (first_new, second_new, weight - rate * (update + decay * weight))


X_BIT, C_BIT, Y_BIT, Z_BIT = ("r", 1), ("r", 0), ("s", 0), ("s", 1)
TURNED = (
    (X_BIT, Y_BIT, Z_BIT),
    (Y_BIT, Z_BIT, X_BIT),
    (Z_BIT, X_BIT, Y_BIT),
)
GRAD_TURNED = (
    (X_BIT, Y_BIT, Z_BIT),
    (Y_BIT, X_BIT, Z_BIT),
    (Y_BIT, Z_BIT, X_BIT),
)
MOE_TURNED = (
    (X_BIT, Y_BIT, Z_BIT),
    (Y_BIT, X_BIT, Z_BIT),
    (X_BIT, Z_BIT, Y_BIT),
)
SUM_TURNED = (
    (X_BIT, Y_BIT, Z_BIT),
    (Y_BIT, Z_BIT, X_BIT),
    (Z_BIT, Y_BIT, X_BIT),
)
X_LAST = (
    (Z_BIT, Y_BIT, X_BIT),
    (Y_BIT, Z_BIT, X_BIT),
    (Z_BIT, Y_BIT, X_BIT),
)


def far_bits(shards):
    return tuple(("s", i) for i in range(2, shards.bit_length() - 1))


def only_self(bits):
    return not bits


def same_shard(bits):
    return all(axis == "r" for axis, _ in bits)


def token_flows(source, target, orders):
    width = source.shape[-1] // len(orders)
    flows = []
    for number, order in enumerate(orders):
        columns = pl.ds(number * width, width)
        flows.append(
            (
                order + (C_BIT,),
                lambda place, columns=columns: source.at[:, columns],
                lambda place, columns=columns: target.at[place[0], place[1] % GROUP, :, columns],
                only_self,
            )
        )
    return flows


def share_flows(source, target, orders, reps):
    height = source.shape[0] // len(orders)
    width = source.shape[1] // reps
    flows = []

    def columns_of(place):
        return pl.ds(pl.multiple_of(place[0] * width, 128), width)

    for number, order in enumerate(orders):
        rows = pl.ds(number * height, height)
        flows.append(
            (
                order,
                lambda place, rows=rows: source.at[rows, columns_of(place)],
                lambda place, rows=rows: target.at[place[1], rows, columns_of(place)],
                same_shard,
            )
        )
    return flows


def neighbours(me, bits):
    return [moved(me, (bit,)) for bit in bits]


def open_kernel(shards, reps, *refs):
    qkv, out, small, w_in, w_out, cot = refs[:6]
    qkv_all, out_all, small_all, in_all, down_all, cot_all = refs[6:12]
    send, recv, local = refs[12:]
    me = here()
    sems = (send, recv)
    far = far_bits(shards)
    bits = (Y_BIT, Z_BIT) + far
    partners = [moved(me, item) for item in subsets(bits)[1:]][::-1]
    meet(neighbours(me, (X_BIT, C_BIT)) + partners)
    count = Counter()
    own = me[1]
    here_copies = [
        (qkv, qkv_all.at[own]),
        (out, out_all.at[own]),
        (small, small_all.at[own]),
        (w_in.at[own % GROUP], in_all.at[own]),
        (w_out.at[own % GROUP], down_all.at[own]),
        (cot, cot_all.at[me[0], own % GROUP]),
    ]
    for number, (source, target) in enumerate(here_copies):
        pltpu.make_async_copy(source, target, local.at[number]).start()
    sends = []
    orders = [far + order + (C_BIT,) for order in X_LAST]
    flows = share_flows(qkv, qkv_all, orders, reps) + share_flows(out, out_all, orders, reps)
    flows.append(
        (far + (Y_BIT, Z_BIT), lambda place: small, lambda place: small_all.at[place[1]], only_self)
    )
    flows += token_flows(cot, cot_all, X_LAST)
    direct = []

    def send_experts(chosen):
        for place in chosen:
            for source, target in ((w_in, in_all), (w_out, down_all)):
                slot = count.next()
                sends.append(
                    start_copy(source.at[place[1] % GROUP], target.at[own], sems, slot, place)
                )
                direct.append((target.at[place[1]], slot, place))

    hooks = {HOOK: functools.partial(send_experts, partners)}
    sends += gather_flows(flows, me, sems, count, hooks)
    for landed, slot, place in direct:
        pltpu.make_async_remote_copy(
            src_ref=landed,
            dst_ref=landed,
            send_sem=send.at[slot],
            recv_sem=recv.at[slot],
            device_id=place,
            device_id_type=MESH,
        ).wait_recv()
    for copy in sends:
        copy.wait_send()
    for number, (source, target) in enumerate(here_copies):
        pltpu.make_async_copy(source, target, local.at[number]).wait()


def anywhere(count):
    return [pl.BlockSpec(memory_space=pl.ANY)] * count


def open_call(qkv, out, small, w_in, w_out, cot, shards, reps):
    def grown(array):
        return jax.ShapeDtypeStruct((shards,) + array.shape[-2:], array.dtype)

    shapes = [grown(array) for array in (qkv, out, small, w_in, w_out)]
    shapes.append(jax.ShapeDtypeStruct((reps, GROUP) + cot.shape, cot.dtype))
    slots = 6 * (shards * reps - 1) + shards + 2 * shards + 3 * 15
    return pl.pallas_call(
        functools.partial(open_kernel, shards, reps),
        out_shape=shapes,
        in_specs=anywhere(6),
        out_specs=anywhere(6),
        scratch_shapes=[
            pltpu.SemaphoreType.DMA((slots,)),
            pltpu.SemaphoreType.DMA((slots,)),
            pltpu.SemaphoreType.DMA((6,)),
        ],
        compiler_params=pltpu.CompilerParams(
            collective_id=0, has_side_effects=True, vmem_limit_bytes=VMEM_BYTES
        ),
        name="open_gather",
    )(qkv, out, small, w_in, w_out, cot)


def spread_kernel(reps, *refs):
    rows, gate, rows_all, gate_all, send, recv, local = refs
    me = here()
    sems = (send, recv)
    meet(neighbours(me, (X_BIT, C_BIT, Y_BIT, Z_BIT)))
    count = Counter()
    copies = [
        (rows, rows_all.at[me[0], me[1] % GROUP]),
        (gate, gate_all.at[me[0], me[1] % GROUP]),
    ]
    for number, (source, target) in enumerate(copies):
        pltpu.make_async_copy(source, target, local.at[number]).start()
    flows = token_flows(rows, rows_all, TURNED)
    flows.append(
        (
            TURNED[0] + (C_BIT,),
            lambda place: gate,
            lambda place: gate_all.at[place[0], place[1] % GROUP],
            only_self,
        )
    )
    for copy in gather_flows(flows, me, sems, count):
        copy.wait_send()
    for number, (source, target) in enumerate(copies):
        pltpu.make_async_copy(source, target, local.at[number]).wait()


def spread_call(rows, gate, reps):
    slots = 4 * 15
    return pl.pallas_call(
        functools.partial(spread_kernel, reps),
        out_shape=[
            jax.ShapeDtypeStruct((reps, GROUP) + array.shape, array.dtype) for array in (rows, gate)
        ],
        in_specs=anywhere(2),
        out_specs=anywhere(2),
        scratch_shapes=[
            pltpu.SemaphoreType.DMA((slots,)),
            pltpu.SemaphoreType.DMA((slots,)),
            pltpu.SemaphoreType.DMA((2,)),
        ],
        compiler_params=pltpu.CompilerParams(
            collective_id=1, has_side_effects=True, vmem_limit_bytes=VMEM_BYTES
        ),
        name="spread_tokens",
    )(rows, gate)


def collect_kernel(reps, far, *refs):
    moe, grad, gate, g_in, g_down, moe_sum, grad_sum, gate_sum, far_in, far_down = refs[:10]
    buffers = refs[10:17]
    send, recv, local = refs[17:]
    me = here()
    sems = (send, recv)
    away = [moved(me, item) for item in subsets(far)[1:]]
    meet(neighbours(me, (X_BIT, C_BIT, Y_BIT, Z_BIT)) + away)
    count, local_count = Counter(), Counter()
    far_sends = []
    for number, place in enumerate(away):
        for source, target in ((g_in, far_in), (g_down, far_down)):
            far_sends.append(
                start_copy(
                    source.at[place[1] // GROUP], target.at[number], sems, count.next(), place
                )
            )
    flows = []
    results = []
    for which, (source, target, turned) in enumerate(
        ((grad, grad_sum, GRAD_TURNED), (moe, moe_sum, MOE_TURNED))
    ):
        width = source.shape[-1] // len(turned)
        for number, order in enumerate(turned):
            columns = pl.ds(number * width, width)
            flows.append(
                (
                    (C_BIT,) + order,
                    lambda place, source=source, columns=columns: source.at[
                        place[0], place[1] % GROUP, :, columns
                    ],
                    buffers[which * 3 + number],
                    128,
                )
            )
            results.append((buffers[which * 3 + number].at[0], target.at[:, columns]))
    flows.append(
        (
            (C_BIT,) + TURNED[0][::-1],
            lambda place: gate.at[place[0], place[1] % GROUP],
            buffers[6],
            16,
        )
    )
    results.append((buffers[6].at[0], gate_sum))
    sends = sum_flows(flows, me, sems, local, count, local_count)
    stores = []
    for source, target in results:
        copy = pltpu.make_async_copy(source, target, local.at[local_count.next()])
        copy.start()
        stores.append(copy)
    for copy in far_sends:
        copy.wait()
    for copy in sends:
        copy.wait_send()
    for copy in stores:
        copy.wait()


def collect_call(moe, grad, gate, g_in, g_down, shards, reps):
    far = far_bits(shards)
    others = 2 ** len(far) - 1
    _, _, length, width = moe.shape
    pieces = halving_slots(4)
    third = pltpu.VMEM((pieces, length, width // 3), moe.dtype)
    slots = 7 * 15 + 2 * others
    return pl.pallas_call(
        functools.partial(collect_kernel, reps, far),
        out_shape=[jax.ShapeDtypeStruct(array.shape[2:], array.dtype) for array in (moe, grad, gate)]
        + [
            jax.ShapeDtypeStruct((others,) + array.shape[1:], array.dtype)
            for array in (g_in, g_down)
        ],
        in_specs=anywhere(5),
        out_specs=anywhere(5),
        scratch_shapes=[third] * 6
        + [
            pltpu.VMEM((pieces,) + gate.shape[2:], gate.dtype),
            pltpu.SemaphoreType.DMA((slots,)),
            pltpu.SemaphoreType.DMA((slots,)),
            pltpu.SemaphoreType.DMA((7 * 8 + 7,)),
        ],
        compiler_params=pltpu.CompilerParams(
            collective_id=2, has_side_effects=True, vmem_limit_bytes=VMEM_BYTES
        ),
        name="collect_tokens",
    )(moe, grad, gate, g_in, g_down)


def dot(a, b, dims=((1,), (0,))):
    return lax.dot_general(a, b, (dims, ((), ())), preferred_element_type=jnp.float32)


def expert_kernel(
    rows_ref,
    back_ref,
    gate_ref,
    in_ref,
    out_ref,
    moe_ref,
    grad_ref,
    mark_ref,
    grad_in_ref,
    grad_out_ref,
    in_total,
    out_total,
):
    step = pl.program_id(0)

    @pl.when(step == 0)
    def _():
        in_total[...] = jnp.zeros_like(in_total)
        out_total[...] = jnp.zeros_like(out_total)

    low = jnp.bfloat16
    rows = rows_ref[...]
    hidden_in = dot(rows, in_ref[...])
    gate_part = hidden_in[:, :H]
    up_part = hidden_in[:, H:]
    sigma = jax.nn.sigmoid(gate_part)
    active = gate_part * sigma
    hidden = (active * up_part).astype(low)
    result = dot(hidden, out_ref[...])
    back = back_ref[...].astype(jnp.float32)
    gate = gate_ref[...]
    mark_ref[...] = jnp.sum(back * result, axis=1, keepdims=True)
    moe_ref[...] = (gate * result).astype(low)
    grad_result = (gate * back).astype(low)
    grad_hidden = dot(grad_result, out_ref[...], ((1,), (1,)))
    out_total[...] += dot(hidden, grad_result, ((0,), (0,)))
    grad_gate_part = grad_hidden * up_part * sigma * (1.0 + gate_part * (1.0 - sigma))
    grad_up_part = grad_hidden * active
    grad_rows = jnp.concatenate([grad_gate_part, grad_up_part], axis=1).astype(low)
    grad_ref[...] = dot(grad_rows, in_ref[...], ((1,), (1,))).astype(low)
    in_total[...] += dot(rows, grad_rows, ((0,), (0,)))

    @pl.when(step == pl.num_programs(0) - 1)
    def _():
        grad_in_ref[...] = in_total[...].astype(low)
        grad_out_ref[...] = out_total[...].astype(low)


def expert_call(rows, back, gate, full_in, full_out, block):
    count, width = rows.shape
    low = jnp.bfloat16

    def moving(columns):
        return pl.BlockSpec((block, columns), lambda i: (i, 0))

    def fixed(array):
        return pl.BlockSpec(array.shape, lambda i: (0, 0), pipeline_mode=pl.Buffered(1))

    flops = 2 * count * 9 * width * H
    return pl.pallas_call(
        expert_kernel,
        grid=(count // block,),
        out_shape=[
            jax.ShapeDtypeStruct((count, width), low),
            jax.ShapeDtypeStruct((count, width), low),
            jax.ShapeDtypeStruct((count, 1), jnp.float32),
            jax.ShapeDtypeStruct(full_in.shape, low),
            jax.ShapeDtypeStruct(full_out.shape, low),
        ],
        in_specs=[moving(width), moving(width), moving(1), fixed(full_in), fixed(full_out)],
        out_specs=[moving(width), moving(width), moving(1), fixed(full_in), fixed(full_out)],
        scratch_shapes=[
            pltpu.VMEM(full_in.shape, jnp.float32),
            pltpu.VMEM(full_out.shape, jnp.float32),
        ],
        compiler_params=pltpu.CompilerParams(
            vmem_limit_bytes=VMEM_BYTES, dimension_semantics=("arbitrary",)
        ),
        cost_estimate=pl.CostEstimate(
            flops=flops, bytes_accessed=2 * 4 * count * width, transcendentals=count * H
        ),
        name="experts",
    )(rows, back, gate, full_in, full_out)


def close_kernel(shards, reps, *refs):
    qkv, out, small, g_in, g_down = refs[:5]
    qkv_sum, out_sum, small_sum, in_sum, down_sum = refs[5:10]
    dense = refs[10:16]
    tiny, in_land, down_land, send, recv, local = refs[16:]
    me = here()
    sems = (send, recv)
    far = far_bits(shards)
    meet(neighbours(me, (X_BIT, C_BIT, Y_BIT, Z_BIT) + far) + [moved(me, (Y_BIT, Z_BIT))])
    count, local_count = Counter(), Counter()
    sends = []
    flows = []
    results = []
    for which, (source, target) in enumerate(((qkv, qkv_sum), (out, out_sum))):
        height = source.shape[1] // len(SUM_TURNED)
        width = source.shape[2] // reps
        for number, order in enumerate(SUM_TURNED):
            rows = pl.ds(number * height, height)
            buffer = dense[which * 3 + number]

            def piece(place, source=source, rows=rows, width=width):
                return source.at[place[1], rows, pl.ds(pl.multiple_of(place[0] * width, 128), width)]

            def goal(place, target=target, rows=rows, width=width):
                return target.at[rows, pl.ds(pl.multiple_of(place[0] * width, 128), width)]

            flows.append(((C_BIT,) + order + far, piece, buffer, height))
            results.append((buffer, goal))
    tiny_order = (Y_BIT, Z_BIT) + far
    flows.append((tiny_order, lambda place: small.at[place[1]], tiny, 16))
    tail = []

    early = [flow for flow in flows if flow[0][:2] == (C_BIT, X_BIT)]
    late = [flow for flow in flows if flow[0][:2] != (C_BIT, X_BIT)]
    first = sum_steps(early, me, sems, local, count, local_count, sends)
    second = sum_steps(late, me, sems, local, count, local_count, sends)

    def last_steps():
        for buffer, goal in results:
            store = pltpu.make_async_copy(buffer.at[0], goal(me), local.at[local_count.next()])
            store.start()
            tail.append(store)
        columns = [
            ((X_BIT, C_BIT), lambda place, buffer=buffer: buffer.at[0], goal, only_self)
            for buffer, goal in results
        ]
        yield from gather_steps(columns, me, sems, count, sends)
        base = halving_slots(len(tiny_order))
        current = 0
        for bit in (X_BIT, C_BIT):
            slot = count.next()
            landed = tiny.at[base]
            copy = start_copy(tiny.at[current], landed, sems, slot, moved(me, (bit,)))
            copy.wait()
            add_into(tiny.at[base + 1], tiny.at[current], landed, 16)
            current = base + 1
            base += 2
            yield
        store = pltpu.make_async_copy(tiny.at[current], small_sum, local.at[local_count.next()])
        store.start()
        tail.append(store)

    arrays = ((g_in, in_land, in_sum), (g_down, down_land, down_sum))
    waves = subsets((Z_BIT, Y_BIT))
    own = me[1] % GROUP

    def expert_steps():
        waiting = []
        for near in waves:
            place = moved(me, near)
            expert = place[1] % GROUP
            for source, landed, _ in arrays:
                if near:
                    slot = count.next()
                    sends.append(start_copy(source.at[expert], landed.at[own], sems, slot, place))
                    waiting.append(
                        pltpu.make_async_remote_copy(
                            src_ref=landed.at[expert],
                            dst_ref=landed.at[expert],
                            send_sem=send.at[slot],
                            recv_sem=recv.at[slot],
                            device_id=place,
                            device_id_type=MESH,
                        ).wait_recv
                    )
                else:
                    load = pltpu.make_async_copy(
                        source.at[own], landed.at[own], local.at[local_count.next()]
                    )
                    load.start()
                    waiting.append(load.wait)
        yield
        relays = []
        for near in waves:
            expert = moved(me, near)[1] % GROUP
            for _, landed, target in arrays:
                waiting.pop(0)()

                def goal(where, target=target, expert=expert):
                    return target.at[where[0] * GROUP + expert]

                total = landed.at[expert]
                store = pltpu.make_async_copy(total, goal(me), local.at[local_count.next()])
                store.start()
                tail.append(store)
                flow = ((X_BIT, C_BIT), lambda where, total=total: total, goal, only_self)
                relay = gather_steps([flow], me, sems, count, sends)
                relays.append(relay)
                next(relay)
            yield
        for relay in relays:
            for _ in relay:
                yield

    experts = expert_steps()
    for run in (experts, first, second):
        next(run)
    for _ in range(len(early) * reps * shards // 2):
        next(first)
    for _ in waves:
        next(experts)
    mixed = [(second, 4), (first, 1), (experts, 1)]
    alive = [run for run, _ in mixed]
    while alive:
        for run, turns in mixed:
            for _ in range(turns):
                if run in alive and next(run, "end") == "end":
                    alive.remove(run)
    for _ in last_steps():
        pass
    for copy in sends:
        copy.wait_send()
    for copy in tail:
        copy.wait()


def close_call(qkv, out, small, g_in, g_down, shards, reps):
    far = far_bits(shards)
    size = 4 + len(far)
    pieces = halving_slots(size)

    def dense_buffer(array):
        return [
            pltpu.VMEM((pieces, array.shape[1] // 3, array.shape[2] // reps), array.dtype)
        ] * 3

    tiny_pieces = halving_slots(2 + len(far)) + 4
    slots = 7 * (2**size - 1) + 2 * shards + 14 * 3 + 4
    return pl.pallas_call(
        functools.partial(close_kernel, shards, reps),
        out_shape=[jax.ShapeDtypeStruct(array.shape[1:], array.dtype) for array in (qkv, out, small)]
        + [
            jax.ShapeDtypeStruct((reps * GROUP,) + array.shape[1:], array.dtype)
            for array in (g_in, g_down)
        ],
        in_specs=anywhere(5),
        out_specs=anywhere(5),
        scratch_shapes=dense_buffer(qkv)
        + dense_buffer(out)
        + [
            pltpu.VMEM((tiny_pieces,) + small.shape[1:], small.dtype),
            pltpu.VMEM(g_in.shape, g_in.dtype),
            pltpu.VMEM(g_down.shape, g_down.dtype),
            pltpu.SemaphoreType.DMA((slots,)),
            pltpu.SemaphoreType.DMA((slots,)),
            pltpu.SemaphoreType.DMA((7 * 2 ** (size - 1) + 32,)),
        ],
        compiler_params=pltpu.CompilerParams(
            collective_id=3, has_side_effects=True, vmem_limit_bytes=VMEM_BYTES
        ),
        name="close_sums",
    )(qkv, out, small, g_in, g_down)


def on_device(
    shards,
    reps,
    tokens,
    segments,
    routes,
    cotangent,
    wqkv,
    wqkv_first,
    wqkv_second,
    wo,
    wo_first,
    wo_second,
    router,
    router_first,
    router_second,
    w_in,
    w_in_first,
    w_in_second,
    w_out,
    w_out_first,
    w_out_second,
    gains,
    gains_first,
    gains_second,
):
    length, width = tokens.shape
    group = HEADS // KV_HEADS
    members = reps * GROUP
    segs = segments[0]
    rep, shard = here()
    expert = rep * GROUP + shard % GROUP
    low = jnp.bfloat16

    def cut(array):
        return array.astype(low).reshape((shards, array.shape[0] // shards) + array.shape[1:])

    small = jnp.concatenate(
        [router, gains.T, jnp.zeros((router.shape[0], 128 - E - 2), jnp.float32)], axis=1
    ).astype(low)
    mine_in = lax.dynamic_slice_in_dim(w_in, rep * GROUP, GROUP, 0).astype(low)
    mine_out = lax.dynamic_slice_in_dim(w_out, rep * GROUP, GROUP, 0).astype(low)
    qkv_w, out_w, small_w, full_in, full_out, cot_all = open_call(
        wqkv.astype(low), wo.astype(low), small, mine_in, mine_out, cotangent, shards, reps
    )
    qkv_w = qkv_w.reshape(D, -1)
    out_w = out_w.reshape(QD, D)
    small_w = small_w.reshape(D, 128)
    router_w = small_w[:, :E]
    gain_f = small_w[:, E : E + 2].astype(jnp.float32).T

    x = tokens.astype(jnp.float32)
    normed = rms_norm(x, gain_f[0]).astype(low)
    qkv = jnp.dot(normed, qkv_w, preferred_element_type=jnp.float32)
    query = (
        rotary(qkv[:, :QD].reshape(length, HEADS, HD))
        .astype(low)
        .reshape(length, KV_HEADS, group, HD)
    )
    keys = rotary(qkv[:, QD : QD + KVD].reshape(length, KV_HEADS, HD)).astype(low)
    values = qkv[:, QD + KVD :].reshape(length, KV_HEADS, HD).astype(low)
    attended, lses = attend_forward(query, keys, values, segs)
    attention = attended.reshape(length, QD)
    branch = jnp.dot(attention, out_w, preferred_element_type=jnp.float32)
    mid = x + branch
    normed2 = rms_norm(mid, gain_f[1]).astype(low)
    logits = jnp.dot(normed2, router_w, preferred_element_type=jnp.float32)
    picks = (routes[:, :, None] == jnp.arange(E, dtype=jnp.int32)[None, None, :]).any(axis=1)
    gates = jax.nn.softmax(jnp.where(picks, logits, -jnp.inf), axis=-1)

    rows, gates_all = spread_call(normed2, gates.T, reps)
    full_in = full_in.reshape(D, 2 * H)
    full_out = full_out.reshape(H, D)
    rows = rows.reshape(members * length, width)
    back = cot_all.reshape(members * length, width)
    gate = lax.dynamic_index_in_dim(
        gates_all.reshape(members, E, length), expert, axis=1, keepdims=False
    ).reshape(members * length, 1)
    moe_part, grad_rows, grad_gate, grad_in, grad_down = expert_call(
        rows, back, gate, full_in, full_out, 2 * length
    )
    def by_group(array):
        array = cut(array)
        return array.reshape((shards // GROUP, GROUP) + array.shape[1:])

    grad_in, grad_down = by_group(grad_in), by_group(grad_down)
    shape = (reps, GROUP, length, width)
    is_mine = (jnp.arange(E, dtype=jnp.int32) == expert).astype(jnp.float32)
    grad_gate_all = grad_gate.reshape(reps, GROUP, 1, length) * is_mine[:, None]
    moe, grad_normed2, grad_gates, far_in, far_down = collect_call(
        moe_part.reshape(shape),
        grad_rows.reshape(shape),
        grad_gate_all,
        grad_in,
        grad_down,
        shards,
        reps,
    )
    mixed = (mid + moe.astype(jnp.float32)).astype(low)

    grad_gates = grad_gates.T
    grad_logits = gates * (grad_gates - jnp.sum(grad_gates * gates, axis=-1, keepdims=True))
    grad_router = jnp.dot(normed2.astype(jnp.float32).T, grad_logits, precision=HIGH)
    grad_normed2 = grad_normed2.astype(jnp.float32) + jnp.dot(
        grad_logits, router_w.astype(jnp.float32).T, precision=HIGH
    )
    cot = cotangent.astype(jnp.float32)
    grad_mid_norm, grad_gain2 = norm_back(mid, gain_f[1], grad_normed2)
    grad_mid = cot + grad_mid_norm
    grad_branch = grad_mid.astype(low)
    grad_out_w = jnp.einsum("sq,sd->qd", attention, grad_branch, preferred_element_type=jnp.float32)
    grad_attention = jnp.einsum(
        "sd,qd->sq", grad_branch, out_w, preferred_element_type=jnp.float32
    ).astype(low)
    grad_query, grad_key, grad_value = attend_backward(
        query, keys, values, segs, lses, grad_attention.reshape(length, KV_HEADS, group, HD)
    )
    grad_query = rotary_back(grad_query.reshape(length, HEADS, HD))
    grad_key = rotary_back(grad_key)
    grad_qkv = jnp.concatenate(
        [
            grad_query.reshape(length, QD),
            grad_key.reshape(length, KVD),
            grad_value.reshape(length, KVD),
        ],
        axis=1,
    ).astype(low)
    grad_qkv_w = jnp.einsum("sd,sq->dq", normed, grad_qkv, preferred_element_type=jnp.float32)
    grad_normed = jnp.einsum("sq,dq->sd", grad_qkv, qkv_w, preferred_element_type=jnp.float32)
    grad_x_norm, grad_gain1 = norm_back(x, gain_f[0], grad_normed)
    tokens_grad = grad_mid + grad_x_norm

    grad_small = jnp.concatenate(
        [
            grad_router,
            jnp.stack([grad_gain1, grad_gain2], axis=1),
            jnp.zeros((D, 128 - E - 2), jnp.float32),
        ],
        axis=1,
    )

    grad_qkv_w, grad_out_w, grad_small, grad_in_all, grad_down_all = close_call(
        cut(grad_qkv_w),
        cut(grad_out_w),
        cut(grad_small),
        *[
            lax.dynamic_index_in_dim(array, shard // GROUP, 0, keepdims=False) + jnp.sum(away, axis=0)
            for array, away in ((grad_in, far_in), (grad_down, far_down))
        ],
        shards,
        reps,
    )
    grad_small = grad_small.astype(jnp.float32)
    grad_router = grad_small[:, :E]
    grad_gains = grad_small[:, E : E + 2].T
    qkv_m, qkv_v, qkv_new = adamw(
        wqkv, wqkv_first, wqkv_second, grad_qkv_w.astype(jnp.float32), 3.0 * D ** (-0.5), decay_rate
    )
    out_m, out_v, out_new = adamw(
        wo, wo_first, wo_second, grad_out_w.astype(jnp.float32), 3.0 * (QD // 64) ** (-0.5), decay_rate
    )
    rout_m, rout_v, rout_new = adamw(
        router, router_first, router_second, grad_router, 1.5 * D ** (-0.5), decay_rate
    )
    in_m, in_v, in_new = adamw(
        w_in, w_in_first, w_in_second, grad_in_all.astype(jnp.float32), 3.0 * D ** (-0.5), decay_rate
    )
    down_m, down_v, down_new = adamw(
        w_out,
        w_out_first,
        w_out_second,
        grad_down_all.astype(jnp.float32),
        3.0 * (H // 16) ** (-0.5),
        decay_rate,
    )
    gain_m, gain_v, gain_new = adamw(gains, gains_first, gains_second, grad_gains, 0.6, 0.0)
    return (
        mixed,
        tokens_grad,
        qkv_m,
        qkv_v,
        qkv_new,
        out_m,
        out_v,
        out_new,
        rout_m,
        rout_v,
        rout_new,
        in_m,
        in_v,
        in_new,
        down_m,
        down_v,
        down_new,
        gain_m,
        gain_v,
        gain_new,
    )


def solution(mesh):
    in_specs = (
        P(("rep", "shard"), None),
        P(("rep", "shard"), None),
        P(("rep", "shard"), None),
        P(("rep", "shard"), None),
        P("shard", None),
        P("shard", None),
        P("shard", None),
        P("shard", None),
        P("shard", None),
        P("shard", None),
        P("shard", None),
        P("shard", None),
        P("shard", None),
        P(None, "shard", None),
        P(None, "shard", None),
        P(None, "shard", None),
        P(None, "shard", None),
        P(None, "shard", None),
        P(None, "shard", None),
        P(None, "shard"),
        P(None, "shard"),
        P(None, "shard"),
    )
    out_specs = (
        P(("rep", "shard"), None),
        P(("rep", "shard"), None),
        P("shard", None),
        P("shard", None),
        P("shard", None),
        P("shard", None),
        P("shard", None),
        P("shard", None),
        P("shard", None),
        P("shard", None),
        P("shard", None),
        P(None, "shard", None),
        P(None, "shard", None),
        P(None, "shard", None),
        P(None, "shard", None),
        P(None, "shard", None),
        P(None, "shard", None),
        P(None, "shard"),
        P(None, "shard"),
        P(None, "shard"),
    )
    return jax.shard_map(
        functools.partial(on_device, mesh.shape["shard"], mesh.shape["rep"]), mesh=mesh, in_specs=in_specs, out_specs=out_specs, check_vma=False
    )
```

```python
import functools

import jax
import jax.numpy as jnp
from jax import lax
from jax.experimental import pallas as pl
from jax.experimental.pallas import tpu as pltpu
from jax.sharding import PartitionSpec as P

D = 1536
H = 512
HEADS = 24
KV_HEADS = 8
HD = 64
E = 16
TOP = 8
STEP = 10
QD = 1536
KVD = 512
GROUP = 4

HIGH = lax.Precision.HIGHEST
MESH = pl.DeviceIdType.MESH
norm_eps = 1e-06
beta_one = 0.9
beta_two = 0.95
adam_eps = 1e-08
decay_rate = 0.1
masked_score = -1e30
HOOK = 0
VMEM_BYTES = 56 * 2**20
EXPERT_VMEM_BYTES = 62 * 2**20


def flip(index, bit):
    step = 2**bit
    return index + (1 - 2 * ((index // step) % 2)) * step


def moved(place, bits):
    rep, shard = place
    for axis, bit in bits:
        if axis == "r":
            rep = flip(rep, bit)
        else:
            shard = flip(shard, bit)
    return (rep, shard)


def subsets(bits):
    result = [()]
    for bit in bits:
        result = result + [item + (bit,) for item in result]
    return result


def here():
    return (lax.axis_index("rep"), lax.axis_index("shard"))


def meet(places):
    barrier = pltpu.get_barrier_semaphore()
    for place in places:
        pl.semaphore_signal(barrier, inc=1, device_id=place, device_id_type=MESH)
    pl.semaphore_wait(barrier, len(places))


def start_copy(source, target, sems, index, place):
    copy = pltpu.make_async_remote_copy(
        src_ref=source,
        dst_ref=target,
        send_sem=sems[0].at[index],
        recv_sem=sems[1].at[index],
        device_id=place,
        device_id_type=MESH,
    )
    copy.start()
    return copy


class Counter:
    def __init__(self):
        self.value = 0

    def next(self):
        self.value += 1
        return self.value - 1


def gather_flows(flows, me, sems, count, hooks=()):
    sends = []
    for _ in gather_steps(flows, me, sems, count, sends, hooks):
        pass
    return sends


def gather_steps(flows, me, sems, count, sends, hooks=()):
    plans = []
    for order, source, target, local in flows:
        index = {}
        for level, bit in enumerate(order):
            for bits in subsets(order[:level]):
                if not (bit[0] == "r" and local(bits) and local(bits + (bit,))):
                    index[(level, bits)] = count.next()
        plans.append(index)
    deepest = max(len(order) for order, _, _, _ in flows)

    def push(flow, number, level, bits, ready):
        order, source, target, local = flow
        if (level, bits) not in plans[number]:
            return
        place = moved(me, bits)
        origin = source(place) if ready else target(place, bits)
        goal = target(place, bits + (order[level],))
        slot = plans[number][(level, bits)]
        sends.append(start_copy(origin, goal, sems, slot, moved(me, (order[level],))))

    for level in range(deepest):
        for number, flow in enumerate(flows):
            order, source, target, local = flow
            if level < len(order):
                for bits in subsets(order[:level]):
                    if local(bits):
                        push(flow, number, level, bits, True)
    yield
    hooks = dict(hooks)
    if -1 in hooks:
        hooks[-1]()
    for level in range(deepest):
        for turn in range(2**level):
            for number, flow in enumerate(flows):
                order, source, target, local = flow
                if level >= len(order):
                    continue
                bits = subsets(order[:level])[turn]
                key = (level, bits)
                if key not in plans[number]:
                    continue
                full = bits + (order[level],)
                place = moved(me, full)
                slot = plans[number][key]
                pltpu.make_async_remote_copy(
                    src_ref=target(place, full),
                    dst_ref=target(place, full),
                    send_sem=sems[0].at[slot],
                    recv_sem=sems[1].at[slot],
                    device_id=moved(me, (order[level],)),
                    device_id_type=MESH,
                ).wait_recv()
                for later in range(level + 1, len(order)):
                    push(flow, number, later, full, False)
                yield
        if level in hooks:
            hooks[level]()


def gather_slots(orders):
    return sum(2 ** len(order) - 1 for order in orders)


def add_into(target, first, second, block):
    rows = first.shape[0]

    def body(index, carry):
        window = pl.ds(pl.multiple_of(index * block, block), block)
        target[window] = first[window] + second[window]
        return carry

    if rows == block:
        target[...] = first[...] + second[...]
    else:
        lax.fori_loop(0, rows // block, body, 0)


def halving_slots(length):
    return 2 ** (length - 1) + 2**length - 1


def sum_flows(flows, me, sems, local_sems, count, local_count):
    sends = []
    for _ in sum_steps(flows, me, sems, local_sems, count, local_count, sends):
        pass
    return sends


def sum_steps(flows, me, sems, local_sems, count, local_count, sends):
    loads = []
    plans = []
    for order, source, buffer, block in flows:
        size = len(order)
        held = subsets(order[1:][::-1])
        place_of = {frozenset(bits): i for i, bits in enumerate(held)}
        index, slots, base = {}, {}, len(held)
        for level in range(size):
            for bits in subsets(order[level + 1 :][::-1]):
                index[(level, frozenset(bits))] = count.next()
                slots[(level, frozenset(bits))] = base
                base += 1
        plans.append((place_of, index, slots))
    deepest = max(len(order) for order, _, _, _ in flows)

    def turns(order, level):
        names = subsets(order[level + 1 :][::-1])
        return names[::-1]

    for turn in range(2 ** (deepest - 1)):
        for number, (order, source, buffer, block) in enumerate(flows):
            names = turns(order, 0)
            if turn >= len(names):
                continue
            bits = names[turn]
            key = frozenset(bits)
            place_of, index, slots = plans[number]
            sends.append(
                start_copy(
                    source(moved(me, bits + (order[0],))),
                    buffer.at[slots[(0, key)]],
                    sems,
                    index[(0, key)],
                    moved(me, (order[0],)),
                )
            )
            load = pltpu.make_async_copy(
                source(moved(me, bits)), buffer.at[place_of[key]], local_sems.at[local_count.next()]
            )
            load.start()
            loads.append(((number, key), load))
    waiting = dict(loads)
    yield
    for level in range(deepest):
        for turn in range(2 ** (deepest - 1 - level)):
            for number, (order, source, buffer, block) in enumerate(flows):
                if level >= len(order):
                    continue
                names = turns(order, level)
                if turn >= len(names):
                    continue
                bits = names[turn]
                key = frozenset(bits)
                place_of, index, slots = plans[number]
                slot = index[(level, key)]
                landed = buffer.at[slots[(level, key)]]
                pltpu.make_async_remote_copy(
                    src_ref=landed,
                    dst_ref=landed,
                    send_sem=sems[0].at[slot],
                    recv_sem=sems[1].at[slot],
                    device_id=moved(me, (order[level],)),
                    device_id_type=MESH,
                ).wait_recv()
                if level == 0:
                    waiting[(number, key)].wait()
                kept = buffer.at[place_of[key]]
                add_into(kept, kept, landed, block)
                if level + 1 < len(order) and order[level + 1] in key:
                    after = key - {order[level + 1]}
                    sends.append(
                        start_copy(
                            kept,
                            buffer.at[slots[(level + 1, after)]],
                            sems,
                            index[(level + 1, after)],
                            moved(me, (order[level + 1],)),
                        )
                    )
                yield


def rms_norm(value, gain):
    scale = lax.rsqrt(jnp.mean(value * value, axis=-1, keepdims=True) + norm_eps)
    return value * scale * gain


def norm_back(value, gain, grad):
    scale = lax.rsqrt(jnp.mean(value * value, axis=-1, keepdims=True) + norm_eps)
    normal = value * scale
    grad_gain = jnp.sum(grad * normal, axis=0)
    inner = grad * gain
    grad_value = scale * (inner - normal * jnp.mean(inner * normal, axis=-1, keepdims=True))
    return (grad_value, grad_gain)


def angle_tables(length, width):
    halfway = width // 2
    freqs = 10000.0 ** (-jnp.arange(halfway, dtype=jnp.float32) / halfway)
    angles = jnp.arange(length, dtype=jnp.float32)[:, None] * freqs[None, :]
    return (jnp.cos(angles)[:, None, :], jnp.sin(angles)[:, None, :], halfway)


def rotary(value):
    cosine, sine, halfway = angle_tables(value.shape[0], value.shape[-1])
    first = value[..., :halfway]
    second = value[..., halfway:]
    return jnp.concatenate(
        [first * cosine - second * sine, second * cosine + first * sine], axis=-1
    )


def rotary_back(grad):
    cosine, sine, halfway = angle_tables(grad.shape[0], grad.shape[-1])
    first = grad[..., :halfway]
    second = grad[..., halfway:]
    return jnp.concatenate(
        [first * cosine + second * sine, second * cosine - first * sine], axis=-1
    )


def block_scores(rows, keys, segs):
    places = jnp.arange(keys.shape[0], dtype=jnp.int32)
    scores = jnp.einsum(
        "sgrd,tgd->grst", rows, keys, preferred_element_type=jnp.float32
    ) * rows.shape[-1] ** (-0.5)
    allowed = (places[:, None] >= places[None, :]) & (segs[:, None] == segs[None, :])
    return jnp.where(allowed, scores, masked_score)


def attend_forward(query, keys, values, segs):
    length = query.shape[0]
    block = min(length, 512)

    def one_block(index):
        scores = block_scores(query, keys, segs)
        top = jnp.max(scores, axis=-1, keepdims=True)
        lse = top + jnp.log(jnp.sum(jnp.exp(scores - top), axis=-1, keepdims=True))
        probs = jnp.exp(scores - lse).astype(jnp.bfloat16)
        output = jnp.einsum("grst,tgd->sgrd", probs, values, preferred_element_type=jnp.float32)
        return (output.astype(jnp.bfloat16), lse)

    outputs, lses = lax.map(one_block, jnp.arange(length // block))
    return (outputs.reshape(query.shape), lses)


def attend_backward(query, keys, values, segs, lses, grad_out):
    length = query.shape[0]
    block = min(length, 512)
    scale = query.shape[-1] ** (-0.5)

    def step(carry, item):
        grad_key, grad_value = carry
        index, lse = item
        probs = jnp.exp(block_scores(query, keys, segs) - lse)
        grad_value = grad_value + jnp.einsum(
            "grst,sgrd->tgd",
            probs.astype(jnp.bfloat16),
            grad_out,
            preferred_element_type=jnp.float32,
        )
        grad_probs = jnp.einsum(
            "sgrd,tgd->grst", grad_out, values, preferred_element_type=jnp.float32
        )
        grad_scores = (
            probs * (grad_probs - jnp.sum(grad_probs * probs, axis=-1, keepdims=True))
        ).astype(jnp.bfloat16)
        grad_rows = (
            jnp.einsum("grst,tgd->sgrd", grad_scores, keys, preferred_element_type=jnp.float32)
            * scale
        )
        grad_key = (
            grad_key
            + jnp.einsum("grst,sgrd->tgd", grad_scores, query, preferred_element_type=jnp.float32)
            * scale
        )
        return ((grad_key, grad_value), grad_rows)

    zeros = jnp.zeros(keys.shape, jnp.float32)
    (grad_key, grad_value), grad_query = lax.scan(
        step, (zeros, zeros), (jnp.arange(length // block), lses)
    )
    return (grad_query.reshape(query.shape), grad_key, grad_value)


def adamw(weight, first, second, grad, rate, decay):
    first_new = beta_one * first + (1.0 - beta_one) * grad
    second_new = beta_two * second + (1.0 - beta_two) * grad * grad
    first_fix = 1.0 - beta_one**STEP
    second_fix = 1.0 - beta_two**STEP
    update = first_new / first_fix / (jnp.sqrt(second_new / second_fix) + adam_eps)
    return (first_new, second_new, weight - rate * (update + decay * weight))


X_BIT, C_BIT, Y_BIT, Z_BIT = ("r", 1), ("r", 0), ("s", 0), ("s", 1)
TURNED = (
    (X_BIT, Y_BIT, Z_BIT),
    (Y_BIT, Z_BIT, X_BIT),
    (Z_BIT, X_BIT, Y_BIT),
)
SUM_TURNED = (
    (X_BIT, Y_BIT, Z_BIT),
    (Y_BIT, Z_BIT, X_BIT),
    (Z_BIT, Y_BIT, X_BIT),
)
X_LAST = (
    (Z_BIT, Y_BIT, X_BIT),
    (Y_BIT, Z_BIT, X_BIT),
    (Z_BIT, Y_BIT, X_BIT),
)


POSITIONS = [
    frozenset(bits)
    for bits in (
        (X_BIT, Y_BIT, Z_BIT),
        (X_BIT, Y_BIT),
        (X_BIT, Z_BIT),
        (Y_BIT, Z_BIT),
        (X_BIT,),
        (Y_BIT,),
        (Z_BIT,),
        (),
    )
]


def position(bits):
    return POSITIONS.index(frozenset(bits))


def far_bits(shards):
    return tuple(("s", i) for i in range(2, shards.bit_length() - 1))


def only_self(bits):
    return not bits


def same_shard(bits):
    return all(axis == "r" for axis, _ in bits)


def token_flows(source, target, orders):
    width = source.shape[-1] // len(orders)
    flows = []
    for number, order in enumerate(orders):
        columns = pl.ds(number * width, width)
        flows.append(
            (
                order,
                lambda place, columns=columns: source.at[:, columns],
                lambda place, bits, columns=columns: target.at[position(bits), :, columns],
                only_self,
            )
        )
    return flows


def share_flows(source, target, orders, reps):
    height = source.shape[0] // len(orders)
    width = source.shape[1] // reps
    flows = []

    def columns_of(place):
        return pl.ds(pl.multiple_of(place[0] * width, 128), width)

    for number, order in enumerate(orders):
        rows = pl.ds(number * height, height)
        flows.append(
            (
                order,
                lambda place, rows=rows: source.at[rows, columns_of(place)],
                lambda place, bits, rows=rows: target.at[place[1], rows, columns_of(place)],
                same_shard,
            )
        )
    return flows


def neighbours(me, bits):
    return [moved(me, (bit,)) for bit in bits]


def open_kernel(shards, reps, *refs):
    qkv, out, small, w_in, w_out, cot = refs[:6]
    qkv_all, out_all, small_all, in_all, down_all, cot_all = refs[6:12]
    send, recv, local = refs[12:]
    me = here()
    sems = (send, recv)
    far = far_bits(shards)
    bits = (Y_BIT, Z_BIT) + far
    partners = [moved(me, item) for item in subsets(bits)[1:]][::-1]
    meet(neighbours(me, (X_BIT, C_BIT)) + partners)
    count = Counter()
    own = me[1]
    here_copies = [
        (qkv, qkv_all.at[own]),
        (out, out_all.at[own]),
        (small, small_all.at[own]),
        (w_in.at[own % GROUP], in_all.at[1, own]),
        (w_out.at[own % GROUP], down_all.at[1, own]),
        (cot, cot_all.at[position(())]),
    ]
    for number, (source, target) in enumerate(here_copies):
        pltpu.make_async_copy(source, target, local.at[number]).start()
    sends = []
    orders = [far + order + (C_BIT,) for order in X_LAST]
    flows = share_flows(qkv, qkv_all, orders, reps) + share_flows(out, out_all, orders, reps)
    flows.append(
        (far + (Y_BIT, Z_BIT), lambda place: small, lambda place, bits: small_all.at[place[1]], only_self)
    )
    flows += token_flows(cot, cot_all, X_LAST)
    direct = []

    def send_experts(chosen):
        for place in chosen:
            for source, target in ((w_in, in_all), (w_out, down_all)):
                slot = count.next()
                sends.append(
                    start_copy(source.at[place[1] % GROUP], target.at[1, own], sems, slot, place)
                )
                direct.append((target, place[1], slot, place))

    hooks = {HOOK: functools.partial(send_experts, partners)}
    sends += gather_flows(flows, me, sems, count, hooks)
    twin = moved(me, (C_BIT,))
    for source, target in ((w_in, in_all), (w_out, down_all)):
        sends.append(
            start_copy(source.at[own % GROUP], target.at[0, own], sems, count.next(), twin)
        )
    passed = [(target, own, count.value - 2 + i) for i, target in enumerate((in_all, down_all))]
    for target, index, slot, place in direct:
        landed = target.at[1, index]
        pltpu.make_async_remote_copy(
            src_ref=landed,
            dst_ref=landed,
            send_sem=send.at[slot],
            recv_sem=recv.at[slot],
            device_id=place,
            device_id_type=MESH,
        ).wait_recv()
        slot = count.next()
        sends.append(start_copy(landed, target.at[0, index], sems, slot, twin))
        passed.append((target, index, slot))
    for target, index, slot in passed:
        landed = target.at[0, index]
        pltpu.make_async_remote_copy(
            src_ref=landed,
            dst_ref=landed,
            send_sem=send.at[slot],
            recv_sem=recv.at[slot],
            device_id=twin,
            device_id_type=MESH,
        ).wait_recv()
    for copy in sends:
        copy.wait_send()
    for number, (source, target) in enumerate(here_copies):
        pltpu.make_async_copy(source, target, local.at[number]).wait()


def anywhere(count):
    return [pl.BlockSpec(memory_space=pl.ANY)] * count


def open_call(qkv, out, small, w_in, w_out, cot, shards, reps):
    def grown(array):
        return jax.ShapeDtypeStruct((shards,) + array.shape[-2:], array.dtype)

    shapes = [grown(array) for array in (qkv, out, small)]
    shapes += [
        jax.ShapeDtypeStruct((2, shards) + array.shape[1:], array.dtype) for array in (w_in, w_out)
    ]
    shapes.append(jax.ShapeDtypeStruct((len(POSITIONS),) + cot.shape, cot.dtype))
    slots = 6 * (shards * reps - 1) + shards + 4 * shards + 3 * 7
    return pl.pallas_call(
        functools.partial(open_kernel, shards, reps),
        out_shape=shapes,
        in_specs=anywhere(6),
        out_specs=anywhere(6),
        scratch_shapes=[
            pltpu.SemaphoreType.DMA((slots,)),
            pltpu.SemaphoreType.DMA((slots,)),
            pltpu.SemaphoreType.DMA((6,)),
        ],
        compiler_params=pltpu.CompilerParams(
            collective_id=0, has_side_effects=True, vmem_limit_bytes=VMEM_BYTES
        ),
        name="open_gather",
    )(qkv, out, small, w_in, w_out, cot)


def spread_kernel(*refs):
    rows, gate, rows_all, gate_all, send, recv, local = refs
    me = here()
    sems = (send, recv)
    meet(neighbours(me, (X_BIT, Y_BIT, Z_BIT)))
    count = Counter()
    copies = [
        (rows, rows_all.at[position(())]),
        (gate, gate_all.at[position(())]),
    ]
    for number, (source, target) in enumerate(copies):
        pltpu.make_async_copy(source, target, local.at[number]).start()
    flows = token_flows(rows, rows_all, TURNED)
    flows.append(
        (
            TURNED[0],
            lambda place: gate,
            lambda place, bits: gate_all.at[position(bits)],
            only_self,
        )
    )
    for copy in gather_flows(flows, me, sems, count):
        copy.wait_send()
    for number, (source, target) in enumerate(copies):
        pltpu.make_async_copy(source, target, local.at[number]).wait()


def spread_call(rows, gate):
    slots = 4 * 7
    return pl.pallas_call(
        spread_kernel,
        out_shape=[
            jax.ShapeDtypeStruct((len(POSITIONS),) + array.shape, array.dtype)
            for array in (rows, gate)
        ],
        in_specs=anywhere(2),
        out_specs=anywhere(2),
        scratch_shapes=[
            pltpu.SemaphoreType.DMA((slots,)),
            pltpu.SemaphoreType.DMA((slots,)),
            pltpu.SemaphoreType.DMA((2,)),
        ],
        compiler_params=pltpu.CompilerParams(
            collective_id=1, has_side_effects=True, vmem_limit_bytes=VMEM_BYTES
        ),
        name="spread_tokens",
    )(rows, gate)


def dot(a, b, dims=((1,), (0,))):
    return lax.dot_general(a, b, (dims, ((), ())), preferred_element_type=jnp.float32)


class PieceSum:
    def __init__(self, order, buffer, block, me, sems, count):
        self.order, self.buffer, self.block, self.me, self.sems = order, buffer, block, me, sems
        self.slots, self.index = {}, {}
        for level in range(len(order)):
            for bits in subsets(order[level + 1 :]):
                key = (level, frozenset(bits))
                self.slots[key] = len(POSITIONS) + len(self.slots)
                self.index[key] = count.next()

    def copy(self, level, bits):
        bit = self.order[level]
        key = (level, bits - {bit})
        return pltpu.make_async_remote_copy(
            src_ref=self.buffer.at[position(bits)],
            dst_ref=self.buffer.at[self.slots[key]],
            send_sem=self.sems[0].at[self.index[key]],
            recv_sem=self.sems[1].at[self.index[key]],
            device_id=moved(self.me, (bit,)),
            device_id_type=MESH,
        )

    def computed(self, bits):
        if self.order[0] in bits:
            self.copy(0, bits).start()

    def settle(self, level, bits):
        if any(bit in bits for bit in self.order[: level + 1]):
            return
        self.copy(level, bits | {self.order[level]}).wait_recv()
        kept = self.buffer.at[position(bits)]
        add_into(kept, kept, self.buffer.at[self.slots[(level, bits)]], self.block)
        if level + 1 < len(self.order) and self.order[level + 1] in bits:
            self.copy(level + 1, bits).start()

    def finish(self):
        for level, bits in self.index:
            self.copy(level, bits | {self.order[level]}).wait_send()


BLOCKS = 4


def expert_kernel(*refs):
    rows_ref, back_ref, gate_ref, in_ref, out_ref = refs[:5]
    moe_sum, grad_sum, mark_sum, half_in, half_out, grad_in, grad_out = refs[5:12]
    grad_buffers, moe_buffers, mark_buffer = refs[12:15], refs[15:18], refs[18]
    in_total, out_total, stage_in, stage_out, scaled, send, recv, local = refs[19:]
    low = jnp.bfloat16
    step = pl.program_id(0)
    block = step % BLOCKS
    me = here()
    twin = moved(me, (C_BIT,))
    sems = (send, recv)
    count = Counter()
    length = rows_ref.shape[0] // 2
    sums = [
        PieceSum(order, buffer, 128, me, sems, count)
        for turned, buffers in ((TURNED, grad_buffers), (TURNED, moe_buffers))
        for order, buffer in zip(turned, buffers)
    ]
    sums.append(PieceSum(TURNED[0], mark_buffer, length, me, sems, count))
    exchanged = [(stage_in, half_in, count.next()), (stage_out, half_out, count.next())]

    def halves():
        return [
            pltpu.make_async_remote_copy(
                src_ref=stage,
                dst_ref=half,
                send_sem=send.at[slot],
                recv_sem=recv.at[slot],
                device_id=twin,
                device_id_type=MESH,
            )
            for stage, half, slot in exchanged
        ]

    @pl.when(step == 0)
    def _():
        meet(neighbours(me, (X_BIT, C_BIT, Y_BIT, Z_BIT)))
        in_total[...] = jnp.zeros_like(in_total)
        out_total[...] = jnp.zeros_like(out_total)
        for buffer in grad_buffers + moe_buffers + (mark_buffer,):
            kept = buffer.at[pl.ds(0, len(POSITIONS))]
            kept[...] = jnp.zeros_like(kept)

    rows = rows_ref[...]
    gate = gate_ref[0]
    hidden_in = dot(rows, in_ref[0])
    gate_part = hidden_in[:, :H]
    up_part = hidden_in[:, H:]
    sigma = jax.nn.sigmoid(gate_part)
    active = gate_part * sigma
    hidden = (active * up_part).astype(low)
    width = rows.shape[1] // 3
    pair = pl.ds(2 * block, 2)

    def add_pieces(buffer, value):
        value = value.reshape((2, length) + value.shape[1:])
        buffer[pair] = (buffer[pair].astype(jnp.float32) + value).astype(low)

    mark = jnp.zeros((2 * length, 1), jnp.float32)
    for third in range(3):
        columns = slice(third * width, (third + 1) * width)
        result = dot(hidden, out_ref[0, :, columns])
        back = back_ref[:, columns].astype(jnp.float32)
        mark += jnp.sum(back * result, axis=1, keepdims=True)
        add_pieces(moe_buffers[third], gate * result)
        scaled[:, columns] = (gate * back).astype(low)
    expert = jnp.where(step < BLOCKS, twin[0], me[0]) * GROUP + me[1] % GROUP
    mark_low = mark.astype(low).astype(jnp.float32)
    lane = lax.broadcasted_iota(jnp.int32, (2 * length, 128), 1)
    add_pieces(
        mark_buffer,
        jnp.where(lane == expert, mark_low, jnp.where(lane == expert + E, mark - mark_low, 0.0)),
    )
    grad_result = scaled[...]
    grad_hidden = dot(grad_result, out_ref[0], ((1,), (1,)))
    out_total[...] += dot(hidden, grad_result, ((0,), (0,)))
    grad_gate_part = grad_hidden * up_part * sigma * (1.0 + gate_part * (1.0 - sigma))
    grad_up_part = grad_hidden * active
    grad_rows = jnp.concatenate([grad_gate_part, grad_up_part], axis=1).astype(low)
    for third in range(3):
        columns = slice(third * width, (third + 1) * width)
        add_pieces(grad_buffers[third], dot(grad_rows, in_ref[0, columns], ((1,), (1,))))
    in_total[...] += dot(rows, grad_rows, ((0,), (0,)))

    @pl.when(step == BLOCKS - 1)
    def _():
        stage_in[...] = in_total[...].astype(low)
        stage_out[...] = out_total[...].astype(low)
        for copy in halves():
            copy.start()
        in_total[...] = jnp.zeros_like(in_total)
        out_total[...] = jnp.zeros_like(out_total)

    def settle(level, number):
        for bits in POSITIONS[2 * number : 2 * number + 2]:
            for item in sums:
                item.settle(level, bits)

    for number in range(BLOCKS):

        @pl.when(step == BLOCKS + number)
        def _():
            for bits in POSITIONS[2 * number : 2 * number + 2]:
                for item in sums:
                    item.computed(bits)
            if number >= 1:
                settle(0, number - 1)
            if number >= 2:
                settle(1, number - 2)

    @pl.when(step == 2 * BLOCKS - 1)
    def _():
        settle(0, BLOCKS - 1)
        for number in (BLOCKS - 2, BLOCKS - 1):
            settle(1, number)
        loads = []
        for number, (copy, (stage, half, _)) in enumerate(zip(halves(), exchanged)):
            copy.wait()
            load = pltpu.make_async_copy(half, stage, local.at[number])
            load.start()
            loads.append(load)
        stores = []
        for number, (total, stage, goal) in enumerate(
            ((in_total, stage_in, grad_in), (out_total, stage_out, grad_out))
        ):
            loads[number].wait()
            stage[...] = (total[...] + stage[...].astype(jnp.float32)).astype(low)
            store = pltpu.make_async_copy(stage, goal, local.at[2 + number])
            store.start()
            stores.append(store)
        for number in range(BLOCKS):
            settle(2, number)
        own = position(())
        for item, goal in zip(
            sums,
            [grad_sum.at[:, pl.ds(i * width, width)] for i in range(3)]
            + [moe_sum.at[:, pl.ds(i * width, width)] for i in range(3)]
            + [mark_sum],
        ):
            store = pltpu.make_async_copy(item.buffer.at[own], goal, local.at[len(stores) + 2])
            store.start()
            stores.append(store)
        for item in sums:
            item.finish()
        for store in stores:
            store.wait()


def expert_call(rows, back, gate, full_in, full_out):
    _, length, width = rows.shape
    count = len(POSITIONS) * length
    low = jnp.bfloat16
    block = 2 * length
    rows, back = rows.reshape(count, width), back.reshape(count, width)

    def weights(array):
        return pl.BlockSpec(
            (1,) + array.shape[1:], lambda i: (i // BLOCKS, 0, 0), pipeline_mode=pl.Buffered(1)
        )

    def like(array):
        return jax.ShapeDtypeStruct(array.shape[1:], low)

    sequence = jax.ShapeDtypeStruct((length, width), low)
    pieces = 2 * len(POSITIONS) - 1
    slots = 7 * 7 + 2
    return pl.pallas_call(
        expert_kernel,
        grid=(2 * BLOCKS,),
        out_shape=[
            sequence,
            sequence,
            jax.ShapeDtypeStruct((length, 128), low),
            like(full_in),
            like(full_out),
            like(full_in),
            like(full_out),
        ],
        in_specs=[
            pl.BlockSpec((block, width), lambda i: (i % BLOCKS, 0)),
            pl.BlockSpec((block, width), lambda i: (i % BLOCKS, 0)),
            pl.BlockSpec((1, block, 1), lambda i: (i // BLOCKS, i % BLOCKS, 0)),
            weights(full_in),
            weights(full_out),
        ],
        out_specs=anywhere(7),
        scratch_shapes=[pltpu.VMEM((pieces, length, width // 3), low)] * 6
        + [
            pltpu.VMEM((pieces, length, 128), low),
            pltpu.VMEM(full_in.shape[1:], jnp.float32),
            pltpu.VMEM(full_out.shape[1:], jnp.float32),
            pltpu.VMEM(full_in.shape[1:], low),
            pltpu.VMEM(full_out.shape[1:], low),
            pltpu.VMEM((block, width), low),
            pltpu.SemaphoreType.DMA((slots,)),
            pltpu.SemaphoreType.DMA((slots,)),
            pltpu.SemaphoreType.DMA((12,)),
        ],
        compiler_params=pltpu.CompilerParams(
            collective_id=2,
            has_side_effects=True,
            vmem_limit_bytes=EXPERT_VMEM_BYTES,
            dimension_semantics=("arbitrary",),
        ),
        name="experts",
    )(rows, back, gate, full_in, full_out)


def close_kernel(shards, reps, *refs):
    qkv, out, small, g_in, g_down = refs[:5]
    qkv_sum, out_sum, small_sum, in_sum, down_sum = refs[5:10]
    dense = refs[10:16]
    tiny, in_land, down_land, in_own, down_own, send, recv, local = refs[16:]
    me = here()
    sems = (send, recv)
    far = far_bits(shards)
    partners = [moved(me, item) for item in subsets((Y_BIT, Z_BIT) + far)[1:]]
    meet(neighbours(me, (X_BIT, C_BIT)) + partners)
    count, local_count = Counter(), Counter()
    sends = []
    flows = []
    results = []
    for which, (source, target) in enumerate(((qkv, qkv_sum), (out, out_sum))):
        height = source.shape[1] // len(SUM_TURNED)
        width = source.shape[2] // reps
        for number, order in enumerate(SUM_TURNED):
            rows = pl.ds(number * height, height)
            buffer = dense[which * 3 + number]

            def piece(place, source=source, rows=rows, width=width):
                return source.at[place[1], rows, pl.ds(pl.multiple_of(place[0] * width, 128), width)]

            def goal(place, bits=(), target=target, rows=rows, width=width):
                return target.at[rows, pl.ds(pl.multiple_of(place[0] * width, 128), width)]

            flows.append(((C_BIT,) + order + far, piece, buffer, height))
            results.append((buffer, goal))
    tiny_order = (Y_BIT, Z_BIT) + far
    flows.append((tiny_order, lambda place: small.at[place[1]], tiny, 16))
    tail = []

    early = [flow for flow in flows if flow[0][:2] == (C_BIT, X_BIT)]
    late = [flow for flow in flows if flow[0][:2] != (C_BIT, X_BIT)]
    first = sum_steps(early, me, sems, local, count, local_count, sends)
    second = sum_steps(late, me, sems, local, count, local_count, sends)

    def last_steps():
        for buffer, goal in results:
            store = pltpu.make_async_copy(buffer.at[0], goal(me), local.at[local_count.next()])
            store.start()
            tail.append(store)
        columns = [
            ((X_BIT, C_BIT), lambda place, buffer=buffer: buffer.at[0], goal, only_self)
            for buffer, goal in results
        ]
        yield from gather_steps(columns, me, sems, count, sends)
        base = halving_slots(len(tiny_order))
        current = 0
        for bit in (X_BIT, C_BIT):
            slot = count.next()
            landed = tiny.at[base]
            copy = start_copy(tiny.at[current], landed, sems, slot, moved(me, (bit,)))
            copy.wait()
            add_into(tiny.at[base + 1], tiny.at[current], landed, 16)
            current = base + 1
            base += 2
            yield
        store = pltpu.make_async_copy(tiny.at[current], small_sum, local.at[local_count.next()])
        store.start()
        tail.append(store)

    arrays = ((g_in, in_land, in_own, in_sum), (g_down, down_land, down_own, down_sum))
    waves = subsets((Z_BIT, Y_BIT))

    def expert_steps():
        waiting = {}
        for items in (subsets(far)[:1], subsets(far)[1:]):
            for number, near in enumerate(waves):
                for item in items:
                    place = moved(me, near + item)
                    for source, landed, _, _ in arrays:
                        if near + item:
                            slot = count.next()
                            sends.append(
                                start_copy(source.at[place[1]], landed.at[me[1]], sems, slot, place)
                            )
                            wait = pltpu.make_async_remote_copy(
                                src_ref=landed.at[place[1]],
                                dst_ref=landed.at[place[1]],
                                send_sem=send.at[slot],
                                recv_sem=recv.at[slot],
                                device_id=place,
                                device_id_type=MESH,
                            ).wait_recv
                        else:
                            load = pltpu.make_async_copy(
                                source.at[me[1]], landed.at[me[1]], local.at[local_count.next()]
                            )
                            load.start()
                            wait = load.wait
                        waiting.setdefault(number, []).append(wait)
        yield
        relays = []
        for number, near in enumerate(waves):
            for wait in waiting[number]:
                wait()
            place = moved(me, near)
            expert = place[1] % GROUP
            for _, landed, held, target in arrays:
                total = landed.at[place[1]]
                for item in subsets(far)[1:]:
                    part = landed.at[moved(place, item)[1]]
                    add_into(held.at[number], total, part, part.shape[0])
                    total = held.at[number]

                def goal(where, bits=(), target=target, expert=expert):
                    return target.at[where[0] * GROUP + expert]

                store = pltpu.make_async_copy(total, goal(me), local.at[local_count.next()])
                store.start()
                tail.append(store)
                flow = ((X_BIT, C_BIT), lambda where, total=total: total, goal, only_self)
                relay = gather_steps([flow], me, sems, count, sends)
                relays.append(relay)
                next(relay)
            yield
        for relay in relays:
            for _ in relay:
                yield

    experts = expert_steps()
    for run in (experts, first, second):
        next(run)
    for _ in range(len(early) * reps * shards // 2):
        next(first)
    mixed = [(second, 8), (first, 2), (experts, 1)]
    alive = [run for run, _ in mixed]
    while alive:
        for run, turns in mixed:
            for _ in range(turns):
                if run in alive and next(run, "end") == "end":
                    alive.remove(run)
    for _ in last_steps():
        pass
    for copy in sends:
        copy.wait_send()
    for copy in tail:
        copy.wait()


def close_call(qkv, out, small, g_in, g_down, shards, reps):
    far = far_bits(shards)
    size = 4 + len(far)
    pieces = halving_slots(size)

    def dense_buffer(array):
        return [
            pltpu.VMEM((pieces, array.shape[1] // 3, array.shape[2] // reps), array.dtype)
        ] * 3

    tiny_pieces = halving_slots(2 + len(far)) + 4
    slots = 7 * (2**size - 1) + 2 * shards + 14 * 3 + 4
    return pl.pallas_call(
        functools.partial(close_kernel, shards, reps),
        out_shape=[jax.ShapeDtypeStruct(array.shape[1:], array.dtype) for array in (qkv, out, small)]
        + [
            jax.ShapeDtypeStruct((reps * GROUP,) + array.shape[1:], array.dtype)
            for array in (g_in, g_down)
        ],
        in_specs=anywhere(5),
        out_specs=anywhere(5),
        scratch_shapes=dense_buffer(qkv)
        + dense_buffer(out)
        + [
            pltpu.VMEM((tiny_pieces,) + small.shape[1:], small.dtype),
            pltpu.VMEM(g_in.shape, g_in.dtype),
            pltpu.VMEM(g_down.shape, g_down.dtype),
            pltpu.VMEM((GROUP,) + g_in.shape[1:], g_in.dtype),
            pltpu.VMEM((GROUP,) + g_down.shape[1:], g_down.dtype),
            pltpu.SemaphoreType.DMA((slots,)),
            pltpu.SemaphoreType.DMA((slots,)),
            pltpu.SemaphoreType.DMA((7 * 2 ** (size - 1) + 32,)),
        ],
        compiler_params=pltpu.CompilerParams(
            collective_id=3, has_side_effects=True, vmem_limit_bytes=VMEM_BYTES
        ),
        name="close_sums",
    )(qkv, out, small, g_in, g_down)


def on_device(
    shards,
    reps,
    tokens,
    segments,
    routes,
    cotangent,
    wqkv,
    wqkv_first,
    wqkv_second,
    wo,
    wo_first,
    wo_second,
    router,
    router_first,
    router_second,
    w_in,
    w_in_first,
    w_in_second,
    w_out,
    w_out_first,
    w_out_second,
    gains,
    gains_first,
    gains_second,
):
    length, width = tokens.shape
    group = HEADS // KV_HEADS
    segs = segments[0]
    rep, shard = here()
    low = jnp.bfloat16

    def cut(array):
        return array.astype(low).reshape((shards, array.shape[0] // shards) + array.shape[1:])

    small = jnp.concatenate(
        [router, gains.T, jnp.zeros((router.shape[0], 128 - E - 2), jnp.float32)], axis=1
    ).astype(low)
    mine_in = lax.dynamic_slice_in_dim(w_in, rep * GROUP, GROUP, 0).astype(low)
    mine_out = lax.dynamic_slice_in_dim(w_out, rep * GROUP, GROUP, 0).astype(low)
    qkv_w, out_w, small_w, full_in, full_out, cot_all = open_call(
        wqkv.astype(low), wo.astype(low), small, mine_in, mine_out, cotangent, shards, reps
    )
    qkv_w = qkv_w.reshape(D, -1)
    out_w = out_w.reshape(QD, D)
    small_w = small_w.reshape(D, 128)
    router_w = small_w[:, :E]
    gain_f = small_w[:, E : E + 2].astype(jnp.float32).T

    x = tokens.astype(jnp.float32)
    normed = rms_norm(x, gain_f[0]).astype(low)
    qkv = jnp.dot(normed, qkv_w, preferred_element_type=jnp.float32)
    query = (
        rotary(qkv[:, :QD].reshape(length, HEADS, HD))
        .astype(low)
        .reshape(length, KV_HEADS, group, HD)
    )
    keys = rotary(qkv[:, QD : QD + KVD].reshape(length, KV_HEADS, HD)).astype(low)
    values = qkv[:, QD + KVD :].reshape(length, KV_HEADS, HD).astype(low)
    attended, lses = attend_forward(query, keys, values, segs)
    attention = attended.reshape(length, QD)
    branch = jnp.dot(attention, out_w, preferred_element_type=jnp.float32)
    mid = x + branch
    normed2 = rms_norm(mid, gain_f[1]).astype(low)
    logits = jnp.dot(normed2, router_w, preferred_element_type=jnp.float32)
    picks = (routes[:, :, None] == jnp.arange(E, dtype=jnp.int32)[None, None, :]).any(axis=1)
    gates = jax.nn.softmax(jnp.where(picks, logits, -jnp.inf), axis=-1)

    rows, gates_all = spread_call(normed2, gates.T)
    gate = jnp.stack(
        [
            lax.dynamic_index_in_dim(gates_all, flip(rep, 0) * GROUP + shard % GROUP, 1, False),
            lax.dynamic_index_in_dim(gates_all, rep * GROUP + shard % GROUP, 1, False),
        ]
    ).reshape(2, -1, 1)
    moe, grad_normed2, marks, _, _, grad_in, grad_down = expert_call(
        rows, cot_all, gate, full_in.reshape(2, D, 2 * H), full_out.reshape(2, H, D)
    )
    marks = marks.astype(jnp.float32)
    grad_gates = marks[:, :E] + marks[:, E : 2 * E]
    mixed = (mid + moe.astype(jnp.float32)).astype(low)

    grad_logits = gates * (grad_gates - jnp.sum(grad_gates * gates, axis=-1, keepdims=True))
    grad_router = jnp.dot(normed2.astype(jnp.float32).T, grad_logits, precision=HIGH)
    grad_normed2 = grad_normed2.astype(jnp.float32) + jnp.dot(
        grad_logits, router_w.astype(jnp.float32).T, precision=HIGH
    )
    cot = cotangent.astype(jnp.float32)
    grad_mid_norm, grad_gain2 = norm_back(mid, gain_f[1], grad_normed2)
    grad_mid = cot + grad_mid_norm
    grad_branch = grad_mid.astype(low)
    grad_out_w = jnp.einsum("sq,sd->qd", attention, grad_branch, preferred_element_type=jnp.float32)
    grad_attention = jnp.einsum(
        "sd,qd->sq", grad_branch, out_w, preferred_element_type=jnp.float32
    ).astype(low)
    grad_query, grad_key, grad_value = attend_backward(
        query, keys, values, segs, lses, grad_attention.reshape(length, KV_HEADS, group, HD)
    )
    grad_query = rotary_back(grad_query.reshape(length, HEADS, HD))
    grad_key = rotary_back(grad_key)
    grad_qkv = jnp.concatenate(
        [
            grad_query.reshape(length, QD),
            grad_key.reshape(length, KVD),
            grad_value.reshape(length, KVD),
        ],
        axis=1,
    ).astype(low)
    grad_qkv_w = jnp.einsum("sd,sq->dq", normed, grad_qkv, preferred_element_type=jnp.float32)
    grad_normed = jnp.einsum("sq,dq->sd", grad_qkv, qkv_w, preferred_element_type=jnp.float32)
    grad_x_norm, grad_gain1 = norm_back(x, gain_f[0], grad_normed)
    tokens_grad = grad_mid + grad_x_norm

    grad_small = jnp.concatenate(
        [
            grad_router,
            jnp.stack([grad_gain1, grad_gain2], axis=1),
            jnp.zeros((D, 128 - E - 2), jnp.float32),
        ],
        axis=1,
    )

    grad_qkv_w, grad_out_w, grad_small, grad_in_all, grad_down_all = close_call(
        cut(grad_qkv_w),
        cut(grad_out_w),
        cut(grad_small),
        cut(grad_in),
        cut(grad_down),
        shards,
        reps,
    )
    grad_small = grad_small.astype(jnp.float32)
    grad_router = grad_small[:, :E]
    grad_gains = grad_small[:, E : E + 2].T
    qkv_m, qkv_v, qkv_new = adamw(
        wqkv, wqkv_first, wqkv_second, grad_qkv_w.astype(jnp.float32), 3.0 * D ** (-0.5), decay_rate
    )
    out_m, out_v, out_new = adamw(
        wo, wo_first, wo_second, grad_out_w.astype(jnp.float32), 3.0 * (QD // 64) ** (-0.5), decay_rate
    )
    rout_m, rout_v, rout_new = adamw(
        router, router_first, router_second, grad_router, 1.5 * D ** (-0.5), decay_rate
    )
    in_m, in_v, in_new = adamw(
        w_in, w_in_first, w_in_second, grad_in_all.astype(jnp.float32), 3.0 * D ** (-0.5), decay_rate
    )
    down_m, down_v, down_new = adamw(
        w_out,
        w_out_first,
        w_out_second,
        grad_down_all.astype(jnp.float32),
        3.0 * (H // 16) ** (-0.5),
        decay_rate,
    )
    gain_m, gain_v, gain_new = adamw(gains, gains_first, gains_second, grad_gains, 0.6, 0.0)
    return (
        mixed,
        tokens_grad,
        qkv_m,
        qkv_v,
        qkv_new,
        out_m,
        out_v,
        out_new,
        rout_m,
        rout_v,
        rout_new,
        in_m,
        in_v,
        in_new,
        down_m,
        down_v,
        down_new,
        gain_m,
        gain_v,
        gain_new,
    )


def solution(mesh):
    in_specs = (
        P(("rep", "shard"), None),
        P(("rep", "shard"), None),
        P(("rep", "shard"), None),
        P(("rep", "shard"), None),
        P("shard", None),
        P("shard", None),
        P("shard", None),
        P("shard", None),
        P("shard", None),
        P("shard", None),
        P("shard", None),
        P("shard", None),
        P("shard", None),
        P(None, "shard", None),
        P(None, "shard", None),
        P(None, "shard", None),
        P(None, "shard", None),
        P(None, "shard", None),
        P(None, "shard", None),
        P(None, "shard"),
        P(None, "shard"),
        P(None, "shard"),
    )
    out_specs = (
        P(("rep", "shard"), None),
        P(("rep", "shard"), None),
        P("shard", None),
        P("shard", None),
        P("shard", None),
        P("shard", None),
        P("shard", None),
        P("shard", None),
        P("shard", None),
        P("shard", None),
        P("shard", None),
        P(None, "shard", None),
        P(None, "shard", None),
        P(None, "shard", None),
        P(None, "shard", None),
        P(None, "shard", None),
        P(None, "shard", None),
        P(None, "shard"),
        P(None, "shard"),
        P(None, "shard"),
    )
    return jax.shard_map(
        functools.partial(on_device, mesh.shape["shard"], mesh.shape["rep"]), mesh=mesh, in_specs=in_specs, out_specs=out_specs, check_vma=False
    )
```

```python
import functools

import jax
import jax.numpy as jnp
from jax import lax
from jax.experimental import pallas as pl
from jax.experimental.pallas import tpu as pltpu
from jax.sharding import PartitionSpec as P

D = 1536
H = 512
HEADS = 24
KV_HEADS = 8
HD = 64
E = 16
TOP = 8
STEP = 10
QD = 1536
KVD = 512
GROUP = 4

HIGH = lax.Precision.HIGHEST
MESH = pl.DeviceIdType.MESH
norm_eps = 1e-06
beta_one = 0.9
beta_two = 0.95
adam_eps = 1e-08
decay_rate = 0.1
masked_score = -1e30
HOOK = 0
OUT_STEPS = (0, 24, 24, 24)
EARLY = (1, 1, 1, 1)
VMEM_BYTES = 56 * 2**20
EXPERT_VMEM_BYTES = 62 * 2**20


def flip(index, bit):
    step = 2**bit
    return index + (1 - 2 * ((index // step) % 2)) * step


def moved(place, bits):
    rep, shard = place
    for axis, bit in bits:
        if axis == "r":
            rep = flip(rep, bit)
        else:
            shard = flip(shard, bit)
    return (rep, shard)


def subsets(bits):
    result = [()]
    for bit in bits:
        result = result + [item + (bit,) for item in result]
    return result


def here():
    return (lax.axis_index("rep"), lax.axis_index("shard"))


def meet(places):
    barrier = pltpu.get_barrier_semaphore()
    for place in places:
        pl.semaphore_signal(barrier, inc=1, device_id=place, device_id_type=MESH)
    pl.semaphore_wait(barrier, len(places))


def start_copy(source, target, sems, index, place):
    copy = pltpu.make_async_remote_copy(
        src_ref=source,
        dst_ref=target,
        send_sem=sems[0].at[index],
        recv_sem=sems[1].at[index],
        device_id=place,
        device_id_type=MESH,
    )
    copy.start()
    return copy


class Counter:
    def __init__(self):
        self.value = 0

    def next(self):
        self.value += 1
        return self.value - 1


def gather_flows(flows, me, sems, count, hooks=()):
    sends = []
    for _ in gather_steps(flows, me, sems, count, sends, hooks):
        pass
    return sends


def gather_steps(flows, me, sems, count, sends, hooks=()):
    plans = []
    for order, source, target, local in flows:
        index = {}
        for level, bit in enumerate(order):
            for bits in subsets(order[:level]):
                if not (bit[0] == "r" and local(bits) and local(bits + (bit,))):
                    index[(level, bits)] = count.next()
        plans.append(index)
    deepest = max(len(order) for order, _, _, _ in flows)

    def push(flow, number, level, bits, ready):
        order, source, target, local = flow
        if (level, bits) not in plans[number]:
            return
        place = moved(me, bits)
        origin = source(place) if ready else target(place, bits)
        goal = target(place, bits + (order[level],))
        slot = plans[number][(level, bits)]
        sends.append(start_copy(origin, goal, sems, slot, moved(me, (order[level],))))

    for level in range(deepest):
        for number, flow in enumerate(flows):
            order, source, target, local = flow
            if level < len(order):
                for bits in subsets(order[:level]):
                    if local(bits):
                        push(flow, number, level, bits, True)
    yield
    hooks = dict(hooks)
    if -1 in hooks:
        hooks[-1]()
    for level in range(deepest):
        for turn in range(2**level):
            for number, flow in enumerate(flows):
                order, source, target, local = flow
                if level >= len(order):
                    continue
                bits = subsets(order[:level])[turn]
                key = (level, bits)
                if key not in plans[number]:
                    continue
                full = bits + (order[level],)
                place = moved(me, full)
                slot = plans[number][key]
                pltpu.make_async_remote_copy(
                    src_ref=target(place, full),
                    dst_ref=target(place, full),
                    send_sem=sems[0].at[slot],
                    recv_sem=sems[1].at[slot],
                    device_id=moved(me, (order[level],)),
                    device_id_type=MESH,
                ).wait_recv()
                for later in range(level + 1, len(order)):
                    push(flow, number, later, full, False)
                yield
        if level in hooks:
            hooks[level]()


def gather_slots(orders):
    return sum(2 ** len(order) - 1 for order in orders)


def add_into(target, first, second, block):
    rows = first.shape[0]

    def body(index, carry):
        window = pl.ds(pl.multiple_of(index * block, block), block)
        target[window] = first[window] + second[window]
        return carry

    if rows == block:
        target[...] = first[...] + second[...]
    else:
        lax.fori_loop(0, rows // block, body, 0)


def halving_slots(length):
    return 2 ** (length - 1) + 2**length - 1


def sum_flows(flows, me, sems, local_sems, count, local_count):
    sends = []
    for _ in sum_steps(flows, me, sems, local_sems, count, local_count, sends):
        pass
    return sends


def sum_steps(flows, me, sems, local_sems, count, local_count, sends):
    loads = []
    plans = []
    for order, source, buffer, block in flows:
        size = len(order)
        held = subsets(order[1:][::-1])
        place_of = {frozenset(bits): i for i, bits in enumerate(held)}
        index, slots, base = {}, {}, len(held)
        for level in range(size):
            for bits in subsets(order[level + 1 :][::-1]):
                index[(level, frozenset(bits))] = count.next()
                slots[(level, frozenset(bits))] = base
                base += 1
        plans.append((place_of, index, slots))
    deepest = max(len(order) for order, _, _, _ in flows)

    def turns(order, level):
        names = subsets(order[level + 1 :][::-1])
        return names[::-1]

    for turn in range(2 ** (deepest - 1)):
        for number, (order, source, buffer, block) in enumerate(flows):
            names = turns(order, 0)
            if turn >= len(names):
                continue
            bits = names[turn]
            key = frozenset(bits)
            place_of, index, slots = plans[number]
            sends.append(
                start_copy(
                    source(moved(me, bits + (order[0],))),
                    buffer.at[slots[(0, key)]],
                    sems,
                    index[(0, key)],
                    moved(me, (order[0],)),
                )
            )
            load = pltpu.make_async_copy(
                source(moved(me, bits)), buffer.at[place_of[key]], local_sems.at[local_count.next()]
            )
            load.start()
            loads.append(((number, key), load))
    waiting = dict(loads)
    yield
    for level in range(deepest):
        for turn in range(2 ** (deepest - 1 - level)):
            for number, (order, source, buffer, block) in enumerate(flows):
                if level >= len(order):
                    continue
                names = turns(order, level)
                if turn >= len(names):
                    continue
                bits = names[turn]
                key = frozenset(bits)
                place_of, index, slots = plans[number]
                slot = index[(level, key)]
                landed = buffer.at[slots[(level, key)]]
                pltpu.make_async_remote_copy(
                    src_ref=landed,
                    dst_ref=landed,
                    send_sem=sems[0].at[slot],
                    recv_sem=sems[1].at[slot],
                    device_id=moved(me, (order[level],)),
                    device_id_type=MESH,
                ).wait_recv()
                if level == 0:
                    waiting[(number, key)].wait()
                kept = buffer.at[place_of[key]]
                add_into(kept, kept, landed, block)
                if level + 1 < len(order) and order[level + 1] in key:
                    after = key - {order[level + 1]}
                    sends.append(
                        start_copy(
                            kept,
                            buffer.at[slots[(level + 1, after)]],
                            sems,
                            index[(level + 1, after)],
                            moved(me, (order[level + 1],)),
                        )
                    )
                yield


def rms_norm(value, gain):
    scale = lax.rsqrt(jnp.mean(value * value, axis=-1, keepdims=True) + norm_eps)
    return value * scale * gain


def norm_back(value, gain, grad):
    scale = lax.rsqrt(jnp.mean(value * value, axis=-1, keepdims=True) + norm_eps)
    normal = value * scale
    grad_gain = jnp.sum(grad * normal, axis=0)
    inner = grad * gain
    grad_value = scale * (inner - normal * jnp.mean(inner * normal, axis=-1, keepdims=True))
    return (grad_value, grad_gain)


def angle_tables(length, width):
    halfway = width // 2
    freqs = 10000.0 ** (-jnp.arange(halfway, dtype=jnp.float32) / halfway)
    angles = jnp.arange(length, dtype=jnp.float32)[:, None] * freqs[None, :]
    return (jnp.cos(angles)[:, None, :], jnp.sin(angles)[:, None, :], halfway)


def rotary(value):
    cosine, sine, halfway = angle_tables(value.shape[0], value.shape[-1])
    first = value[..., :halfway]
    second = value[..., halfway:]
    return jnp.concatenate(
        [first * cosine - second * sine, second * cosine + first * sine], axis=-1
    )


def rotary_back(grad):
    cosine, sine, halfway = angle_tables(grad.shape[0], grad.shape[-1])
    first = grad[..., :halfway]
    second = grad[..., halfway:]
    return jnp.concatenate(
        [first * cosine + second * sine, second * cosine - first * sine], axis=-1
    )


def block_scores(rows, keys, segs):
    places = jnp.arange(keys.shape[0], dtype=jnp.int32)
    scores = jnp.einsum(
        "sgrd,tgd->grst", rows, keys, preferred_element_type=jnp.float32
    ) * rows.shape[-1] ** (-0.5)
    allowed = (places[:, None] >= places[None, :]) & (segs[:, None] == segs[None, :])
    return jnp.where(allowed, scores, masked_score)


def attend_forward(query, keys, values, segs):
    length = query.shape[0]
    block = min(length, 512)

    def one_block(index):
        scores = block_scores(query, keys, segs)
        top = jnp.max(scores, axis=-1, keepdims=True)
        lse = top + jnp.log(jnp.sum(jnp.exp(scores - top), axis=-1, keepdims=True))
        probs = jnp.exp(scores - lse).astype(jnp.bfloat16)
        output = jnp.einsum("grst,tgd->sgrd", probs, values, preferred_element_type=jnp.float32)
        return (output.astype(jnp.bfloat16), lse)

    outputs, lses = lax.map(one_block, jnp.arange(length // block))
    return (outputs.reshape(query.shape), lses)


def attend_backward(query, keys, values, segs, lses, grad_out):
    length = query.shape[0]
    block = min(length, 512)
    scale = query.shape[-1] ** (-0.5)

    def step(carry, item):
        grad_key, grad_value = carry
        index, lse = item
        probs = jnp.exp(block_scores(query, keys, segs) - lse)
        grad_value = grad_value + jnp.einsum(
            "grst,sgrd->tgd",
            probs.astype(jnp.bfloat16),
            grad_out,
            preferred_element_type=jnp.float32,
        )
        grad_probs = jnp.einsum(
            "sgrd,tgd->grst", grad_out, values, preferred_element_type=jnp.float32
        )
        grad_scores = (
            probs * (grad_probs - jnp.sum(grad_probs * probs, axis=-1, keepdims=True))
        ).astype(jnp.bfloat16)
        grad_rows = (
            jnp.einsum("grst,tgd->sgrd", grad_scores, keys, preferred_element_type=jnp.float32)
            * scale
        )
        grad_key = (
            grad_key
            + jnp.einsum("grst,sgrd->tgd", grad_scores, query, preferred_element_type=jnp.float32)
            * scale
        )
        return ((grad_key, grad_value), grad_rows)

    zeros = jnp.zeros(keys.shape, jnp.float32)
    (grad_key, grad_value), grad_query = lax.scan(
        step, (zeros, zeros), (jnp.arange(length // block), lses)
    )
    return (grad_query.reshape(query.shape), grad_key, grad_value)


def adamw(weight, first, second, grad, rate, decay):
    first_new = beta_one * first + (1.0 - beta_one) * grad
    second_new = beta_two * second + (1.0 - beta_two) * grad * grad
    first_fix = 1.0 - beta_one**STEP
    second_fix = 1.0 - beta_two**STEP
    update = first_new / first_fix / (jnp.sqrt(second_new / second_fix) + adam_eps)
    return (first_new, second_new, weight - rate * (update + decay * weight))


X_BIT, C_BIT, Y_BIT, Z_BIT = ("r", 1), ("r", 0), ("s", 0), ("s", 1)
TURNED = (
    (X_BIT, Y_BIT, Z_BIT),
    (Y_BIT, Z_BIT, X_BIT),
    (Z_BIT, X_BIT, Y_BIT),
)
SUM_TURNED = (
    (Y_BIT, Z_BIT, X_BIT),
    (Z_BIT, Y_BIT, X_BIT),
    (Y_BIT, Z_BIT, X_BIT),
)
X_LAST = (
    (Z_BIT, Y_BIT, X_BIT),
    (Y_BIT, Z_BIT, X_BIT),
    (Z_BIT, Y_BIT, X_BIT),
)


POSITIONS = [
    frozenset(bits)
    for bits in (
        (X_BIT, Y_BIT, Z_BIT),
        (X_BIT, Y_BIT),
        (X_BIT, Z_BIT),
        (Y_BIT, Z_BIT),
        (X_BIT,),
        (Y_BIT,),
        (Z_BIT,),
        (),
    )
]


def position(bits):
    return POSITIONS.index(frozenset(bits))


def far_bits(shards):
    return tuple(("s", i) for i in range(2, shards.bit_length() - 1))


def only_self(bits):
    return not bits


def same_shard(bits):
    return all(axis == "r" for axis, _ in bits)


def token_flows(source, target, orders):
    width = source.shape[-1] // len(orders)
    flows = []
    for number, order in enumerate(orders):
        columns = pl.ds(number * width, width)
        flows.append(
            (
                order,
                lambda place, columns=columns: source.at[:, columns],
                lambda place, bits, columns=columns: target.at[position(bits), :, columns],
                only_self,
            )
        )
    return flows


def share_flows(source, target, orders, reps):
    height = source.shape[0] // len(orders)
    width = source.shape[1] // reps
    flows = []

    def columns_of(place):
        return pl.ds(pl.multiple_of(place[0] * width, 128), width)

    for number, order in enumerate(orders):
        rows = pl.ds(number * height, height)
        flows.append(
            (
                order,
                lambda place, rows=rows: source.at[rows, columns_of(place)],
                lambda place, bits, rows=rows: target.at[place[1], rows, columns_of(place)],
                same_shard,
            )
        )
    return flows


def neighbours(me, bits):
    return [moved(me, (bit,)) for bit in bits]


def open_kernel(shards, reps, *refs):
    qkv, out, small, w_in, w_out, cot = refs[:6]
    qkv_all, out_all, small_all, in_all, down_all, cot_all = refs[6:12]
    send, recv, local = refs[12:]
    me = here()
    sems = (send, recv)
    far = far_bits(shards)
    bits = (Y_BIT, Z_BIT) + far
    partners = [moved(me, item) for item in subsets(bits)[1:]][::-1]
    meet(neighbours(me, (X_BIT, C_BIT)) + partners)
    count = Counter()
    own = me[1]
    here_copies = [
        (qkv, qkv_all.at[own]),
        (out, out_all.at[own]),
        (small, small_all.at[own]),
        (w_in.at[own % GROUP], in_all.at[1, own]),
        (w_out.at[own % GROUP], down_all.at[1, own]),
        (cot, cot_all.at[position(())]),
    ]
    for number, (source, target) in enumerate(here_copies):
        pltpu.make_async_copy(source, target, local.at[number]).start()
    sends = []
    orders = [far + order + (C_BIT,) for order in X_LAST]
    flows = share_flows(qkv, qkv_all, orders, reps) + share_flows(out, out_all, orders, reps)
    flows.append(
        (far + (Y_BIT, Z_BIT), lambda place: small, lambda place, bits: small_all.at[place[1]], only_self)
    )
    flows += token_flows(cot, cot_all, X_LAST)
    direct = []

    def send_experts(chosen):
        for place in chosen:
            for source, target in ((w_in, in_all), (w_out, down_all)):
                slot = count.next()
                sends.append(
                    start_copy(source.at[place[1] % GROUP], target.at[1, own], sems, slot, place)
                )
                direct.append((target, place[1], slot, place))

    hooks = {HOOK: functools.partial(send_experts, partners)}
    sends += gather_flows(flows, me, sems, count, hooks)
    twin = moved(me, (C_BIT,))
    for source, target in ((w_in, in_all), (w_out, down_all)):
        sends.append(
            start_copy(source.at[own % GROUP], target.at[0, own], sems, count.next(), twin)
        )
    passed = [(target, own, count.value - 2 + i) for i, target in enumerate((in_all, down_all))]
    for target, index, slot, place in direct:
        landed = target.at[1, index]
        pltpu.make_async_remote_copy(
            src_ref=landed,
            dst_ref=landed,
            send_sem=send.at[slot],
            recv_sem=recv.at[slot],
            device_id=place,
            device_id_type=MESH,
        ).wait_recv()
        slot = count.next()
        sends.append(start_copy(landed, target.at[0, index], sems, slot, twin))
        passed.append((target, index, slot))
    for target, index, slot in passed:
        landed = target.at[0, index]
        pltpu.make_async_remote_copy(
            src_ref=landed,
            dst_ref=landed,
            send_sem=send.at[slot],
            recv_sem=recv.at[slot],
            device_id=twin,
            device_id_type=MESH,
        ).wait_recv()
    for copy in sends:
        copy.wait_send()
    for number, (source, target) in enumerate(here_copies):
        pltpu.make_async_copy(source, target, local.at[number]).wait()


def anywhere(count):
    return [pl.BlockSpec(memory_space=pl.ANY)] * count


def open_call(qkv, out, small, w_in, w_out, cot, shards, reps):
    def grown(array):
        return jax.ShapeDtypeStruct((shards,) + array.shape[-2:], array.dtype)

    shapes = [grown(array) for array in (qkv, out, small)]
    shapes += [
        jax.ShapeDtypeStruct((2, shards) + array.shape[1:], array.dtype) for array in (w_in, w_out)
    ]
    shapes.append(jax.ShapeDtypeStruct((len(POSITIONS),) + cot.shape, cot.dtype))
    slots = 6 * (shards * reps - 1) + shards + 4 * shards + 3 * 7
    return pl.pallas_call(
        functools.partial(open_kernel, shards, reps),
        out_shape=shapes,
        in_specs=anywhere(6),
        out_specs=anywhere(6),
        scratch_shapes=[
            pltpu.SemaphoreType.DMA((slots,)),
            pltpu.SemaphoreType.DMA((slots,)),
            pltpu.SemaphoreType.DMA((6,)),
        ],
        compiler_params=pltpu.CompilerParams(
            collective_id=0, has_side_effects=True, vmem_limit_bytes=VMEM_BYTES
        ),
        name="open_gather",
    )(qkv, out, small, w_in, w_out, cot)


def spread_kernel(*refs):
    rows, gate, rows_all, gate_all, send, recv, local = refs
    me = here()
    sems = (send, recv)
    meet(neighbours(me, (X_BIT, Y_BIT, Z_BIT)))
    count = Counter()
    copies = [
        (rows, rows_all.at[position(())]),
        (gate, gate_all.at[position(())]),
    ]
    for number, (source, target) in enumerate(copies):
        pltpu.make_async_copy(source, target, local.at[number]).start()
    flows = token_flows(rows, rows_all, TURNED)
    flows.append(
        (
            TURNED[0],
            lambda place: gate,
            lambda place, bits: gate_all.at[position(bits)],
            only_self,
        )
    )
    for copy in gather_flows(flows, me, sems, count):
        copy.wait_send()
    for number, (source, target) in enumerate(copies):
        pltpu.make_async_copy(source, target, local.at[number]).wait()


def spread_call(rows, gate):
    slots = 4 * 7
    return pl.pallas_call(
        spread_kernel,
        out_shape=[
            jax.ShapeDtypeStruct((len(POSITIONS),) + array.shape, array.dtype)
            for array in (rows, gate)
        ],
        in_specs=anywhere(2),
        out_specs=anywhere(2),
        scratch_shapes=[
            pltpu.SemaphoreType.DMA((slots,)),
            pltpu.SemaphoreType.DMA((slots,)),
            pltpu.SemaphoreType.DMA((2,)),
        ],
        compiler_params=pltpu.CompilerParams(
            collective_id=1, has_side_effects=True, vmem_limit_bytes=VMEM_BYTES
        ),
        name="spread_tokens",
    )(rows, gate)


def dot(a, b, dims=((1,), (0,))):
    return lax.dot_general(a, b, (dims, ((), ())), preferred_element_type=jnp.float32)


class PieceSum:
    def __init__(self, order, buffer, block, me, sems, count):
        self.order, self.buffer, self.block, self.me, self.sems = order, buffer, block, me, sems
        self.slots, self.index = {}, {}
        for level in range(len(order)):
            for bits in subsets(order[level + 1 :]):
                key = (level, frozenset(bits))
                self.slots[key] = len(POSITIONS) + len(self.slots)
                self.index[key] = count.next()

    def copy(self, level, bits):
        bit = self.order[level]
        key = (level, bits - {bit})
        return pltpu.make_async_remote_copy(
            src_ref=self.buffer.at[position(bits)],
            dst_ref=self.buffer.at[self.slots[key]],
            send_sem=self.sems[0].at[self.index[key]],
            recv_sem=self.sems[1].at[self.index[key]],
            device_id=moved(self.me, (bit,)),
            device_id_type=MESH,
        )

    def computed(self, bits):
        if self.order[0] in bits:
            self.copy(0, bits).start()

    def settle(self, level, bits):
        if any(bit in bits for bit in self.order[: level + 1]):
            return
        self.copy(level, bits | {self.order[level]}).wait_recv()
        kept = self.buffer.at[position(bits)]
        add_into(kept, kept, self.buffer.at[self.slots[(level, bits)]], self.block)
        if level + 1 < len(self.order) and self.order[level + 1] in bits:
            self.copy(level + 1, bits).start()

    def finish(self):
        for level, bits in self.index:
            self.copy(level, bits | {self.order[level]}).wait_send()


BLOCKS = 4


WAVES = subsets((Z_BIT, Y_BIT))
AHEAD = 1


def expert_kernel(shards, *refs):
    rows_ref, back_ref, gate_ref, in_ref, out_ref = refs[:5]
    moe_sum, grad_sum, mark_sum, half_in, half_out, grad_in, grad_out, far_in, far_out = refs[5:14]
    grad_buffers, moe_buffers, mark_buffer = refs[14:17], refs[17:20], refs[20]
    in_total, out_total, stage_in, stage_out, scaled, send, recv, local = refs[21:]
    away = [
        near + item for near in WAVES[:AHEAD] for item in subsets(far_bits(shards))[1:]
    ]
    low = jnp.bfloat16
    step = pl.program_id(0)
    block = step % BLOCKS
    me = here()
    twin = moved(me, (C_BIT,))
    sems = (send, recv)
    count = Counter()
    length = rows_ref.shape[0] // 2
    sums = [
        PieceSum(order, buffer, 128, me, sems, count)
        for turned, buffers in ((TURNED, grad_buffers), (TURNED, moe_buffers))
        for order, buffer in zip(turned, buffers)
    ]
    sums.append(PieceSum(TURNED[0], mark_buffer, length, me, sems, count))
    exchanged = [(stage_in, half_in, count.next()), (stage_out, half_out, count.next())]

    def halves():
        return [
            pltpu.make_async_remote_copy(
                src_ref=stage,
                dst_ref=half,
                send_sem=send.at[slot],
                recv_sem=recv.at[slot],
                device_id=twin,
                device_id_type=MESH,
            )
            for stage, half, slot in exchanged
        ]

    @pl.when(step == 0)
    def _():
        meet(neighbours(me, (X_BIT, C_BIT, Y_BIT, Z_BIT)) + [moved(me, bits) for bits in away])
        in_total[...] = jnp.zeros_like(in_total)
        out_total[...] = jnp.zeros_like(out_total)
        for buffer in grad_buffers + moe_buffers + (mark_buffer,):
            kept = buffer.at[pl.ds(0, len(POSITIONS))]
            kept[...] = jnp.zeros_like(kept)

    rows = rows_ref[...]
    gate = gate_ref[0]
    hidden_in = dot(rows, in_ref[0])
    gate_part = hidden_in[:, :H]
    up_part = hidden_in[:, H:]
    sigma = jax.nn.sigmoid(gate_part)
    active = gate_part * sigma
    hidden = (active * up_part).astype(low)
    width = rows.shape[1] // 3
    pair = pl.ds(2 * block, 2)

    def add_pieces(buffer, value):
        value = value.reshape((2, length) + value.shape[1:])
        buffer[pair] = (buffer[pair].astype(jnp.float32) + value).astype(low)

    mark = jnp.zeros((2 * length, 1), jnp.float32)
    for third in range(3):
        columns = slice(third * width, (third + 1) * width)
        result = dot(hidden, out_ref[0, :, columns])
        back = back_ref[:, columns].astype(jnp.float32)
        mark += jnp.sum(back * result, axis=1, keepdims=True)
        add_pieces(moe_buffers[third], gate * result)
        scaled[:, columns] = (gate * back).astype(low)
    expert = jnp.where(step < BLOCKS, twin[0], me[0]) * GROUP + me[1] % GROUP
    mark_low = mark.astype(low).astype(jnp.float32)
    lane = lax.broadcasted_iota(jnp.int32, (2 * length, 128), 1)
    add_pieces(
        mark_buffer,
        jnp.where(lane == expert, mark_low, jnp.where(lane == expert + E, mark - mark_low, 0.0)),
    )
    grad_result = scaled[...]
    grad_hidden = dot(grad_result, out_ref[0], ((1,), (1,)))
    out_total[...] += dot(hidden, grad_result, ((0,), (0,)))
    grad_gate_part = grad_hidden * up_part * sigma * (1.0 + gate_part * (1.0 - sigma))
    grad_up_part = grad_hidden * active
    grad_rows = jnp.concatenate([grad_gate_part, grad_up_part], axis=1).astype(low)
    for third in range(3):
        columns = slice(third * width, (third + 1) * width)
        add_pieces(grad_buffers[third], dot(grad_rows, in_ref[0, columns], ((1,), (1,))))
    in_total[...] += dot(rows, grad_rows, ((0,), (0,)))

    @pl.when(step == BLOCKS - 1)
    def _():
        stage_in[...] = in_total[...].astype(low)
        stage_out[...] = out_total[...].astype(low)
        for copy in halves():
            copy.start()
        in_total[...] = jnp.zeros_like(in_total)
        out_total[...] = jnp.zeros_like(out_total)

    def settle(level, number):
        for bits in POSITIONS[2 * number : 2 * number + 2]:
            for item in sums:
                item.settle(level, bits)

    for number in range(BLOCKS):

        @pl.when(step == BLOCKS + number)
        def _():
            for bits in POSITIONS[2 * number : 2 * number + 2]:
                for item in sums:
                    item.computed(bits)
            if number >= 1:
                settle(0, number - 1)
            if number >= 2:
                settle(1, number - 2)

    @pl.when(step == 2 * BLOCKS - 1)
    def _():
        loads = []
        for number, (copy, (stage, half, _)) in enumerate(zip(halves(), exchanged)):
            copy.wait()
            load = pltpu.make_async_copy(half, stage, local.at[number])
            load.start()
            loads.append(load)
        stores = []
        far_copies = []
        for number, (total, stage, goal, landed) in enumerate(
            ((in_total, stage_in, grad_in, far_in), (out_total, stage_out, grad_out, far_out))
        ):
            loads[number].wait()
            stage[...] = (total[...] + stage[...].astype(jnp.float32)).astype(low)
            store = pltpu.make_async_copy(stage, goal, local.at[2 + number])
            store.start()
            stores.append(store)
            rows_each = stage.shape[0] // shards
            for index, bits in enumerate(away):
                place = moved(me, bits)
                window = pl.ds(pl.multiple_of(place[1] * rows_each, 16), rows_each)
                far_copies.append(
                    start_copy(stage.at[window], landed.at[index], sems, count.next(), place)
                )
        settle(0, BLOCKS - 1)
        for number in (BLOCKS - 2, BLOCKS - 1):
            settle(1, number)
        for number in range(BLOCKS):
            settle(2, number)
        own = position(())
        for item, goal in zip(
            sums,
            [grad_sum.at[:, pl.ds(i * width, width)] for i in range(3)]
            + [moe_sum.at[:, pl.ds(i * width, width)] for i in range(3)]
            + [mark_sum],
        ):
            store = pltpu.make_async_copy(item.buffer.at[own], goal, local.at[len(stores) + 2])
            store.start()
            stores.append(store)
        for item in sums:
            item.finish()
        for copy in far_copies:
            copy.wait()
        for store in stores:
            store.wait()


def expert_call(rows, back, gate, full_in, full_out, shards):
    _, length, width = rows.shape
    count = len(POSITIONS) * length
    low = jnp.bfloat16
    block = 2 * length
    rows, back = rows.reshape(count, width), back.reshape(count, width)

    def weights(array):
        return pl.BlockSpec(
            (1,) + array.shape[1:], lambda i: (i // BLOCKS, 0, 0), pipeline_mode=pl.Buffered(1)
        )

    def like(array):
        return jax.ShapeDtypeStruct(array.shape[1:], low)

    sequence = jax.ShapeDtypeStruct((length, width), low)
    pieces = 2 * len(POSITIONS) - 1
    ahead = AHEAD * (shards // GROUP - 1)
    slots = 7 * 7 + 2 + 2 * ahead

    def landing(array):
        return jax.ShapeDtypeStruct((ahead, array.shape[1] // shards, array.shape[2]), low)

    return pl.pallas_call(
        functools.partial(expert_kernel, shards),
        grid=(2 * BLOCKS,),
        out_shape=[
            sequence,
            sequence,
            jax.ShapeDtypeStruct((length, 128), low),
            like(full_in),
            like(full_out),
            like(full_in),
            like(full_out),
            landing(full_in),
            landing(full_out),
        ],
        in_specs=[
            pl.BlockSpec((block, width), lambda i: (i % BLOCKS, 0)),
            pl.BlockSpec((block, width), lambda i: (i % BLOCKS, 0)),
            pl.BlockSpec((1, block, 1), lambda i: (i // BLOCKS, i % BLOCKS, 0)),
            weights(full_in),
            weights(full_out),
        ],
        out_specs=anywhere(9),
        scratch_shapes=[pltpu.VMEM((pieces, length, width // 3), low)] * 6
        + [
            pltpu.VMEM((pieces, length, 128), low),
            pltpu.VMEM(full_in.shape[1:], jnp.float32),
            pltpu.VMEM(full_out.shape[1:], jnp.float32),
            pltpu.VMEM(full_in.shape[1:], low),
            pltpu.VMEM(full_out.shape[1:], low),
            pltpu.VMEM((block, width), low),
            pltpu.SemaphoreType.DMA((slots,)),
            pltpu.SemaphoreType.DMA((slots,)),
            pltpu.SemaphoreType.DMA((12,)),
        ],
        compiler_params=pltpu.CompilerParams(
            collective_id=2,
            has_side_effects=True,
            vmem_limit_bytes=EXPERT_VMEM_BYTES,
            dimension_semantics=("arbitrary",),
        ),
        name="experts",
    )(rows, back, gate, full_in, full_out)


def turned_back(tile, tables):
    cosine, sine_up, sine_down = tables
    return (
        tile * cosine - pltpu.roll(tile, 96, 1) * sine_up - pltpu.roll(tile, 32, 1) * sine_down
    )


def close_kernel(shards, reps, *refs):
    (branch, attention, acts, lse, allowed, normed, x, grad_mid, gain, small) = refs[:10]
    tables = [ref[...] for ref in refs[10:13]]
    qkv_w, out_w, g_in, g_down, far_in, far_down = refs[13:19]
    qkv_sum, out_sum, small_sum, in_sum, down_sum, tokens_grad, qkv_part, out_part = refs[19:27]
    dense = refs[27:33]
    tiny, in_land, down_land, in_own, down_own = refs[33:38]
    qkv_held, out_held, stage, acts_grad, heads_grad, small_held = refs[38:44]
    send, recv, local = refs[44:]
    low = jnp.bfloat16
    me = here()
    sems = (send, recv)
    far = far_bits(shards)
    partners = [moved(me, item) for item in subsets((Y_BIT, Z_BIT) + far)[1:]]
    meet(neighbours(me, (X_BIT, C_BIT)) + partners)
    count, local_count = Counter(), Counter()
    sends = []
    tail = []
    loads = []
    for source, held in ((out_w, out_held), (qkv_w, qkv_held)):
        load = pltpu.make_async_copy(source, held, local.at[local_count.next()])
        load.start()
        loads.append(load)
    columns_of = []
    groups = []
    for which, (source, target) in enumerate(((qkv_part, qkv_sum), (out_part, out_sum))):
        flows = []
        rows_each = source.shape[0] // shards
        height = rows_each // len(SUM_TURNED)
        width = source.shape[1] // reps
        for number, order in enumerate(SUM_TURNED):
            buffer = dense[which * 3 + number]

            def piece(place, source=source, number=number, height=height, width=width):
                start = place[1] * (height * len(SUM_TURNED)) + number * height
                return source.at[
                    pl.ds(pl.multiple_of(start, 16), height),
                    pl.ds(pl.multiple_of(place[0] * width, 128), width),
                ]

            def goal(place, bits=(), target=target, number=number, height=height, width=width):
                return target.at[
                    pl.ds(number * height, height),
                    pl.ds(pl.multiple_of(place[0] * width, 128), width),
                ]

            flows.append(((C_BIT,) + order + far, piece, buffer, height))
            columns_of.append((buffer, goal))
        groups.append(flows)
    tiny_order = (Y_BIT, Z_BIT) + far
    rows_each = small_held.shape[0] // shards

    def tiny_piece(place):
        return small_held.at[pl.ds(pl.multiple_of(place[1] * rows_each, 16), rows_each)]

    tiny_flow = (tiny_order, tiny_piece, tiny, 16)

    def sum_run(flows):
        return sum_steps(flows, me, sems, local, count, local_count, sends)

    def last_steps():
        for buffer, goal in columns_of:
            store = pltpu.make_async_copy(buffer.at[0], goal(me), local.at[local_count.next()])
            store.start()
            tail.append(store)
        columns = [
            ((X_BIT, C_BIT), lambda place, buffer=buffer: buffer.at[0], goal, only_self)
            for buffer, goal in columns_of
        ]
        yield from gather_steps(columns, me, sems, count, sends)
        base = halving_slots(len(tiny_order))
        current = 0
        for bit in (X_BIT, C_BIT):
            slot = count.next()
            landed = tiny.at[base]
            copy = start_copy(tiny.at[current], landed, sems, slot, moved(me, (bit,)))
            copy.wait()
            add_into(tiny.at[base + 1], tiny.at[current], landed, 16)
            current = base + 1
            base += 2
            yield
        store = pltpu.make_async_copy(tiny.at[current], small_sum, local.at[local_count.next()])
        store.start()
        tail.append(store)

    arrays = (
        (g_in, far_in, in_land, in_own, in_sum),
        (g_down, far_down, down_land, down_own, down_sum),
    )
    waves = WAVES
    ahead = [near + item for near in WAVES[:AHEAD] for item in subsets(far)[1:]]

    def expert_steps():
        waiting = [[] for _ in waves]

        def send_wave(number, items):
            for item in items:
                place = moved(me, waves[number] + item)
                for source, arrived, landed, _, _ in arrays:
                    bits = waves[number] + item
                    if bits and bits not in ahead:
                        slot = count.next()
                        sends.append(
                            start_copy(source.at[place[1]], landed.at[me[1]], sems, slot, place)
                        )
                        wait = pltpu.make_async_remote_copy(
                            src_ref=landed.at[place[1]],
                            dst_ref=landed.at[place[1]],
                            send_sem=send.at[slot],
                            recv_sem=recv.at[slot],
                            device_id=place,
                            device_id_type=MESH,
                        ).wait_recv
                    else:
                        origin = arrived.at[ahead.index(bits)] if bits else source.at[me[1]]
                        load = pltpu.make_async_copy(
                            origin, landed.at[place[1]], local.at[local_count.next()]
                        )
                        load.start()
                        wait = load.wait
                    waiting[number].append(wait)

        away = subsets(far)[1:]
        for number in range(len(waves)):
            send_wave(number, ((),))
        for number in range(len(waves)):
            send_wave(number, away)
        yield
        relays = []
        for number, near in enumerate(waves):
            for wait in waiting[number]:
                wait()
            place = moved(me, near)
            expert = place[1] % GROUP
            for _, _, landed, held, target in arrays:
                total = landed.at[place[1]]
                for item in subsets(far)[1:]:
                    part = landed.at[moved(place, item)[1]]
                    add_into(held.at[number], total, part, part.shape[0])
                    total = held.at[number]

                def goal(where, bits=(), target=target, expert=expert):
                    return target.at[where[0] * GROUP + expert]

                store = pltpu.make_async_copy(total, goal(me), local.at[local_count.next()])
                store.start()
                tail.append(store)
                flow = ((X_BIT, C_BIT), lambda where, total=total: total, goal, only_self)
                relay = gather_steps([flow], me, sems, count, sends)
                relays.append(relay)
                next(relay)
            yield
        for relay in relays:
            for _ in relay:
                yield

    def weight_grad(rows, grads, part):
        width = grads.shape[1]
        stores = []
        for number in range(rows.shape[1] // 256):
            if number >= 2:
                stores[number - 2].wait()
            held = stage.at[number % 2, :, pl.ds(0, width)]
            piece = rows[:, number * 256 : (number + 1) * 256]
            held[...] = dot(piece, grads[...], ((0,), (0,))).astype(low)
            store = pltpu.make_async_copy(
                held, part.at[pl.ds(number * 256, 256)], local.at[local_count.next()]
            )
            store.start()
            stores.append(store)
        for store in stores[-2:]:
            store.wait()

    def advance(run, steps):
        for _ in range(steps):
            if next(run, "end") == "end":
                return

    experts = expert_steps()
    next(experts)
    weight_grad(attention, branch, out_part)
    out_run = sum_run(groups[1])
    next(out_run)
    loads[0].wait()
    heads_grad[...] = dot(branch[...], out_held[...], ((1,), (1,))).astype(low)

    lane = lax.broadcasted_iota(jnp.int32, (1, 128), 1)
    sides = [(lane < HD).astype(jnp.float32), (lane >= HD).astype(jnp.float32)]
    sides_low = [side.astype(low) for side in sides]
    scale = HD ** (-0.5)
    group = HEADS // KV_HEADS

    def doubled(tile):
        tile = tile.astype(jnp.float32)
        other = pltpu.roll(tile, HD, 1)
        return [
            (tile * sides[0] + other * sides[1]).astype(low),
            (other * sides[0] + tile * sides[1]).astype(low),
        ]

    for pair in range(KV_HEADS // 2):
        keys = doubled(acts[:, QD + 128 * pair : QD + 128 * (pair + 1)])
        values = doubled(acts[:, QD + KVD + 128 * pair : QD + KVD + 128 * (pair + 1)])
        query_grads = [None] * group
        key_tile = value_tile = None
        for half in range(2):
            key_total = value_total = None
            for number in range(group):
                head = (2 * pair + half) * group + number
                tile, side = head // 2, head % 2
                columns = slice(128 * tile, 128 * (tile + 1))
                query = acts[:, columns] * sides_low[side]
                grad_out = heads_grad[:, columns] * sides_low[side]
                scores = dot(query, keys[half], ((1,), (1,))) * scale
                scores = jnp.where(allowed[...] > 0.5, scores, masked_score)
                probs = jnp.exp(scores - lse[:, head : head + 1])
                grad_probs = dot(grad_out, values[half], ((1,), (1,)))
                inner = jnp.sum(grad_probs * probs, axis=1, keepdims=True)
                grad_scores = (probs * (grad_probs - inner)).astype(low)
                value_part = dot(probs.astype(low), grad_out, ((0,), (0,)))
                key_part = dot(grad_scores, query, ((0,), (0,)))
                query_part = dot(grad_scores, keys[half]) * sides[side]
                local_tile = tile - group * pair
                if query_grads[local_tile] is None:
                    query_grads[local_tile] = query_part
                else:
                    query_grads[local_tile] += query_part
                key_total = key_part if key_total is None else key_total + key_part
                value_total = value_part if value_total is None else value_total + value_part
            key_total = (key_total + pltpu.roll(key_total, HD, 1)) * sides[half]
            value_total = (value_total + pltpu.roll(value_total, HD, 1)) * sides[half]
            key_tile = key_total if key_tile is None else key_tile + key_total
            value_tile = value_total if value_tile is None else value_tile + value_total
        for number in range(group):
            tile = group * pair + number
            acts_grad[:, 128 * tile : 128 * (tile + 1)] = turned_back(
                query_grads[number] * scale, tables
            ).astype(low)
        acts_grad[:, QD + 128 * pair : QD + 128 * (pair + 1)] = turned_back(
            key_tile * scale, tables
        ).astype(low)
        acts_grad[:, QD + KVD + 128 * pair : QD + KVD + 128 * (pair + 1)] = value_tile.astype(low)
        advance(out_run, OUT_STEPS[pair])
        advance(experts, EARLY[pair])

    weight_grad(normed, acts_grad, qkv_part)
    qkv_run = sum_run(groups[0])
    next(qkv_run)
    loads[1].wait()
    grad_normed = dot(acts_grad[...], qkv_held[...], ((1,), (1,)))
    value = x[...].astype(jnp.float32)
    spread = lax.rsqrt(jnp.mean(value * value, axis=-1, keepdims=True) + norm_eps)
    normal = value * spread
    inner = grad_normed * gain[...]
    tokens_grad[...] = grad_mid[...] + spread * (
        inner - normal * jnp.mean(inner * normal, axis=-1, keepdims=True)
    )
    gain_grad = lax.dot_general(
        grad_normed * normal,
        jnp.ones((value.shape[0], 128), jnp.float32),
        (((0,), (0,)), ((), ())),
        precision=HIGH,
        preferred_element_type=jnp.float32,
    )
    column = lax.broadcasted_iota(jnp.int32, gain_grad.shape, 1)
    small_held[...] = jnp.where(
        column == E, gain_grad, small[...].astype(jnp.float32)
    ).astype(low)
    third = sum_run([tiny_flow])
    next(third)

    mixed = [(qkv_run, 6), (out_run, 6), (experts, 1), (third, 1)]
    alive = [run for run, _ in mixed]
    while alive:
        for run, turns in mixed:
            for _ in range(turns):
                if run in alive and next(run, "end") == "end":
                    alive.remove(run)
    for _ in last_steps():
        pass
    for copy in sends:
        copy.wait_send()
    for copy in tail:
        copy.wait()


def close_call(near, weights, experts, shards, reps):
    branch, acts, small = near[0], near[2], near[9]
    qkv_w, out_w = weights
    g_in, g_down = experts[:2]
    far = far_bits(shards)
    size = 4 + len(far)
    pieces = halving_slots(size)
    low = jnp.bfloat16
    length = branch.shape[0]

    def part(array):
        return array.shape[0] // shards, array.shape[1]

    def dense_buffer(array):
        rows, columns = part(array)
        return [pltpu.VMEM((pieces, rows // 3, columns // reps), low)] * 3

    small_rows = small.shape[0] // shards
    tiny_pieces = halving_slots(2 + len(far)) + 4
    slots = 7 * (2**size - 1) + 2 * shards + 14 * 3 + 4
    vmem = pl.BlockSpec(memory_space=pltpu.VMEM)
    return pl.pallas_call(
        functools.partial(close_kernel, shards, reps),
        out_shape=[
            jax.ShapeDtypeStruct(part(qkv_w), low),
            jax.ShapeDtypeStruct(part(out_w), low),
            jax.ShapeDtypeStruct((small_rows, 128), low),
        ]
        + [
            jax.ShapeDtypeStruct((reps * GROUP,) + array.shape[1:], low) for array in (g_in, g_down)
        ]
        + [
            jax.ShapeDtypeStruct((length, D), jnp.float32),
            jax.ShapeDtypeStruct(qkv_w.shape, low),
            jax.ShapeDtypeStruct(out_w.shape, low),
        ],
        in_specs=[vmem] * len(near) + anywhere(6),
        out_specs=anywhere(5) + [vmem] + anywhere(2),
        scratch_shapes=dense_buffer(qkv_w)
        + dense_buffer(out_w)
        + [
            pltpu.VMEM((tiny_pieces, small_rows, 128), low),
            pltpu.VMEM(g_in.shape, low),
            pltpu.VMEM(g_down.shape, low),
            pltpu.VMEM((GROUP,) + g_in.shape[1:], low),
            pltpu.VMEM((GROUP,) + g_down.shape[1:], low),
            pltpu.VMEM(qkv_w.shape, low),
            pltpu.VMEM(out_w.shape, low),
            pltpu.VMEM((2, 256, qkv_w.shape[1]), low),
            pltpu.VMEM(acts.shape, low),
            pltpu.VMEM(branch.shape, low),
            pltpu.VMEM(small.shape, low),
            pltpu.SemaphoreType.DMA((slots,)),
            pltpu.SemaphoreType.DMA((slots,)),
            pltpu.SemaphoreType.DMA((7 * 2 ** (size - 1) + 64,)),
        ],
        compiler_params=pltpu.CompilerParams(
            collective_id=3, has_side_effects=True, vmem_limit_bytes=EXPERT_VMEM_BYTES
        ),
        name="close_sums",
    )(*near, *weights, *experts)


def on_device(
    shards,
    reps,
    tokens,
    segments,
    routes,
    cotangent,
    wqkv,
    wqkv_first,
    wqkv_second,
    wo,
    wo_first,
    wo_second,
    router,
    router_first,
    router_second,
    w_in,
    w_in_first,
    w_in_second,
    w_out,
    w_out_first,
    w_out_second,
    gains,
    gains_first,
    gains_second,
):
    length, width = tokens.shape
    group = HEADS // KV_HEADS
    segs = segments[0]
    rep, shard = here()
    low = jnp.bfloat16

    def cut(array):
        return array.astype(low).reshape((shards, array.shape[0] // shards) + array.shape[1:])

    small = jnp.concatenate(
        [router, gains.T, jnp.zeros((router.shape[0], 128 - E - 2), jnp.float32)], axis=1
    ).astype(low)
    mine_in = lax.dynamic_slice_in_dim(w_in, rep * GROUP, GROUP, 0).astype(low)
    mine_out = lax.dynamic_slice_in_dim(w_out, rep * GROUP, GROUP, 0).astype(low)
    qkv_w, out_w, small_w, full_in, full_out, cot_all = open_call(
        wqkv.astype(low), wo.astype(low), small, mine_in, mine_out, cotangent, shards, reps
    )
    qkv_w = qkv_w.reshape(D, -1)
    out_w = out_w.reshape(QD, D)
    small_w = small_w.reshape(D, 128)
    router_w = small_w[:, :E]
    gain_f = small_w[:, E : E + 2].astype(jnp.float32).T

    x = tokens.astype(jnp.float32)
    normed = rms_norm(x, gain_f[0]).astype(low)
    qkv = jnp.dot(normed, qkv_w, preferred_element_type=jnp.float32)
    query = (
        rotary(qkv[:, :QD].reshape(length, HEADS, HD))
        .astype(low)
        .reshape(length, KV_HEADS, group, HD)
    )
    keys = rotary(qkv[:, QD : QD + KVD].reshape(length, KV_HEADS, HD)).astype(low)
    values = qkv[:, QD + KVD :].reshape(length, KV_HEADS, HD).astype(low)
    attended, lses = attend_forward(query, keys, values, segs)
    attention = attended.reshape(length, QD)
    branch = jnp.dot(attention, out_w, preferred_element_type=jnp.float32)
    mid = x + branch
    normed2 = rms_norm(mid, gain_f[1]).astype(low)
    logits = jnp.dot(normed2, router_w, preferred_element_type=jnp.float32)
    picks = (routes[:, :, None] == jnp.arange(E, dtype=jnp.int32)[None, None, :]).any(axis=1)
    gates = jax.nn.softmax(jnp.where(picks, logits, -jnp.inf), axis=-1)

    rows, gates_all = spread_call(normed2, gates.T)
    gate = jnp.stack(
        [
            lax.dynamic_index_in_dim(gates_all, flip(rep, 0) * GROUP + shard % GROUP, 1, False),
            lax.dynamic_index_in_dim(gates_all, rep * GROUP + shard % GROUP, 1, False),
        ]
    ).reshape(2, -1, 1)
    moe, grad_normed2, marks, _, _, grad_in, grad_down, far_in, far_down = expert_call(
        rows, cot_all, gate, full_in.reshape(2, D, 2 * H), full_out.reshape(2, H, D), shards
    )
    marks = marks.astype(jnp.float32)
    grad_gates = marks[:, :E] + marks[:, E : 2 * E]
    mixed = (mid + moe.astype(jnp.float32)).astype(low)

    grad_logits = gates * (grad_gates - jnp.sum(grad_gates * gates, axis=-1, keepdims=True))
    grad_router = jnp.dot(normed2.astype(jnp.float32).T, grad_logits, precision=HIGH)
    grad_normed2 = grad_normed2.astype(jnp.float32) + jnp.dot(
        grad_logits, router_w.astype(jnp.float32).T, precision=HIGH
    )
    cot = cotangent.astype(jnp.float32)
    grad_mid_norm, grad_gain2 = norm_back(mid, gain_f[1], grad_normed2)
    grad_mid = cot + grad_mid_norm
    grad_branch = grad_mid.astype(low)
    grad_small = jnp.concatenate(
        [
            grad_router,
            jnp.zeros((D, 1), jnp.float32),
            grad_gain2[:, None],
            jnp.zeros((D, 128 - E - 2), jnp.float32),
        ],
        axis=1,
    ).astype(low)
    acts = jnp.concatenate(
        [query.reshape(length, QD), keys.reshape(length, KVD), values.reshape(length, KVD)], axis=1
    )
    lse_columns = jnp.pad(lses.reshape(HEADS, length).T, ((0, 0), (0, 128 - HEADS)))
    places = jnp.arange(length, dtype=jnp.int32)
    allowed = (places[:, None] >= places[None, :]) & (segs[:, None] == segs[None, :])
    cosine, sine, _ = angle_tables(length, HD)
    cosine, sine = cosine[:, 0], sine[:, 0]
    blank = jnp.zeros_like(sine)
    grad_qkv_w, grad_out_w, grad_small, grad_in_all, grad_down_all, tokens_grad, _, _ = close_call(
        (
            grad_branch,
            attention,
            acts,
            lse_columns,
            allowed.astype(jnp.float32),
            normed,
            tokens,
            grad_mid,
            gain_f[:1],
            grad_small,
            jnp.concatenate([cosine] * 4, axis=1),
            jnp.concatenate([-sine, blank] * 2, axis=1),
            jnp.concatenate([blank, sine] * 2, axis=1),
        ),
        (qkv_w, out_w),
        (cut(grad_in), cut(grad_down), far_in, far_down),
        shards,
        reps,
    )
    grad_small = grad_small.astype(jnp.float32)
    grad_router = grad_small[:, :E]
    grad_gains = grad_small[:, E : E + 2].T
    qkv_m, qkv_v, qkv_new = adamw(
        wqkv, wqkv_first, wqkv_second, grad_qkv_w.astype(jnp.float32), 3.0 * D ** (-0.5), decay_rate
    )
    out_m, out_v, out_new = adamw(
        wo, wo_first, wo_second, grad_out_w.astype(jnp.float32), 3.0 * (QD // 64) ** (-0.5), decay_rate
    )
    rout_m, rout_v, rout_new = adamw(
        router, router_first, router_second, grad_router, 1.5 * D ** (-0.5), decay_rate
    )
    in_m, in_v, in_new = adamw(
        w_in, w_in_first, w_in_second, grad_in_all.astype(jnp.float32), 3.0 * D ** (-0.5), decay_rate
    )
    down_m, down_v, down_new = adamw(
        w_out,
        w_out_first,
        w_out_second,
        grad_down_all.astype(jnp.float32),
        3.0 * (H // 16) ** (-0.5),
        decay_rate,
    )
    gain_m, gain_v, gain_new = adamw(gains, gains_first, gains_second, grad_gains, 0.6, 0.0)
    return (
        mixed,
        tokens_grad,
        qkv_m,
        qkv_v,
        qkv_new,
        out_m,
        out_v,
        out_new,
        rout_m,
        rout_v,
        rout_new,
        in_m,
        in_v,
        in_new,
        down_m,
        down_v,
        down_new,
        gain_m,
        gain_v,
        gain_new,
    )


def solution(mesh):
    in_specs = (
        P(("rep", "shard"), None),
        P(("rep", "shard"), None),
        P(("rep", "shard"), None),
        P(("rep", "shard"), None),
        P("shard", None),
        P("shard", None),
        P("shard", None),
        P("shard", None),
        P("shard", None),
        P("shard", None),
        P("shard", None),
        P("shard", None),
        P("shard", None),
        P(None, "shard", None),
        P(None, "shard", None),
        P(None, "shard", None),
        P(None, "shard", None),
        P(None, "shard", None),
        P(None, "shard", None),
        P(None, "shard"),
        P(None, "shard"),
        P(None, "shard"),
    )
    out_specs = (
        P(("rep", "shard"), None),
        P(("rep", "shard"), None),
        P("shard", None),
        P("shard", None),
        P("shard", None),
        P("shard", None),
        P("shard", None),
        P("shard", None),
        P("shard", None),
        P("shard", None),
        P("shard", None),
        P(None, "shard", None),
        P(None, "shard", None),
        P(None, "shard", None),
        P(None, "shard", None),
        P(None, "shard", None),
        P(None, "shard", None),
        P(None, "shard"),
        P(None, "shard"),
        P(None, "shard"),
    )
    return jax.shard_map(
        functools.partial(on_device, mesh.shape["shard"], mesh.shape["rep"]), mesh=mesh, in_specs=in_specs, out_specs=out_specs, check_vma=False
    )
```

```python
import functools

import jax
import jax.numpy as jnp
from jax import lax
from jax.experimental import pallas as pl
from jax.experimental.pallas import tpu as pltpu
from jax.sharding import PartitionSpec as P

D = 1536
H = 512
HEADS = 24
KV_HEADS = 8
HD = 64
E = 16
TOP = 8
STEP = 10
QD = 1536
KVD = 512
GROUP = 4

HIGH = lax.Precision.HIGHEST
MESH = pl.DeviceIdType.MESH
norm_eps = 1e-06
beta_one = 0.9
beta_two = 0.95
adam_eps = 1e-08
decay_rate = 0.1
masked_score = -1e30
HOOK = 0
OUT_STEPS = (0, 24, 24, 24)
EARLY = (1, 1, 1, 1)
VMEM_BYTES = 56 * 2**20
EXPERT_VMEM_BYTES = 62 * 2**20


def flip(index, bit):
    step = 2**bit
    return index + (1 - 2 * ((index // step) % 2)) * step


def moved(place, bits):
    rep, shard = place
    for axis, bit in bits:
        if axis == "r":
            rep = flip(rep, bit)
        else:
            shard = flip(shard, bit)
    return (rep, shard)


def subsets(bits):
    result = [()]
    for bit in bits:
        result = result + [item + (bit,) for item in result]
    return result


def here():
    return (lax.axis_index("rep"), lax.axis_index("shard"))


def meet(places):
    barrier = pltpu.get_barrier_semaphore()
    for place in places:
        pl.semaphore_signal(barrier, inc=1, device_id=place, device_id_type=MESH)
    pl.semaphore_wait(barrier, len(places))


def start_copy(source, target, sems, index, place):
    copy = pltpu.make_async_remote_copy(
        src_ref=source,
        dst_ref=target,
        send_sem=sems[0].at[index],
        recv_sem=sems[1].at[index],
        device_id=place,
        device_id_type=MESH,
    )
    copy.start()
    return copy


class Counter:
    def __init__(self):
        self.value = 0

    def next(self):
        self.value += 1
        return self.value - 1


def gather_flows(flows, me, sems, count, hooks=()):
    sends = []
    for _ in gather_steps(flows, me, sems, count, sends, hooks):
        pass
    return sends


def gather_steps(flows, me, sems, count, sends, hooks=()):
    plans = []
    for order, source, target, local in flows:
        index = {}
        for level, bit in enumerate(order):
            for bits in subsets(order[:level]):
                if not (bit[0] == "r" and local(bits) and local(bits + (bit,))):
                    index[(level, bits)] = count.next()
        plans.append(index)
    deepest = max(len(order) for order, _, _, _ in flows)

    def push(flow, number, level, bits, ready):
        order, source, target, local = flow
        if (level, bits) not in plans[number]:
            return
        place = moved(me, bits)
        origin = source(place) if ready else target(place, bits)
        goal = target(place, bits + (order[level],))
        slot = plans[number][(level, bits)]
        sends.append(start_copy(origin, goal, sems, slot, moved(me, (order[level],))))

    for level in range(deepest):
        for number, flow in enumerate(flows):
            order, source, target, local = flow
            if level < len(order):
                for bits in subsets(order[:level]):
                    if local(bits):
                        push(flow, number, level, bits, True)
    yield
    hooks = dict(hooks)
    if -1 in hooks:
        hooks[-1]()
    for level in range(deepest):
        for turn in range(2**level):
            for number, flow in enumerate(flows):
                order, source, target, local = flow
                if level >= len(order):
                    continue
                bits = subsets(order[:level])[turn]
                key = (level, bits)
                if key not in plans[number]:
                    continue
                full = bits + (order[level],)
                place = moved(me, full)
                slot = plans[number][key]
                pltpu.make_async_remote_copy(
                    src_ref=target(place, full),
                    dst_ref=target(place, full),
                    send_sem=sems[0].at[slot],
                    recv_sem=sems[1].at[slot],
                    device_id=moved(me, (order[level],)),
                    device_id_type=MESH,
                ).wait_recv()
                for later in range(level + 1, len(order)):
                    push(flow, number, later, full, False)
                yield
        if level in hooks:
            hooks[level]()


def gather_slots(orders):
    return sum(2 ** len(order) - 1 for order in orders)


def add_into(target, first, second, block):
    rows = first.shape[0]

    def body(index, carry):
        window = pl.ds(pl.multiple_of(index * block, block), block)
        target[window] = first[window] + second[window]
        return carry

    if rows == block:
        target[...] = first[...] + second[...]
    else:
        lax.fori_loop(0, rows // block, body, 0)


def halving_slots(length):
    return 2 ** (length - 1) + 2**length - 1


def sum_flows(flows, me, sems, local_sems, count, local_count):
    sends = []
    for _ in sum_steps(flows, me, sems, local_sems, count, local_count, sends):
        pass
    return sends


def sum_steps(flows, me, sems, local_sems, count, local_count, sends):
    loads = []
    plans = []
    for order, source, buffer, block in flows:
        size = len(order)
        held = subsets(order[1:][::-1])
        place_of = {frozenset(bits): i for i, bits in enumerate(held)}
        index, slots, base = {}, {}, len(held)
        for level in range(size):
            for bits in subsets(order[level + 1 :][::-1]):
                index[(level, frozenset(bits))] = count.next()
                slots[(level, frozenset(bits))] = base
                base += 1
        plans.append((place_of, index, slots))
    deepest = max(len(order) for order, _, _, _ in flows)

    def turns(order, level):
        names = subsets(order[level + 1 :][::-1])
        return names[::-1]

    for turn in range(2 ** (deepest - 1)):
        for number, (order, source, buffer, block) in enumerate(flows):
            names = turns(order, 0)
            if turn >= len(names):
                continue
            bits = names[turn]
            key = frozenset(bits)
            place_of, index, slots = plans[number]
            sends.append(
                start_copy(
                    source(moved(me, bits + (order[0],))),
                    buffer.at[slots[(0, key)]],
                    sems,
                    index[(0, key)],
                    moved(me, (order[0],)),
                )
            )
            load = pltpu.make_async_copy(
                source(moved(me, bits)), buffer.at[place_of[key]], local_sems.at[local_count.next()]
            )
            load.start()
            loads.append(((number, key), load))
    waiting = dict(loads)
    yield
    for level in range(deepest):
        for turn in range(2 ** (deepest - 1 - level)):
            for number, (order, source, buffer, block) in enumerate(flows):
                if level >= len(order):
                    continue
                names = turns(order, level)
                if turn >= len(names):
                    continue
                bits = names[turn]
                key = frozenset(bits)
                place_of, index, slots = plans[number]
                slot = index[(level, key)]
                landed = buffer.at[slots[(level, key)]]
                pltpu.make_async_remote_copy(
                    src_ref=landed,
                    dst_ref=landed,
                    send_sem=sems[0].at[slot],
                    recv_sem=sems[1].at[slot],
                    device_id=moved(me, (order[level],)),
                    device_id_type=MESH,
                ).wait_recv()
                if level == 0:
                    waiting[(number, key)].wait()
                kept = buffer.at[place_of[key]]
                add_into(kept, kept, landed, block)
                if level + 1 < len(order) and order[level + 1] in key:
                    after = key - {order[level + 1]}
                    sends.append(
                        start_copy(
                            kept,
                            buffer.at[slots[(level + 1, after)]],
                            sems,
                            index[(level + 1, after)],
                            moved(me, (order[level + 1],)),
                        )
                    )
                yield


def rms_norm(value, gain):
    scale = lax.rsqrt(jnp.mean(value * value, axis=-1, keepdims=True) + norm_eps)
    return value * scale * gain


def norm_back(value, gain, grad):
    scale = lax.rsqrt(jnp.mean(value * value, axis=-1, keepdims=True) + norm_eps)
    normal = value * scale
    grad_gain = jnp.sum(grad * normal, axis=0)
    inner = grad * gain
    grad_value = scale * (inner - normal * jnp.mean(inner * normal, axis=-1, keepdims=True))
    return (grad_value, grad_gain)


def angle_tables(length, width):
    halfway = width // 2
    freqs = 10000.0 ** (-jnp.arange(halfway, dtype=jnp.float32) / halfway)
    angles = jnp.arange(length, dtype=jnp.float32)[:, None] * freqs[None, :]
    return (jnp.cos(angles)[:, None, :], jnp.sin(angles)[:, None, :], halfway)


def rotary(value):
    cosine, sine, halfway = angle_tables(value.shape[0], value.shape[-1])
    first = value[..., :halfway]
    second = value[..., halfway:]
    return jnp.concatenate(
        [first * cosine - second * sine, second * cosine + first * sine], axis=-1
    )


def rotary_back(grad):
    cosine, sine, halfway = angle_tables(grad.shape[0], grad.shape[-1])
    first = grad[..., :halfway]
    second = grad[..., halfway:]
    return jnp.concatenate(
        [first * cosine + second * sine, second * cosine - first * sine], axis=-1
    )


def block_scores(rows, keys, segs):
    places = jnp.arange(keys.shape[0], dtype=jnp.int32)
    scores = jnp.einsum(
        "sgrd,tgd->grst", rows, keys, preferred_element_type=jnp.float32
    ) * rows.shape[-1] ** (-0.5)
    allowed = (places[:, None] >= places[None, :]) & (segs[:, None] == segs[None, :])
    return jnp.where(allowed, scores, masked_score)


def attend_forward(query, keys, values, segs):
    length = query.shape[0]
    block = min(length, 512)

    def one_block(index):
        scores = block_scores(query, keys, segs)
        top = jnp.max(scores, axis=-1, keepdims=True)
        lse = top + jnp.log(jnp.sum(jnp.exp(scores - top), axis=-1, keepdims=True))
        probs = jnp.exp(scores - lse).astype(jnp.bfloat16)
        output = jnp.einsum("grst,tgd->sgrd", probs, values, preferred_element_type=jnp.float32)
        return (output.astype(jnp.bfloat16), lse)

    outputs, lses = lax.map(one_block, jnp.arange(length // block))
    return (outputs.reshape(query.shape), lses)


def attend_backward(query, keys, values, segs, lses, grad_out):
    length = query.shape[0]
    block = min(length, 512)
    scale = query.shape[-1] ** (-0.5)

    def step(carry, item):
        grad_key, grad_value = carry
        index, lse = item
        probs = jnp.exp(block_scores(query, keys, segs) - lse)
        grad_value = grad_value + jnp.einsum(
            "grst,sgrd->tgd",
            probs.astype(jnp.bfloat16),
            grad_out,
            preferred_element_type=jnp.float32,
        )
        grad_probs = jnp.einsum(
            "sgrd,tgd->grst", grad_out, values, preferred_element_type=jnp.float32
        )
        grad_scores = (
            probs * (grad_probs - jnp.sum(grad_probs * probs, axis=-1, keepdims=True))
        ).astype(jnp.bfloat16)
        grad_rows = (
            jnp.einsum("grst,tgd->sgrd", grad_scores, keys, preferred_element_type=jnp.float32)
            * scale
        )
        grad_key = (
            grad_key
            + jnp.einsum("grst,sgrd->tgd", grad_scores, query, preferred_element_type=jnp.float32)
            * scale
        )
        return ((grad_key, grad_value), grad_rows)

    zeros = jnp.zeros(keys.shape, jnp.float32)
    (grad_key, grad_value), grad_query = lax.scan(
        step, (zeros, zeros), (jnp.arange(length // block), lses)
    )
    return (grad_query.reshape(query.shape), grad_key, grad_value)


def adamw(weight, first, second, grad, rate, decay):
    first_new = beta_one * first + (1.0 - beta_one) * grad
    second_new = beta_two * second + (1.0 - beta_two) * grad * grad
    first_fix = 1.0 - beta_one**STEP
    second_fix = 1.0 - beta_two**STEP
    update = first_new / first_fix / (jnp.sqrt(second_new / second_fix) + adam_eps)
    return (first_new, second_new, weight - rate * (update + decay * weight))


X_BIT, C_BIT, Y_BIT, Z_BIT = ("r", 1), ("r", 0), ("s", 0), ("s", 1)
TURNED = (
    (X_BIT, Y_BIT, Z_BIT),
    (Y_BIT, Z_BIT, X_BIT),
    (Z_BIT, X_BIT, Y_BIT),
)
SUM_TURNED = (
    (Y_BIT, Z_BIT, X_BIT),
    (Z_BIT, Y_BIT, X_BIT),
    (Y_BIT, Z_BIT, X_BIT),
)
X_LAST = (
    (Z_BIT, Y_BIT, X_BIT),
    (Z_BIT, Y_BIT, X_BIT),
    (Z_BIT, Y_BIT, X_BIT),
)


POSITIONS = [
    frozenset(bits)
    for bits in (
        (X_BIT, Y_BIT, Z_BIT),
        (X_BIT, Y_BIT),
        (X_BIT, Z_BIT),
        (Y_BIT, Z_BIT),
        (X_BIT,),
        (Y_BIT,),
        (Z_BIT,),
        (),
    )
]


def position(bits):
    return POSITIONS.index(frozenset(bits))


def far_bits(shards):
    return tuple(("s", i) for i in range(2, shards.bit_length() - 1))


def only_self(bits):
    return not bits


def same_shard(bits):
    return all(axis == "r" for axis, _ in bits)


def token_flows(source, target, orders):
    width = source.shape[-1] // len(orders)
    flows = []
    for number, order in enumerate(orders):
        columns = pl.ds(number * width, width)
        flows.append(
            (
                order,
                lambda place, columns=columns: source.at[:, columns],
                lambda place, bits, columns=columns: target.at[position(bits), :, columns],
                only_self,
            )
        )
    return flows


def share_flows(source, target, orders, reps):
    height = source.shape[0] // len(orders)
    width = source.shape[1] // reps
    flows = []

    def columns_of(place):
        return pl.ds(pl.multiple_of(place[0] * width, 128), width)

    for number, order in enumerate(orders):
        rows = pl.ds(number * height, height)
        flows.append(
            (
                order,
                lambda place, rows=rows: source.at[rows, columns_of(place)],
                lambda place, bits, rows=rows: target.at[place[1], rows, columns_of(place)],
                same_shard,
            )
        )
    return flows


def neighbours(me, bits):
    return [moved(me, (bit,)) for bit in bits]


def open_kernel(shards, reps, *refs):
    qkv, out, small, w_in, w_out, cot = refs[:6]
    qkv_all, out_all, small_all, in_all, down_all, cot_all = refs[6:12]
    send, recv, local = refs[12:]
    me = here()
    sems = (send, recv)
    far = far_bits(shards)
    bits = (Y_BIT, Z_BIT) + far
    partners = [moved(me, item) for item in subsets(bits)[1:]][::-1]
    meet(neighbours(me, (X_BIT, C_BIT)) + partners)
    count = Counter()
    own = me[1]
    here_copies = [
        (qkv, qkv_all.at[own]),
        (out, out_all.at[own]),
        (small, small_all.at[own]),
        (w_in.at[own % GROUP], in_all.at[1, own]),
        (w_out.at[own % GROUP], down_all.at[1, own]),
        (cot, cot_all.at[position(())]),
    ]
    for number, (source, target) in enumerate(here_copies):
        pltpu.make_async_copy(source, target, local.at[number]).start()
    sends = []
    orders = [far + order + (C_BIT,) for order in X_LAST]
    flows = share_flows(qkv, qkv_all, orders, reps) + share_flows(out, out_all, orders, reps)
    flows.append(
        (far + (Y_BIT, Z_BIT), lambda place: small, lambda place, bits: small_all.at[place[1]], only_self)
    )
    flows += token_flows(cot, cot_all, X_LAST)
    direct = []

    def send_experts(chosen):
        for place in chosen:
            for source, target in ((w_in, in_all), (w_out, down_all)):
                slot = count.next()
                sends.append(
                    start_copy(source.at[place[1] % GROUP], target.at[1, own], sems, slot, place)
                )
                direct.append((target, place[1], slot, place))

    hooks = {HOOK: functools.partial(send_experts, partners)}
    sends += gather_flows(flows, me, sems, count, hooks)
    twin = moved(me, (C_BIT,))
    for source, target in ((w_in, in_all), (w_out, down_all)):
        sends.append(
            start_copy(source.at[own % GROUP], target.at[0, own], sems, count.next(), twin)
        )
    passed = [(target, own, count.value - 2 + i) for i, target in enumerate((in_all, down_all))]
    for target, index, slot, place in direct:
        landed = target.at[1, index]
        pltpu.make_async_remote_copy(
            src_ref=landed,
            dst_ref=landed,
            send_sem=send.at[slot],
            recv_sem=recv.at[slot],
            device_id=place,
            device_id_type=MESH,
        ).wait_recv()
        slot = count.next()
        sends.append(start_copy(landed, target.at[0, index], sems, slot, twin))
        passed.append((target, index, slot))
    for target, index, slot in passed:
        landed = target.at[0, index]
        pltpu.make_async_remote_copy(
            src_ref=landed,
            dst_ref=landed,
            send_sem=send.at[slot],
            recv_sem=recv.at[slot],
            device_id=twin,
            device_id_type=MESH,
        ).wait_recv()
    for copy in sends:
        copy.wait_send()
    for number, (source, target) in enumerate(here_copies):
        pltpu.make_async_copy(source, target, local.at[number]).wait()


def anywhere(count):
    return [pl.BlockSpec(memory_space=pl.ANY)] * count


def open_call(qkv, out, small, w_in, w_out, cot, shards, reps):
    def grown(array):
        return jax.ShapeDtypeStruct((shards,) + array.shape[-2:], array.dtype)

    shapes = [grown(array) for array in (qkv, out, small)]
    shapes += [
        jax.ShapeDtypeStruct((2, shards) + array.shape[1:], array.dtype) for array in (w_in, w_out)
    ]
    shapes.append(jax.ShapeDtypeStruct((len(POSITIONS),) + cot.shape, cot.dtype))
    slots = 6 * (shards * reps - 1) + shards + 4 * shards + 3 * 7
    return pl.pallas_call(
        functools.partial(open_kernel, shards, reps),
        out_shape=shapes,
        in_specs=anywhere(6),
        out_specs=anywhere(6),
        scratch_shapes=[
            pltpu.SemaphoreType.DMA((slots,)),
            pltpu.SemaphoreType.DMA((slots,)),
            pltpu.SemaphoreType.DMA((6,)),
        ],
        compiler_params=pltpu.CompilerParams(
            collective_id=0, has_side_effects=True, vmem_limit_bytes=VMEM_BYTES
        ),
        name="open_gather",
    )(qkv, out, small, w_in, w_out, cot)


def spread_kernel(*refs):
    rows, gate, rows_all, gate_all, send, recv, local = refs
    me = here()
    sems = (send, recv)
    meet(neighbours(me, (X_BIT, Y_BIT, Z_BIT)))
    count = Counter()
    copies = [
        (rows, rows_all.at[position(())]),
        (gate, gate_all.at[position(())]),
    ]
    for number, (source, target) in enumerate(copies):
        pltpu.make_async_copy(source, target, local.at[number]).start()
    flows = token_flows(rows, rows_all, TURNED)
    flows.append(
        (
            TURNED[0],
            lambda place: gate,
            lambda place, bits: gate_all.at[position(bits)],
            only_self,
        )
    )
    for copy in gather_flows(flows, me, sems, count):
        copy.wait_send()
    for number, (source, target) in enumerate(copies):
        pltpu.make_async_copy(source, target, local.at[number]).wait()


def spread_call(rows, gate):
    slots = 4 * 7
    return pl.pallas_call(
        spread_kernel,
        out_shape=[
            jax.ShapeDtypeStruct((len(POSITIONS),) + array.shape, array.dtype)
            for array in (rows, gate)
        ],
        in_specs=anywhere(2),
        out_specs=anywhere(2),
        scratch_shapes=[
            pltpu.SemaphoreType.DMA((slots,)),
            pltpu.SemaphoreType.DMA((slots,)),
            pltpu.SemaphoreType.DMA((2,)),
        ],
        compiler_params=pltpu.CompilerParams(
            collective_id=1, has_side_effects=True, vmem_limit_bytes=VMEM_BYTES
        ),
        name="spread_tokens",
    )(rows, gate)


def dot(a, b, dims=((1,), (0,))):
    return lax.dot_general(a, b, (dims, ((), ())), preferred_element_type=jnp.float32)


class PieceSum:
    def __init__(self, order, buffer, block, me, sems, count):
        self.order, self.buffer, self.block, self.me, self.sems = order, buffer, block, me, sems
        self.slots, self.index = {}, {}
        for level in range(len(order)):
            for bits in subsets(order[level + 1 :]):
                key = (level, frozenset(bits))
                self.slots[key] = len(POSITIONS) + len(self.slots)
                self.index[key] = count.next()

    def copy(self, level, bits):
        bit = self.order[level]
        key = (level, bits - {bit})
        return pltpu.make_async_remote_copy(
            src_ref=self.buffer.at[position(bits)],
            dst_ref=self.buffer.at[self.slots[key]],
            send_sem=self.sems[0].at[self.index[key]],
            recv_sem=self.sems[1].at[self.index[key]],
            device_id=moved(self.me, (bit,)),
            device_id_type=MESH,
        )

    def computed(self, bits):
        if self.order[0] in bits:
            self.copy(0, bits).start()

    def settle(self, level, bits):
        if any(bit in bits for bit in self.order[: level + 1]):
            return
        self.copy(level, bits | {self.order[level]}).wait_recv()
        kept = self.buffer.at[position(bits)]
        add_into(kept, kept, self.buffer.at[self.slots[(level, bits)]], self.block)
        if level + 1 < len(self.order) and self.order[level + 1] in bits:
            self.copy(level + 1, bits).start()

    def finish(self):
        for level, bits in self.index:
            self.copy(level, bits | {self.order[level]}).wait_send()


BLOCKS = 4


WAVES = subsets((Z_BIT, Y_BIT))
AHEAD = 1


def expert_kernel(shards, *refs):
    rows_ref, back_ref, gate_ref, in_ref, out_ref = refs[:5]
    moe_sum, grad_sum, mark_sum, half_in, half_out, grad_in, grad_out, far_in, far_out = refs[5:14]
    grad_buffers, moe_buffers, mark_buffer = refs[14:17], refs[17:20], refs[20]
    in_total, out_total, stage_in, stage_out, scaled, send, recv, local = refs[21:]
    away = [
        near + item for near in WAVES[:AHEAD] for item in subsets(far_bits(shards))[1:]
    ]
    low = jnp.bfloat16
    step = pl.program_id(0)
    block = step % BLOCKS
    me = here()
    twin = moved(me, (C_BIT,))
    sems = (send, recv)
    count = Counter()
    length = rows_ref.shape[0] // 2
    sums = [
        PieceSum(order, buffer, 128, me, sems, count)
        for turned, buffers in ((TURNED, grad_buffers), (TURNED, moe_buffers))
        for order, buffer in zip(turned, buffers)
    ]
    sums.append(PieceSum(TURNED[0], mark_buffer, length, me, sems, count))
    exchanged = [(stage_in, half_in, count.next()), (stage_out, half_out, count.next())]

    def halves():
        return [
            pltpu.make_async_remote_copy(
                src_ref=stage,
                dst_ref=half,
                send_sem=send.at[slot],
                recv_sem=recv.at[slot],
                device_id=twin,
                device_id_type=MESH,
            )
            for stage, half, slot in exchanged
        ]

    @pl.when(step == 0)
    def _():
        meet(neighbours(me, (X_BIT, C_BIT, Y_BIT, Z_BIT)) + [moved(me, bits) for bits in away])
        in_total[...] = jnp.zeros_like(in_total)
        out_total[...] = jnp.zeros_like(out_total)
        for buffer in grad_buffers + moe_buffers + (mark_buffer,):
            kept = buffer.at[pl.ds(0, len(POSITIONS))]
            kept[...] = jnp.zeros_like(kept)

    rows = rows_ref[...]
    gate = gate_ref[0]
    hidden_in = dot(rows, in_ref[0])
    gate_part = hidden_in[:, :H]
    up_part = hidden_in[:, H:]
    sigma = jax.nn.sigmoid(gate_part)
    active = gate_part * sigma
    hidden = (active * up_part).astype(low)
    width = rows.shape[1] // 3
    pair = pl.ds(2 * block, 2)

    def add_pieces(buffer, value):
        value = value.reshape((2, length) + value.shape[1:])
        buffer[pair] = (buffer[pair].astype(jnp.float32) + value).astype(low)

    mark = jnp.zeros((2 * length, 1), jnp.float32)
    for third in range(3):
        columns = slice(third * width, (third + 1) * width)
        result = dot(hidden, out_ref[0, :, columns])
        back = back_ref[:, columns].astype(jnp.float32)
        mark += jnp.sum(back * result, axis=1, keepdims=True)
        add_pieces(moe_buffers[third], gate * result)
        scaled[:, columns] = (gate * back).astype(low)
    expert = jnp.where(step < BLOCKS, twin[0], me[0]) * GROUP + me[1] % GROUP
    mark_low = mark.astype(low).astype(jnp.float32)
    lane = lax.broadcasted_iota(jnp.int32, (2 * length, 128), 1)
    add_pieces(
        mark_buffer,
        jnp.where(lane == expert, mark_low, jnp.where(lane == expert + E, mark - mark_low, 0.0)),
    )
    grad_result = scaled[...]
    grad_hidden = dot(grad_result, out_ref[0], ((1,), (1,)))
    out_total[...] += dot(hidden, grad_result, ((0,), (0,)))
    grad_gate_part = grad_hidden * up_part * sigma * (1.0 + gate_part * (1.0 - sigma))
    grad_up_part = grad_hidden * active
    grad_rows = jnp.concatenate([grad_gate_part, grad_up_part], axis=1).astype(low)
    for third in range(3):
        columns = slice(third * width, (third + 1) * width)
        add_pieces(grad_buffers[third], dot(grad_rows, in_ref[0, columns], ((1,), (1,))))
    in_total[...] += dot(rows, grad_rows, ((0,), (0,)))

    @pl.when(step == BLOCKS - 1)
    def _():
        stage_in[...] = in_total[...].astype(low)
        stage_out[...] = out_total[...].astype(low)
        for copy in halves():
            copy.start()
        in_total[...] = jnp.zeros_like(in_total)
        out_total[...] = jnp.zeros_like(out_total)

    def settle(level, number):
        for bits in POSITIONS[2 * number : 2 * number + 2]:
            for item in sums:
                item.settle(level, bits)

    for number in range(BLOCKS):

        @pl.when(step == BLOCKS + number)
        def _():
            for bits in POSITIONS[2 * number : 2 * number + 2]:
                for item in sums:
                    item.computed(bits)
            if number >= 1:
                settle(0, number - 1)
            if number >= 2:
                settle(1, number - 2)

    @pl.when(step == 2 * BLOCKS - 1)
    def _():
        loads = []
        for number, (copy, (stage, half, _)) in enumerate(zip(halves(), exchanged)):
            copy.wait()
            load = pltpu.make_async_copy(half, stage, local.at[number])
            load.start()
            loads.append(load)
        stores = []
        far_copies = []
        for number, (total, stage, goal, landed) in enumerate(
            ((in_total, stage_in, grad_in, far_in), (out_total, stage_out, grad_out, far_out))
        ):
            loads[number].wait()
            stage[...] = (total[...] + stage[...].astype(jnp.float32)).astype(low)
            store = pltpu.make_async_copy(stage, goal, local.at[2 + number])
            store.start()
            stores.append(store)
            rows_each = stage.shape[0] // shards
            for index, bits in enumerate(away):
                place = moved(me, bits)
                window = pl.ds(pl.multiple_of(place[1] * rows_each, 16), rows_each)
                far_copies.append(
                    start_copy(stage.at[window], landed.at[index], sems, count.next(), place)
                )
        settle(0, BLOCKS - 1)
        for number in (BLOCKS - 2, BLOCKS - 1):
            settle(1, number)
        for number in range(BLOCKS):
            settle(2, number)
        own = position(())
        for item, goal in zip(
            sums,
            [grad_sum.at[:, pl.ds(i * width, width)] for i in range(3)]
            + [moe_sum.at[:, pl.ds(i * width, width)] for i in range(3)]
            + [mark_sum],
        ):
            store = pltpu.make_async_copy(item.buffer.at[own], goal, local.at[len(stores) + 2])
            store.start()
            stores.append(store)
        for item in sums:
            item.finish()
        for copy in far_copies:
            copy.wait()
        for store in stores:
            store.wait()


def expert_call(rows, back, gate, full_in, full_out, shards):
    _, length, width = rows.shape
    count = len(POSITIONS) * length
    low = jnp.bfloat16
    block = 2 * length
    rows, back = rows.reshape(count, width), back.reshape(count, width)

    def weights(array):
        return pl.BlockSpec(
            (1,) + array.shape[1:], lambda i: (i // BLOCKS, 0, 0), pipeline_mode=pl.Buffered(1)
        )

    def like(array):
        return jax.ShapeDtypeStruct(array.shape[1:], low)

    sequence = jax.ShapeDtypeStruct((length, width), low)
    pieces = 2 * len(POSITIONS) - 1
    ahead = AHEAD * (shards // GROUP - 1)
    slots = 7 * 7 + 2 + 2 * ahead

    def landing(array):
        return jax.ShapeDtypeStruct((ahead, array.shape[1] // shards, array.shape[2]), low)

    return pl.pallas_call(
        functools.partial(expert_kernel, shards),
        grid=(2 * BLOCKS,),
        out_shape=[
            sequence,
            sequence,
            jax.ShapeDtypeStruct((length, 128), low),
            like(full_in),
            like(full_out),
            like(full_in),
            like(full_out),
            landing(full_in),
            landing(full_out),
        ],
        in_specs=[
            pl.BlockSpec((block, width), lambda i: (i % BLOCKS, 0)),
            pl.BlockSpec((block, width), lambda i: (i % BLOCKS, 0)),
            pl.BlockSpec((1, block, 1), lambda i: (i // BLOCKS, i % BLOCKS, 0)),
            weights(full_in),
            weights(full_out),
        ],
        out_specs=anywhere(9),
        scratch_shapes=[pltpu.VMEM((pieces, length, width // 3), low)] * 6
        + [
            pltpu.VMEM((pieces, length, 128), low),
            pltpu.VMEM(full_in.shape[1:], jnp.float32),
            pltpu.VMEM(full_out.shape[1:], jnp.float32),
            pltpu.VMEM(full_in.shape[1:], low),
            pltpu.VMEM(full_out.shape[1:], low),
            pltpu.VMEM((block, width), low),
            pltpu.SemaphoreType.DMA((slots,)),
            pltpu.SemaphoreType.DMA((slots,)),
            pltpu.SemaphoreType.DMA((12,)),
        ],
        compiler_params=pltpu.CompilerParams(
            collective_id=2,
            has_side_effects=True,
            vmem_limit_bytes=EXPERT_VMEM_BYTES,
            dimension_semantics=("arbitrary",),
        ),
        name="experts",
    )(rows, back, gate, full_in, full_out)


def turned_back(tile, tables):
    cosine, sine_up, sine_down = tables
    return (
        tile * cosine - pltpu.roll(tile, 96, 1) * sine_up - pltpu.roll(tile, 32, 1) * sine_down
    )


def close_kernel(shards, reps, *refs):
    (branch, attention, acts, lse, allowed, normed, x, grad_mid, gain, small) = refs[:10]
    tables = [ref[...] for ref in refs[10:13]]
    qkv_w, out_w, g_in, g_down, far_in, far_down = refs[13:19]
    qkv_sum, out_sum, small_sum, in_sum, down_sum, tokens_grad, qkv_part, out_part = refs[19:27]
    dense = refs[27:33]
    tiny, in_land, down_land, in_own, down_own = refs[33:38]
    qkv_held, out_held, stage, acts_grad, heads_grad, small_held = refs[38:44]
    send, recv, local = refs[44:]
    low = jnp.bfloat16
    me = here()
    sems = (send, recv)
    far = far_bits(shards)
    partners = [moved(me, item) for item in subsets((Y_BIT, Z_BIT) + far)[1:]]
    meet(neighbours(me, (X_BIT, C_BIT)) + partners)
    count, local_count = Counter(), Counter()
    sends = []
    tail = []
    loads = []
    for source, held in ((out_w, out_held), (qkv_w, qkv_held)):
        load = pltpu.make_async_copy(source, held, local.at[local_count.next()])
        load.start()
        loads.append(load)
    columns_of = []
    groups = []
    for which, (source, target) in enumerate(((qkv_part, qkv_sum), (out_part, out_sum))):
        flows = []
        rows_each = source.shape[0] // shards
        height = rows_each // len(SUM_TURNED)
        width = source.shape[1] // reps
        for number, order in enumerate(SUM_TURNED):
            buffer = dense[which * 3 + number]

            def piece(place, source=source, number=number, height=height, width=width):
                start = place[1] * (height * len(SUM_TURNED)) + number * height
                return source.at[
                    pl.ds(pl.multiple_of(start, 16), height),
                    pl.ds(pl.multiple_of(place[0] * width, 128), width),
                ]

            def goal(place, bits=(), target=target, number=number, height=height, width=width):
                return target.at[
                    pl.ds(number * height, height),
                    pl.ds(pl.multiple_of(place[0] * width, 128), width),
                ]

            flows.append(((C_BIT,) + order + far, piece, buffer, height))
            columns_of.append((buffer, goal))
        groups.append(flows)
    tiny_order = (Y_BIT, Z_BIT) + far
    rows_each = small_held.shape[0] // shards

    def tiny_piece(place):
        return small_held.at[pl.ds(pl.multiple_of(place[1] * rows_each, 16), rows_each)]

    tiny_flow = (tiny_order, tiny_piece, tiny, 16)

    def sum_run(flows):
        return sum_steps(flows, me, sems, local, count, local_count, sends)

    def last_steps():
        for buffer, goal in columns_of:
            store = pltpu.make_async_copy(buffer.at[0], goal(me), local.at[local_count.next()])
            store.start()
            tail.append(store)
        columns = [
            ((X_BIT, C_BIT), lambda place, buffer=buffer: buffer.at[0], goal, only_self)
            for buffer, goal in columns_of
        ]
        yield from gather_steps(columns, me, sems, count, sends)
        base = halving_slots(len(tiny_order))
        current = 0
        for bit in (X_BIT, C_BIT):
            slot = count.next()
            landed = tiny.at[base]
            copy = start_copy(tiny.at[current], landed, sems, slot, moved(me, (bit,)))
            copy.wait()
            add_into(tiny.at[base + 1], tiny.at[current], landed, 16)
            current = base + 1
            base += 2
            yield
        store = pltpu.make_async_copy(tiny.at[current], small_sum, local.at[local_count.next()])
        store.start()
        tail.append(store)

    arrays = (
        (g_in, far_in, in_land, in_own, in_sum),
        (g_down, far_down, down_land, down_own, down_sum),
    )
    waves = WAVES
    ahead = [near + item for near in WAVES[:AHEAD] for item in subsets(far)[1:]]

    def expert_steps():
        waiting = [[] for _ in waves]

        def send_wave(number, items):
            for item in items:
                place = moved(me, waves[number] + item)
                for source, arrived, landed, _, _ in arrays:
                    bits = waves[number] + item
                    if bits and bits not in ahead:
                        slot = count.next()
                        sends.append(
                            start_copy(source.at[place[1]], landed.at[me[1]], sems, slot, place)
                        )
                        wait = pltpu.make_async_remote_copy(
                            src_ref=landed.at[place[1]],
                            dst_ref=landed.at[place[1]],
                            send_sem=send.at[slot],
                            recv_sem=recv.at[slot],
                            device_id=place,
                            device_id_type=MESH,
                        ).wait_recv
                    else:
                        origin = arrived.at[ahead.index(bits)] if bits else source.at[me[1]]
                        load = pltpu.make_async_copy(
                            origin, landed.at[place[1]], local.at[local_count.next()]
                        )
                        load.start()
                        wait = load.wait
                    waiting[number].append(wait)

        away = subsets(far)[1:]
        for number in range(len(waves)):
            send_wave(number, ((),))
        for number in range(len(waves)):
            send_wave(number, away)
        yield
        relays = []
        for number, near in enumerate(waves):
            for wait in waiting[number]:
                wait()
            place = moved(me, near)
            expert = place[1] % GROUP
            for _, _, landed, held, target in arrays:
                total = landed.at[place[1]]
                for item in subsets(far)[1:]:
                    part = landed.at[moved(place, item)[1]]
                    add_into(held.at[number], total, part, part.shape[0])
                    total = held.at[number]

                def goal(where, bits=(), target=target, expert=expert):
                    return target.at[where[0] * GROUP + expert]

                store = pltpu.make_async_copy(total, goal(me), local.at[local_count.next()])
                store.start()
                tail.append(store)
                flow = ((X_BIT, C_BIT), lambda where, total=total: total, goal, only_self)
                relay = gather_steps([flow], me, sems, count, sends)
                relays.append(relay)
                next(relay)
            yield
        for relay in relays:
            for _ in relay:
                yield

    def weight_grad(rows, grads, part):
        width = grads.shape[1]
        stores = []
        for number in range(rows.shape[1] // 256):
            if number >= 2:
                stores[number - 2].wait()
            held = stage.at[number % 2, :, pl.ds(0, width)]
            piece = rows[:, number * 256 : (number + 1) * 256]
            held[...] = dot(piece, grads[...], ((0,), (0,))).astype(low)
            store = pltpu.make_async_copy(
                held, part.at[pl.ds(number * 256, 256)], local.at[local_count.next()]
            )
            store.start()
            stores.append(store)
        for store in stores[-2:]:
            store.wait()

    def advance(run, steps):
        for _ in range(steps):
            if next(run, "end") == "end":
                return

    experts = expert_steps()
    next(experts)
    weight_grad(attention, branch, out_part)
    out_run = sum_run(groups[1])
    next(out_run)
    loads[0].wait()
    heads_grad[...] = dot(branch[...], out_held[...], ((1,), (1,))).astype(low)

    lane = lax.broadcasted_iota(jnp.int32, (1, 128), 1)
    sides = [(lane < HD).astype(jnp.float32), (lane >= HD).astype(jnp.float32)]
    sides_low = [side.astype(low) for side in sides]
    scale = HD ** (-0.5)
    group = HEADS // KV_HEADS

    def doubled(tile):
        tile = tile.astype(jnp.float32)
        other = pltpu.roll(tile, HD, 1)
        return [
            (tile * sides[0] + other * sides[1]).astype(low),
            (other * sides[0] + tile * sides[1]).astype(low),
        ]

    for pair in range(KV_HEADS // 2):
        keys = doubled(acts[:, QD + 128 * pair : QD + 128 * (pair + 1)])
        values = doubled(acts[:, QD + KVD + 128 * pair : QD + KVD + 128 * (pair + 1)])
        query_grads = [None] * group
        key_tile = value_tile = None
        for half in range(2):
            key_total = value_total = None
            for number in range(group):
                head = (2 * pair + half) * group + number
                tile, side = head // 2, head % 2
                columns = slice(128 * tile, 128 * (tile + 1))
                query = acts[:, columns] * sides_low[side]
                grad_out = heads_grad[:, columns] * sides_low[side]
                scores = dot(query, keys[half], ((1,), (1,))) * scale
                scores = jnp.where(allowed[...] > 0.5, scores, masked_score)
                probs = jnp.exp(scores - lse[:, head : head + 1])
                grad_probs = dot(grad_out, values[half], ((1,), (1,)))
                inner = jnp.sum(grad_probs * probs, axis=1, keepdims=True)
                grad_scores = (probs * (grad_probs - inner)).astype(low)
                value_part = dot(probs.astype(low), grad_out, ((0,), (0,)))
                key_part = dot(grad_scores, query, ((0,), (0,)))
                query_part = dot(grad_scores, keys[half]) * sides[side]
                local_tile = tile - group * pair
                if query_grads[local_tile] is None:
                    query_grads[local_tile] = query_part
                else:
                    query_grads[local_tile] += query_part
                key_total = key_part if key_total is None else key_total + key_part
                value_total = value_part if value_total is None else value_total + value_part
            key_total = (key_total + pltpu.roll(key_total, HD, 1)) * sides[half]
            value_total = (value_total + pltpu.roll(value_total, HD, 1)) * sides[half]
            key_tile = key_total if key_tile is None else key_tile + key_total
            value_tile = value_total if value_tile is None else value_tile + value_total
        for number in range(group):
            tile = group * pair + number
            acts_grad[:, 128 * tile : 128 * (tile + 1)] = turned_back(
                query_grads[number] * scale, tables
            ).astype(low)
        acts_grad[:, QD + 128 * pair : QD + 128 * (pair + 1)] = turned_back(
            key_tile * scale, tables
        ).astype(low)
        acts_grad[:, QD + KVD + 128 * pair : QD + KVD + 128 * (pair + 1)] = value_tile.astype(low)
        advance(out_run, OUT_STEPS[pair])
        advance(experts, EARLY[pair])

    weight_grad(normed, acts_grad, qkv_part)
    qkv_run = sum_run(groups[0])
    next(qkv_run)
    loads[1].wait()
    grad_normed = dot(acts_grad[...], qkv_held[...], ((1,), (1,)))
    value = x[...].astype(jnp.float32)
    spread = lax.rsqrt(jnp.mean(value * value, axis=-1, keepdims=True) + norm_eps)
    normal = value * spread
    inner = grad_normed * gain[...]
    tokens_grad[...] = grad_mid[...] + spread * (
        inner - normal * jnp.mean(inner * normal, axis=-1, keepdims=True)
    )
    gain_grad = lax.dot_general(
        grad_normed * normal,
        jnp.ones((value.shape[0], 128), jnp.float32),
        (((0,), (0,)), ((), ())),
        precision=HIGH,
        preferred_element_type=jnp.float32,
    )
    column = lax.broadcasted_iota(jnp.int32, gain_grad.shape, 1)
    small_held[...] = jnp.where(
        column == E, gain_grad, small[...].astype(jnp.float32)
    ).astype(low)
    third = sum_run([tiny_flow])
    next(third)

    mixed = [(qkv_run, 6), (out_run, 6), (experts, 1), (third, 1)]
    alive = [run for run, _ in mixed]
    while alive:
        for run, turns in mixed:
            for _ in range(turns):
                if run in alive and next(run, "end") == "end":
                    alive.remove(run)
    for _ in last_steps():
        pass
    for copy in sends:
        copy.wait_send()
    for copy in tail:
        copy.wait()


def close_call(near, weights, experts, shards, reps):
    branch, acts, small = near[0], near[2], near[9]
    qkv_w, out_w = weights
    g_in, g_down = experts[:2]
    far = far_bits(shards)
    size = 4 + len(far)
    pieces = halving_slots(size)
    low = jnp.bfloat16
    length = branch.shape[0]

    def part(array):
        return array.shape[0] // shards, array.shape[1]

    def dense_buffer(array):
        rows, columns = part(array)
        return [pltpu.VMEM((pieces, rows // 3, columns // reps), low)] * 3

    small_rows = small.shape[0] // shards
    tiny_pieces = halving_slots(2 + len(far)) + 4
    slots = 7 * (2**size - 1) + 2 * shards + 14 * 3 + 4
    vmem = pl.BlockSpec(memory_space=pltpu.VMEM)
    return pl.pallas_call(
        functools.partial(close_kernel, shards, reps),
        out_shape=[
            jax.ShapeDtypeStruct(part(qkv_w), low),
            jax.ShapeDtypeStruct(part(out_w), low),
            jax.ShapeDtypeStruct((small_rows, 128), low),
        ]
        + [
            jax.ShapeDtypeStruct((reps * GROUP,) + array.shape[1:], low) for array in (g_in, g_down)
        ]
        + [
            jax.ShapeDtypeStruct((length, D), jnp.float32),
            jax.ShapeDtypeStruct(qkv_w.shape, low),
            jax.ShapeDtypeStruct(out_w.shape, low),
        ],
        in_specs=[vmem] * len(near) + anywhere(6),
        out_specs=anywhere(5) + [vmem] + anywhere(2),
        scratch_shapes=dense_buffer(qkv_w)
        + dense_buffer(out_w)
        + [
            pltpu.VMEM((tiny_pieces, small_rows, 128), low),
            pltpu.VMEM(g_in.shape, low),
            pltpu.VMEM(g_down.shape, low),
            pltpu.VMEM((GROUP,) + g_in.shape[1:], low),
            pltpu.VMEM((GROUP,) + g_down.shape[1:], low),
            pltpu.VMEM(qkv_w.shape, low),
            pltpu.VMEM(out_w.shape, low),
            pltpu.VMEM((2, 256, qkv_w.shape[1]), low),
            pltpu.VMEM(acts.shape, low),
            pltpu.VMEM(branch.shape, low),
            pltpu.VMEM(small.shape, low),
            pltpu.SemaphoreType.DMA((slots,)),
            pltpu.SemaphoreType.DMA((slots,)),
            pltpu.SemaphoreType.DMA((7 * 2 ** (size - 1) + 64,)),
        ],
        compiler_params=pltpu.CompilerParams(
            collective_id=3, has_side_effects=True, vmem_limit_bytes=EXPERT_VMEM_BYTES
        ),
        name="close_sums",
    )(*near, *weights, *experts)


def on_device(
    shards,
    reps,
    tokens,
    segments,
    routes,
    cotangent,
    wqkv,
    wqkv_first,
    wqkv_second,
    wo,
    wo_first,
    wo_second,
    router,
    router_first,
    router_second,
    w_in,
    w_in_first,
    w_in_second,
    w_out,
    w_out_first,
    w_out_second,
    gains,
    gains_first,
    gains_second,
):
    length, width = tokens.shape
    group = HEADS // KV_HEADS
    segs = segments[0]
    rep, shard = here()
    low = jnp.bfloat16

    def cut(array):
        return array.astype(low).reshape((shards, array.shape[0] // shards) + array.shape[1:])

    small = jnp.concatenate(
        [router, gains.T, jnp.zeros((router.shape[0], 128 - E - 2), jnp.float32)], axis=1
    ).astype(low)
    mine_in = lax.dynamic_slice_in_dim(w_in, rep * GROUP, GROUP, 0).astype(low)
    mine_out = lax.dynamic_slice_in_dim(w_out, rep * GROUP, GROUP, 0).astype(low)
    qkv_w, out_w, small_w, full_in, full_out, cot_all = open_call(
        wqkv.astype(low), wo.astype(low), small, mine_in, mine_out, cotangent, shards, reps
    )
    qkv_w = qkv_w.reshape(D, -1)
    out_w = out_w.reshape(QD, D)
    small_w = small_w.reshape(D, 128)
    router_w = small_w[:, :E]
    gain_f = small_w[:, E : E + 2].astype(jnp.float32).T

    x = tokens.astype(jnp.float32)
    normed = rms_norm(x, gain_f[0]).astype(low)
    qkv = jnp.dot(normed, qkv_w, preferred_element_type=jnp.float32)
    query = (
        rotary(qkv[:, :QD].reshape(length, HEADS, HD))
        .astype(low)
        .reshape(length, KV_HEADS, group, HD)
    )
    keys = rotary(qkv[:, QD : QD + KVD].reshape(length, KV_HEADS, HD)).astype(low)
    values = qkv[:, QD + KVD :].reshape(length, KV_HEADS, HD).astype(low)
    attended, lses = attend_forward(query, keys, values, segs)
    attention = attended.reshape(length, QD)
    branch = jnp.dot(attention, out_w, preferred_element_type=jnp.float32)
    mid = x + branch
    normed2 = rms_norm(mid, gain_f[1]).astype(low)
    logits = jnp.dot(normed2, router_w, preferred_element_type=jnp.float32)
    picks = (routes[:, :, None] == jnp.arange(E, dtype=jnp.int32)[None, None, :]).any(axis=1)
    gates = jax.nn.softmax(jnp.where(picks, logits, -jnp.inf), axis=-1)

    rows, gates_all = spread_call(normed2, gates.T)
    gate = jnp.stack(
        [
            lax.dynamic_index_in_dim(gates_all, flip(rep, 0) * GROUP + shard % GROUP, 1, False),
            lax.dynamic_index_in_dim(gates_all, rep * GROUP + shard % GROUP, 1, False),
        ]
    ).reshape(2, -1, 1)
    moe, grad_normed2, marks, _, _, grad_in, grad_down, far_in, far_down = expert_call(
        rows, cot_all, gate, full_in.reshape(2, D, 2 * H), full_out.reshape(2, H, D), shards
    )
    marks = marks.astype(jnp.float32)
    grad_gates = marks[:, :E] + marks[:, E : 2 * E]
    mixed = (mid + moe.astype(jnp.float32)).astype(low)

    grad_logits = gates * (grad_gates - jnp.sum(grad_gates * gates, axis=-1, keepdims=True))
    grad_router = jnp.dot(normed2.astype(jnp.float32).T, grad_logits, precision=HIGH)
    grad_normed2 = grad_normed2.astype(jnp.float32) + jnp.dot(
        grad_logits, router_w.astype(jnp.float32).T, precision=HIGH
    )
    cot = cotangent.astype(jnp.float32)
    grad_mid_norm, grad_gain2 = norm_back(mid, gain_f[1], grad_normed2)
    grad_mid = cot + grad_mid_norm
    grad_branch = grad_mid.astype(low)
    grad_small = jnp.concatenate(
        [
            grad_router,
            jnp.zeros((D, 1), jnp.float32),
            grad_gain2[:, None],
            jnp.zeros((D, 128 - E - 2), jnp.float32),
        ],
        axis=1,
    ).astype(low)
    acts = jnp.concatenate(
        [query.reshape(length, QD), keys.reshape(length, KVD), values.reshape(length, KVD)], axis=1
    )
    lse_columns = jnp.pad(lses.reshape(HEADS, length).T, ((0, 0), (0, 128 - HEADS)))
    places = jnp.arange(length, dtype=jnp.int32)
    allowed = (places[:, None] >= places[None, :]) & (segs[:, None] == segs[None, :])
    cosine, sine, _ = angle_tables(length, HD)
    cosine, sine = cosine[:, 0], sine[:, 0]
    blank = jnp.zeros_like(sine)
    grad_qkv_w, grad_out_w, grad_small, grad_in_all, grad_down_all, tokens_grad, _, _ = close_call(
        (
            grad_branch,
            attention,
            acts,
            lse_columns,
            allowed.astype(jnp.float32),
            normed,
            tokens,
            grad_mid,
            gain_f[:1],
            grad_small,
            jnp.concatenate([cosine] * 4, axis=1),
            jnp.concatenate([-sine, blank] * 2, axis=1),
            jnp.concatenate([blank, sine] * 2, axis=1),
        ),
        (qkv_w, out_w),
        (cut(grad_in), cut(grad_down), far_in, far_down),
        shards,
        reps,
    )
    grad_small = grad_small.astype(jnp.float32)
    grad_router = grad_small[:, :E]
    grad_gains = grad_small[:, E : E + 2].T
    qkv_m, qkv_v, qkv_new = adamw(
        wqkv, wqkv_first, wqkv_second, grad_qkv_w.astype(jnp.float32), 3.0 * D ** (-0.5), decay_rate
    )
    out_m, out_v, out_new = adamw(
        wo, wo_first, wo_second, grad_out_w.astype(jnp.float32), 3.0 * (QD // 64) ** (-0.5), decay_rate
    )
    rout_m, rout_v, rout_new = adamw(
        router, router_first, router_second, grad_router, 1.5 * D ** (-0.5), decay_rate
    )
    in_m, in_v, in_new = adamw(
        w_in, w_in_first, w_in_second, grad_in_all.astype(jnp.float32), 3.0 * D ** (-0.5), decay_rate
    )
    down_m, down_v, down_new = adamw(
        w_out,
        w_out_first,
        w_out_second,
        grad_down_all.astype(jnp.float32),
        3.0 * (H // 16) ** (-0.5),
        decay_rate,
    )
    gain_m, gain_v, gain_new = adamw(gains, gains_first, gains_second, grad_gains, 0.6, 0.0)
    return (
        mixed,
        tokens_grad,
        qkv_m,
        qkv_v,
        qkv_new,
        out_m,
        out_v,
        out_new,
        rout_m,
        rout_v,
        rout_new,
        in_m,
        in_v,
        in_new,
        down_m,
        down_v,
        down_new,
        gain_m,
        gain_v,
        gain_new,
    )


def solution(mesh):
    in_specs = (
        P(("rep", "shard"), None),
        P(("rep", "shard"), None),
        P(("rep", "shard"), None),
        P(("rep", "shard"), None),
        P("shard", None),
        P("shard", None),
        P("shard", None),
        P("shard", None),
        P("shard", None),
        P("shard", None),
        P("shard", None),
        P("shard", None),
        P("shard", None),
        P(None, "shard", None),
        P(None, "shard", None),
        P(None, "shard", None),
        P(None, "shard", None),
        P(None, "shard", None),
        P(None, "shard", None),
        P(None, "shard"),
        P(None, "shard"),
        P(None, "shard"),
    )
    out_specs = (
        P(("rep", "shard"), None),
        P(("rep", "shard"), None),
        P("shard", None),
        P("shard", None),
        P("shard", None),
        P("shard", None),
        P("shard", None),
        P("shard", None),
        P("shard", None),
        P("shard", None),
        P("shard", None),
        P(None, "shard", None),
        P(None, "shard", None),
        P(None, "shard", None),
        P(None, "shard", None),
        P(None, "shard", None),
        P(None, "shard", None),
        P(None, "shard"),
        P(None, "shard"),
        P(None, "shard"),
    )
    return jax.shard_map(
        functools.partial(on_device, mesh.shape["shard"], mesh.shape["rep"]), mesh=mesh, in_specs=in_specs, out_specs=out_specs, check_vma=False
    )
```

```python
import functools

import jax
import jax.numpy as jnp
from jax import lax
from jax.experimental import pallas as pl
from jax.experimental.pallas import tpu as pltpu
from jax.sharding import PartitionSpec as P

D = 1536
H = 512
HEADS = 24
KV_HEADS = 8
HD = 64
E = 16
TOP = 8
STEP = 10
QD = 1536
KVD = 512
GROUP = 4

HIGH = lax.Precision.HIGHEST
MESH = pl.DeviceIdType.MESH
norm_eps = 1e-06
beta_one = 0.9
beta_two = 0.95
adam_eps = 1e-08
decay_rate = 0.1
masked_score = -1e30
HOOK = 0
OUT_STEPS = (0, 3, 0, 0)
PIECE = 384
EARLY = (1, 1, 0, 1)
VMEM_BYTES = 56 * 2**20
EXPERT_VMEM_BYTES = 62 * 2**20


def flip(index, bit):
    step = 2**bit
    return index + (1 - 2 * ((index // step) % 2)) * step


def moved(place, bits):
    rep, shard = place
    for axis, bit in bits:
        if axis == "r":
            rep = flip(rep, bit)
        else:
            shard = flip(shard, bit)
    return (rep, shard)


def subsets(bits):
    result = [()]
    for bit in bits:
        result = result + [item + (bit,) for item in result]
    return result


def here():
    return (lax.axis_index("rep"), lax.axis_index("shard"))


def meet(places):
    barrier = pltpu.get_barrier_semaphore()
    for place in places:
        pl.semaphore_signal(barrier, inc=1, device_id=place, device_id_type=MESH)
    pl.semaphore_wait(barrier, len(places))


def start_copy(source, target, sems, index, place):
    copy = pltpu.make_async_remote_copy(
        src_ref=source,
        dst_ref=target,
        send_sem=sems[0].at[index],
        recv_sem=sems[1].at[index],
        device_id=place,
        device_id_type=MESH,
    )
    copy.start()
    return copy


class Counter:
    def __init__(self):
        self.value = 0

    def next(self):
        self.value += 1
        return self.value - 1


def gather_flows(flows, me, sems, count, hooks=()):
    sends = []
    for _ in gather_steps(flows, me, sems, count, sends, hooks):
        pass
    return sends


def gather_steps(flows, me, sems, count, sends, hooks=()):
    plans = []
    for order, source, target, local in flows:
        index = {}
        for level, bit in enumerate(order):
            for bits in subsets(order[:level]):
                if not (bit[0] == "r" and local(bits) and local(bits + (bit,))):
                    index[(level, bits)] = count.next()
        plans.append(index)
    deepest = max(len(order) for order, _, _, _ in flows)

    def push(flow, number, level, bits, ready):
        order, source, target, local = flow
        if (level, bits) not in plans[number]:
            return
        place = moved(me, bits)
        origin = source(place) if ready else target(place, bits)
        goal = target(place, bits + (order[level],))
        slot = plans[number][(level, bits)]
        sends.append(start_copy(origin, goal, sems, slot, moved(me, (order[level],))))

    for level in range(deepest):
        for number, flow in enumerate(flows):
            order, source, target, local = flow
            if level < len(order):
                for bits in subsets(order[:level]):
                    if local(bits):
                        push(flow, number, level, bits, True)
    yield
    hooks = dict(hooks)
    if -1 in hooks:
        hooks[-1]()
    for level in range(deepest):
        for turn in range(2**level):
            for number, flow in enumerate(flows):
                order, source, target, local = flow
                if level >= len(order):
                    continue
                bits = subsets(order[:level])[turn]
                key = (level, bits)
                if key not in plans[number]:
                    continue
                full = bits + (order[level],)
                place = moved(me, full)
                slot = plans[number][key]
                pltpu.make_async_remote_copy(
                    src_ref=target(place, full),
                    dst_ref=target(place, full),
                    send_sem=sems[0].at[slot],
                    recv_sem=sems[1].at[slot],
                    device_id=moved(me, (order[level],)),
                    device_id_type=MESH,
                ).wait_recv()
                for later in range(level + 1, len(order)):
                    push(flow, number, later, full, False)
                yield
        if level in hooks:
            hooks[level]()


def gather_slots(orders):
    return sum(2 ** len(order) - 1 for order in orders)


def add_into(target, first, second, block):
    rows = first.shape[0]

    def body(index, carry):
        window = pl.ds(pl.multiple_of(index * block, block), block)
        target[window] = first[window] + second[window]
        return carry

    if rows == block:
        target[...] = first[...] + second[...]
    else:
        lax.fori_loop(0, rows // block, body, 0)


def halving_slots(length):
    return 2 ** (length - 1) + 2**length - 1


def sum_flows(flows, me, sems, local_sems, count, local_count):
    sends = []
    for _ in sum_steps(flows, me, sems, local_sems, count, local_count, sends):
        pass
    return sends


def sum_steps(flows, me, sems, local_sems, count, local_count, sends):
    loads = []
    plans = []
    for order, source, buffer, block in flows:
        size = len(order)
        held = subsets(order[1:][::-1])
        place_of = {frozenset(bits): i for i, bits in enumerate(held)}
        index, slots, base = {}, {}, len(held)
        for level in range(size):
            for bits in subsets(order[level + 1 :][::-1]):
                index[(level, frozenset(bits))] = count.next()
                slots[(level, frozenset(bits))] = base
                base += 1
        plans.append((place_of, index, slots))
    deepest = max(len(order) for order, _, _, _ in flows)

    def turns(order, level):
        names = subsets(order[level + 1 :][::-1])
        return names[::-1]

    for turn in range(2 ** (deepest - 1)):
        for number, (order, source, buffer, block) in enumerate(flows):
            names = turns(order, 0)
            if turn >= len(names):
                continue
            bits = names[turn]
            key = frozenset(bits)
            place_of, index, slots = plans[number]
            sends.append(
                start_copy(
                    source(moved(me, bits + (order[0],))),
                    buffer.at[slots[(0, key)]],
                    sems,
                    index[(0, key)],
                    moved(me, (order[0],)),
                )
            )
            load = pltpu.make_async_copy(
                source(moved(me, bits)), buffer.at[place_of[key]], local_sems.at[local_count.next()]
            )
            load.start()
            loads.append(((number, key), load))
    waiting = dict(loads)
    yield
    for level in range(deepest):
        for turn in range(2 ** (deepest - 1 - level)):
            for number, (order, source, buffer, block) in enumerate(flows):
                if level >= len(order):
                    continue
                names = turns(order, level)
                if turn >= len(names):
                    continue
                bits = names[turn]
                key = frozenset(bits)
                place_of, index, slots = plans[number]
                slot = index[(level, key)]
                landed = buffer.at[slots[(level, key)]]
                pltpu.make_async_remote_copy(
                    src_ref=landed,
                    dst_ref=landed,
                    send_sem=sems[0].at[slot],
                    recv_sem=sems[1].at[slot],
                    device_id=moved(me, (order[level],)),
                    device_id_type=MESH,
                ).wait_recv()
                if level == 0:
                    waiting[(number, key)].wait()
                kept = buffer.at[place_of[key]]
                add_into(kept, kept, landed, block)
                if level + 1 < len(order) and order[level + 1] in key:
                    after = key - {order[level + 1]}
                    sends.append(
                        start_copy(
                            kept,
                            buffer.at[slots[(level + 1, after)]],
                            sems,
                            index[(level + 1, after)],
                            moved(me, (order[level + 1],)),
                        )
                    )
                yield


def rms_norm(value, gain):
    scale = lax.rsqrt(jnp.mean(value * value, axis=-1, keepdims=True) + norm_eps)
    return value * scale * gain


def norm_back(value, gain, grad):
    scale = lax.rsqrt(jnp.mean(value * value, axis=-1, keepdims=True) + norm_eps)
    normal = value * scale
    grad_gain = jnp.sum(grad * normal, axis=0)
    inner = grad * gain
    grad_value = scale * (inner - normal * jnp.mean(inner * normal, axis=-1, keepdims=True))
    return (grad_value, grad_gain)


def angle_tables(length, width):
    halfway = width // 2
    freqs = 10000.0 ** (-jnp.arange(halfway, dtype=jnp.float32) / halfway)
    angles = jnp.arange(length, dtype=jnp.float32)[:, None] * freqs[None, :]
    return (jnp.cos(angles)[:, None, :], jnp.sin(angles)[:, None, :], halfway)


def rotary(value):
    cosine, sine, halfway = angle_tables(value.shape[0], value.shape[-1])
    first = value[..., :halfway]
    second = value[..., halfway:]
    return jnp.concatenate(
        [first * cosine - second * sine, second * cosine + first * sine], axis=-1
    )


def rotary_back(grad):
    cosine, sine, halfway = angle_tables(grad.shape[0], grad.shape[-1])
    first = grad[..., :halfway]
    second = grad[..., halfway:]
    return jnp.concatenate(
        [first * cosine + second * sine, second * cosine - first * sine], axis=-1
    )


def block_scores(rows, keys, segs):
    places = jnp.arange(keys.shape[0], dtype=jnp.int32)
    scores = jnp.einsum(
        "sgrd,tgd->grst", rows, keys, preferred_element_type=jnp.float32
    ) * rows.shape[-1] ** (-0.5)
    allowed = (places[:, None] >= places[None, :]) & (segs[:, None] == segs[None, :])
    return jnp.where(allowed, scores, masked_score)


def attend_forward(query, keys, values, segs):
    length = query.shape[0]
    block = min(length, 512)

    def one_block(index):
        scores = block_scores(query, keys, segs)
        top = jnp.max(scores, axis=-1, keepdims=True)
        lse = top + jnp.log(jnp.sum(jnp.exp(scores - top), axis=-1, keepdims=True))
        probs = jnp.exp(scores - lse).astype(jnp.bfloat16)
        output = jnp.einsum("grst,tgd->sgrd", probs, values, preferred_element_type=jnp.float32)
        return (output.astype(jnp.bfloat16), lse)

    outputs, lses = lax.map(one_block, jnp.arange(length // block))
    return (outputs.reshape(query.shape), lses)


def attend_backward(query, keys, values, segs, lses, grad_out):
    length = query.shape[0]
    block = min(length, 512)
    scale = query.shape[-1] ** (-0.5)

    def step(carry, item):
        grad_key, grad_value = carry
        index, lse = item
        probs = jnp.exp(block_scores(query, keys, segs) - lse)
        grad_value = grad_value + jnp.einsum(
            "grst,sgrd->tgd",
            probs.astype(jnp.bfloat16),
            grad_out,
            preferred_element_type=jnp.float32,
        )
        grad_probs = jnp.einsum(
            "sgrd,tgd->grst", grad_out, values, preferred_element_type=jnp.float32
        )
        grad_scores = (
            probs * (grad_probs - jnp.sum(grad_probs * probs, axis=-1, keepdims=True))
        ).astype(jnp.bfloat16)
        grad_rows = (
            jnp.einsum("grst,tgd->sgrd", grad_scores, keys, preferred_element_type=jnp.float32)
            * scale
        )
        grad_key = (
            grad_key
            + jnp.einsum("grst,sgrd->tgd", grad_scores, query, preferred_element_type=jnp.float32)
            * scale
        )
        return ((grad_key, grad_value), grad_rows)

    zeros = jnp.zeros(keys.shape, jnp.float32)
    (grad_key, grad_value), grad_query = lax.scan(
        step, (zeros, zeros), (jnp.arange(length // block), lses)
    )
    return (grad_query.reshape(query.shape), grad_key, grad_value)


def adamw(weight, first, second, grad, rate, decay):
    first_new = beta_one * first + (1.0 - beta_one) * grad
    second_new = beta_two * second + (1.0 - beta_two) * grad * grad
    first_fix = 1.0 - beta_one**STEP
    second_fix = 1.0 - beta_two**STEP
    update = first_new / first_fix / (jnp.sqrt(second_new / second_fix) + adam_eps)
    return (first_new, second_new, weight - rate * (update + decay * weight))


X_BIT, C_BIT, Y_BIT, Z_BIT = ("r", 1), ("r", 0), ("s", 0), ("s", 1)
TURNED = (
    (X_BIT, Y_BIT, Z_BIT),
    (Y_BIT, Z_BIT, X_BIT),
    (Z_BIT, X_BIT, Y_BIT),
)
SUM_TURNED = (
    (Y_BIT, Z_BIT, X_BIT),
    (Z_BIT, Y_BIT, X_BIT),
    (Y_BIT, Z_BIT, X_BIT),
)
X_LAST = (
    (Z_BIT, Y_BIT, X_BIT),
    (Z_BIT, Y_BIT, X_BIT),
    (Z_BIT, Y_BIT, X_BIT),
)


POSITIONS = [
    frozenset(bits)
    for bits in (
        (X_BIT, Y_BIT, Z_BIT),
        (X_BIT, Y_BIT),
        (X_BIT, Z_BIT),
        (Y_BIT, Z_BIT),
        (X_BIT,),
        (Y_BIT,),
        (Z_BIT,),
        (),
    )
]


def position(bits):
    return POSITIONS.index(frozenset(bits))


def far_bits(shards):
    return tuple(("s", i) for i in range(2, shards.bit_length() - 1))


def only_self(bits):
    return not bits


def same_shard(bits):
    return all(axis == "r" for axis, _ in bits)


def token_flows(source, target, orders):
    width = source.shape[-1] // len(orders)
    flows = []
    for number, order in enumerate(orders):
        columns = pl.ds(number * width, width)
        flows.append(
            (
                order,
                lambda place, columns=columns: source.at[:, columns],
                lambda place, bits, columns=columns: target.at[position(bits), :, columns],
                only_self,
            )
        )
    return flows


def share_flows(source, target, orders, reps):
    height = source.shape[0] // len(orders)
    width = source.shape[1] // reps
    flows = []

    def columns_of(place):
        return pl.ds(pl.multiple_of(place[0] * width, 128), width)

    for number, order in enumerate(orders):
        rows = pl.ds(number * height, height)
        flows.append(
            (
                order,
                lambda place, rows=rows: source.at[rows, columns_of(place)],
                lambda place, bits, rows=rows: target.at[place[1], rows, columns_of(place)],
                same_shard,
            )
        )
    return flows


def neighbours(me, bits):
    return [moved(me, (bit,)) for bit in bits]


def open_kernel(shards, reps, *refs):
    qkv, out, small, w_in, w_out, cot = refs[:6]
    qkv_all, out_all, small_all, in_all, down_all, cot_all = refs[6:12]
    send, recv, local = refs[12:]
    me = here()
    sems = (send, recv)
    far = far_bits(shards)
    bits = (Y_BIT, Z_BIT) + far
    partners = [moved(me, item) for item in subsets(bits)[1:]][::-1]
    meet(neighbours(me, (X_BIT, C_BIT)) + partners)
    count = Counter()
    own = me[1]
    here_copies = [
        (qkv, qkv_all.at[own]),
        (out, out_all.at[own]),
        (small, small_all.at[own]),
        (w_in.at[own % GROUP], in_all.at[1, own]),
        (w_out.at[own % GROUP], down_all.at[1, own]),
        (cot, cot_all.at[position(())]),
    ]
    for number, (source, target) in enumerate(here_copies):
        pltpu.make_async_copy(source, target, local.at[number]).start()
    sends = []
    orders = [far + order + (C_BIT,) for order in X_LAST]
    flows = share_flows(qkv, qkv_all, orders, reps) + share_flows(out, out_all, orders, reps)
    flows.append(
        (far + (Y_BIT, Z_BIT), lambda place: small, lambda place, bits: small_all.at[place[1]], only_self)
    )
    flows += token_flows(cot, cot_all, X_LAST)
    direct = []

    def send_experts(chosen):
        for place in chosen:
            for source, target in ((w_in, in_all), (w_out, down_all)):
                slot = count.next()
                sends.append(
                    start_copy(source.at[place[1] % GROUP], target.at[1, own], sems, slot, place)
                )
                direct.append((target, place[1], slot, place))

    hooks = {HOOK: functools.partial(send_experts, partners)}
    sends += gather_flows(flows, me, sems, count, hooks)
    twin = moved(me, (C_BIT,))
    for source, target in ((w_in, in_all), (w_out, down_all)):
        sends.append(
            start_copy(source.at[own % GROUP], target.at[0, own], sems, count.next(), twin)
        )
    passed = [(target, own, count.value - 2 + i) for i, target in enumerate((in_all, down_all))]
    for target, index, slot, place in direct:
        landed = target.at[1, index]
        pltpu.make_async_remote_copy(
            src_ref=landed,
            dst_ref=landed,
            send_sem=send.at[slot],
            recv_sem=recv.at[slot],
            device_id=place,
            device_id_type=MESH,
        ).wait_recv()
        slot = count.next()
        sends.append(start_copy(landed, target.at[0, index], sems, slot, twin))
        passed.append((target, index, slot))
    for target, index, slot in passed:
        landed = target.at[0, index]
        pltpu.make_async_remote_copy(
            src_ref=landed,
            dst_ref=landed,
            send_sem=send.at[slot],
            recv_sem=recv.at[slot],
            device_id=twin,
            device_id_type=MESH,
        ).wait_recv()
    for copy in sends:
        copy.wait_send()
    for number, (source, target) in enumerate(here_copies):
        pltpu.make_async_copy(source, target, local.at[number]).wait()


def anywhere(count):
    return [pl.BlockSpec(memory_space=pl.ANY)] * count


def open_call(qkv, out, small, w_in, w_out, cot, shards, reps):
    def grown(array):
        return jax.ShapeDtypeStruct((shards,) + array.shape[-2:], array.dtype)

    shapes = [grown(array) for array in (qkv, out, small)]
    shapes += [
        jax.ShapeDtypeStruct((2, shards) + array.shape[1:], array.dtype) for array in (w_in, w_out)
    ]
    shapes.append(jax.ShapeDtypeStruct((len(POSITIONS),) + cot.shape, cot.dtype))
    slots = 6 * (shards * reps - 1) + shards + 4 * shards + 3 * 7
    return pl.pallas_call(
        functools.partial(open_kernel, shards, reps),
        out_shape=shapes,
        in_specs=anywhere(6),
        out_specs=anywhere(6),
        scratch_shapes=[
            pltpu.SemaphoreType.DMA((slots,)),
            pltpu.SemaphoreType.DMA((slots,)),
            pltpu.SemaphoreType.DMA((6,)),
        ],
        compiler_params=pltpu.CompilerParams(
            collective_id=0, has_side_effects=True, vmem_limit_bytes=VMEM_BYTES
        ),
        name="open_gather",
    )(qkv, out, small, w_in, w_out, cot)


def spread_kernel(*refs):
    rows, gate, rows_all, gate_all, send, recv, local = refs
    me = here()
    sems = (send, recv)
    meet(neighbours(me, (X_BIT, Y_BIT, Z_BIT)))
    count = Counter()
    copies = [
        (rows, rows_all.at[position(())]),
        (gate, gate_all.at[position(())]),
    ]
    for number, (source, target) in enumerate(copies):
        pltpu.make_async_copy(source, target, local.at[number]).start()
    flows = token_flows(rows, rows_all, TURNED)
    flows.append(
        (
            TURNED[0],
            lambda place: gate,
            lambda place, bits: gate_all.at[position(bits)],
            only_self,
        )
    )
    for copy in gather_flows(flows, me, sems, count):
        copy.wait_send()
    for number, (source, target) in enumerate(copies):
        pltpu.make_async_copy(source, target, local.at[number]).wait()


def spread_call(rows, gate):
    slots = 4 * 7
    return pl.pallas_call(
        spread_kernel,
        out_shape=[
            jax.ShapeDtypeStruct((len(POSITIONS),) + array.shape, array.dtype)
            for array in (rows, gate)
        ],
        in_specs=anywhere(2),
        out_specs=anywhere(2),
        scratch_shapes=[
            pltpu.SemaphoreType.DMA((slots,)),
            pltpu.SemaphoreType.DMA((slots,)),
            pltpu.SemaphoreType.DMA((2,)),
        ],
        compiler_params=pltpu.CompilerParams(
            collective_id=1, has_side_effects=True, vmem_limit_bytes=VMEM_BYTES
        ),
        name="spread_tokens",
    )(rows, gate)


def dot(a, b, dims=((1,), (0,))):
    return lax.dot_general(a, b, (dims, ((), ())), preferred_element_type=jnp.float32)


def bit_of(place, bit):
    return (place[0 if bit[0] == "r" else 1] // 2 ** bit[1]) % 2


class BlockSum:
    def __init__(self, order, source, rows, width, kept, lands, tools):
        self.order, self.source, self.rows, self.width = order, source, rows, width
        self.kept, self.lands = kept, lands
        self.me, self.sems, self.local, self.count, self.local_count, self.sends = tools
        self.mine = {bit: bit_of(self.me, bit) for bit in order}
        shard_bits = sorted((bit for bit in order if bit[0] == "s"), reverse=True)
        self.dims = (X_BIT,) + tuple(shard_bits)
        self.waits = {}

    def at(self, ref, level, chosen):
        left = [bit for bit in self.dims if bit not in self.order[1 : level + 1]]
        return ref.at[tuple(chosen.get(bit, slice(None)) for bit in left)]

    def begin(self):
        waits = []
        twin = moved(self.me, (C_BIT,))
        for x in range(2):

            def columns(c):
                start = pl.multiple_of((2 * x + c) * self.width, 128)
                window = (slice(None),) * (len(self.dims) - 1)
                return self.source.at[window + (self.rows, pl.ds(start, self.width))]

            core = self.mine[C_BIT]
            landed = self.lands[0].at[x]
            copy = start_copy(columns(1 - core), landed, self.sems, self.count.next(), twin)
            self.sends.append(copy)
            load = pltpu.make_async_copy(
                columns(core), self.kept.at[x], self.local.at[self.local_count.next()]
            )
            load.start()
            waits += [copy.wait_recv, load.wait]
        self.waits[0] = waits

    def step(self, level):
        for wait in self.waits[level]:
            wait()
        fixed = {bit: self.mine[bit] for bit in self.order[1 : level + 1]}
        following = self.order[level + 1] if level + 1 < len(self.order) else None
        rest = [bit for bit in self.dims if bit not in fixed and bit != following]
        sides = (1 - self.mine[following], self.mine[following]) if following else (None,)
        for number, side in enumerate(sides):
            for mask in range(2 ** len(rest)):
                chosen = {bit: (mask >> i) % 2 for i, bit in enumerate(rest)}
                if following:
                    chosen[following] = side
                landed = self.at(self.lands[level], level, chosen)
                kept = self.at(self.kept, 0, {**fixed, **chosen})
                add_into(kept, kept, landed, kept.shape[0])
            if following and number == 0:
                copy = start_copy(
                    self.at(self.kept, 0, {**fixed, following: side}),
                    self.lands[level + 1],
                    self.sems,
                    self.count.next(),
                    moved(self.me, (following,)),
                )
                self.sends.append(copy)
                self.waits[level + 1] = [copy.wait_recv]

    def result(self):
        return self.at(self.kept, 0, {bit: self.mine[bit] for bit in self.dims})


def block_steps(sums):
    for item in sums:
        item.begin()
    yield
    for level in range(len(sums[0].order)):
        for item in sums:
            item.step(level)
            yield


class PieceSum:
    def __init__(self, order, buffer, block, me, sems, count):
        self.order, self.buffer, self.block, self.me, self.sems = order, buffer, block, me, sems
        self.slots, self.index = {}, {}
        for level in range(len(order)):
            for bits in subsets(order[level + 1 :]):
                key = (level, frozenset(bits))
                self.slots[key] = len(POSITIONS) + len(self.slots)
                self.index[key] = count.next()

    def copy(self, level, bits):
        bit = self.order[level]
        key = (level, bits - {bit})
        return pltpu.make_async_remote_copy(
            src_ref=self.buffer.at[position(bits)],
            dst_ref=self.buffer.at[self.slots[key]],
            send_sem=self.sems[0].at[self.index[key]],
            recv_sem=self.sems[1].at[self.index[key]],
            device_id=moved(self.me, (bit,)),
            device_id_type=MESH,
        )

    def computed(self, bits):
        if self.order[0] in bits:
            self.copy(0, bits).start()

    def settle(self, level, bits):
        if any(bit in bits for bit in self.order[: level + 1]):
            return
        self.copy(level, bits | {self.order[level]}).wait_recv()
        kept = self.buffer.at[position(bits)]
        add_into(kept, kept, self.buffer.at[self.slots[(level, bits)]], self.block)
        if level + 1 < len(self.order) and self.order[level + 1] in bits:
            self.copy(level + 1, bits).start()

    def finish(self):
        for level, bits in self.index:
            self.copy(level, bits | {self.order[level]}).wait_send()


BLOCKS = 4


WAVES = subsets((Z_BIT, Y_BIT))
AHEAD = 1


def expert_kernel(shards, *refs):
    rows_ref, back_ref, gate_ref, in_ref, out_ref = refs[:5]
    moe_sum, grad_sum, mark_sum, half_in, half_out, grad_in, grad_out, far_in, far_out = refs[5:14]
    grad_buffers, moe_buffers, mark_buffer = refs[14:17], refs[17:20], refs[20]
    in_total, out_total, stage_in, stage_out, scaled, send, recv, local = refs[21:]
    away = [
        near + item for near in WAVES[:AHEAD] for item in subsets(far_bits(shards))[1:]
    ]
    low = jnp.bfloat16
    step = pl.program_id(0)
    block = step % BLOCKS
    me = here()
    twin = moved(me, (C_BIT,))
    sems = (send, recv)
    count = Counter()
    length = rows_ref.shape[0] // 2
    sums = [
        PieceSum(order, buffer, 128, me, sems, count)
        for turned, buffers in ((TURNED, grad_buffers), (TURNED, moe_buffers))
        for order, buffer in zip(turned, buffers)
    ]
    sums.append(PieceSum(TURNED[0], mark_buffer, length, me, sems, count))
    exchanged = [(stage_in, half_in, count.next()), (stage_out, half_out, count.next())]

    def halves():
        return [
            pltpu.make_async_remote_copy(
                src_ref=stage,
                dst_ref=half,
                send_sem=send.at[slot],
                recv_sem=recv.at[slot],
                device_id=twin,
                device_id_type=MESH,
            )
            for stage, half, slot in exchanged
        ]

    @pl.when(step == 0)
    def _():
        meet(neighbours(me, (X_BIT, C_BIT, Y_BIT, Z_BIT)) + [moved(me, bits) for bits in away])
        in_total[...] = jnp.zeros_like(in_total)
        out_total[...] = jnp.zeros_like(out_total)
        for buffer in grad_buffers + moe_buffers + (mark_buffer,):
            kept = buffer.at[pl.ds(0, len(POSITIONS))]
            kept[...] = jnp.zeros_like(kept)

    rows = rows_ref[...]
    gate = gate_ref[0]
    hidden_in = dot(rows, in_ref[0])
    gate_part = hidden_in[:, :H]
    up_part = hidden_in[:, H:]
    sigma = jax.nn.sigmoid(gate_part)
    active = gate_part * sigma
    hidden = (active * up_part).astype(low)
    width = rows.shape[1] // 3
    pair = pl.ds(2 * block, 2)

    def add_pieces(buffer, value):
        value = value.reshape((2, length) + value.shape[1:])
        buffer[pair] = (buffer[pair].astype(jnp.float32) + value).astype(low)

    mark = jnp.zeros((2 * length, 1), jnp.float32)
    for third in range(3):
        columns = slice(third * width, (third + 1) * width)
        result = dot(hidden, out_ref[0, :, columns])
        back = back_ref[:, columns].astype(jnp.float32)
        mark += jnp.sum(back * result, axis=1, keepdims=True)
        add_pieces(moe_buffers[third], gate * result)
        scaled[:, columns] = (gate * back).astype(low)
    expert = jnp.where(step < BLOCKS, twin[0], me[0]) * GROUP + me[1] % GROUP
    mark_low = mark.astype(low).astype(jnp.float32)
    lane = lax.broadcasted_iota(jnp.int32, (2 * length, 128), 1)
    add_pieces(
        mark_buffer,
        jnp.where(lane == expert, mark_low, jnp.where(lane == expert + E, mark - mark_low, 0.0)),
    )
    grad_result = scaled[...]
    grad_hidden = dot(grad_result, out_ref[0], ((1,), (1,)))
    out_total[...] += dot(hidden, grad_result, ((0,), (0,)))
    grad_gate_part = grad_hidden * up_part * sigma * (1.0 + gate_part * (1.0 - sigma))
    grad_up_part = grad_hidden * active
    grad_rows = jnp.concatenate([grad_gate_part, grad_up_part], axis=1).astype(low)
    for third in range(3):
        columns = slice(third * width, (third + 1) * width)
        add_pieces(grad_buffers[third], dot(grad_rows, in_ref[0, columns], ((1,), (1,))))
    in_total[...] += dot(rows, grad_rows, ((0,), (0,)))

    @pl.when(step == BLOCKS - 1)
    def _():
        stage_in[...] = in_total[...].astype(low)
        stage_out[...] = out_total[...].astype(low)
        for copy in halves():
            copy.start()
        in_total[...] = jnp.zeros_like(in_total)
        out_total[...] = jnp.zeros_like(out_total)

    def settle(level, number):
        for bits in POSITIONS[2 * number : 2 * number + 2]:
            for item in sums:
                item.settle(level, bits)

    for number in range(BLOCKS):

        @pl.when(step == BLOCKS + number)
        def _():
            for bits in POSITIONS[2 * number : 2 * number + 2]:
                for item in sums:
                    item.computed(bits)
            if number >= 1:
                settle(0, number - 1)
            if number >= 2:
                settle(1, number - 2)

    @pl.when(step == 2 * BLOCKS - 1)
    def _():
        loads = []
        for number, (copy, (stage, half, _)) in enumerate(zip(halves(), exchanged)):
            copy.wait()
            load = pltpu.make_async_copy(half, stage, local.at[number])
            load.start()
            loads.append(load)
        stores = []
        far_copies = []
        for number, (total, stage, goal, landed) in enumerate(
            ((in_total, stage_in, grad_in, far_in), (out_total, stage_out, grad_out, far_out))
        ):
            loads[number].wait()
            stage[...] = (total[...] + stage[...].astype(jnp.float32)).astype(low)
            store = pltpu.make_async_copy(stage, goal, local.at[2 + number])
            store.start()
            stores.append(store)
            rows_each = stage.shape[0] // shards
            for index, bits in enumerate(away):
                place = moved(me, bits)
                window = pl.ds(pl.multiple_of(place[1] * rows_each, 16), rows_each)
                far_copies.append(
                    start_copy(stage.at[window], landed.at[index], sems, count.next(), place)
                )
        settle(0, BLOCKS - 1)
        for number in (BLOCKS - 2, BLOCKS - 1):
            settle(1, number)
        for number in range(BLOCKS):
            settle(2, number)
        own = position(())
        for item, goal in zip(
            sums,
            [grad_sum.at[:, pl.ds(i * width, width)] for i in range(3)]
            + [moe_sum.at[:, pl.ds(i * width, width)] for i in range(3)]
            + [mark_sum],
        ):
            store = pltpu.make_async_copy(item.buffer.at[own], goal, local.at[len(stores) + 2])
            store.start()
            stores.append(store)
        for item in sums:
            item.finish()
        for copy in far_copies:
            copy.wait()
        for store in stores:
            store.wait()


def expert_call(rows, back, gate, full_in, full_out, shards):
    _, length, width = rows.shape
    count = len(POSITIONS) * length
    low = jnp.bfloat16
    block = 2 * length
    rows, back = rows.reshape(count, width), back.reshape(count, width)

    def weights(array):
        return pl.BlockSpec(
            (1,) + array.shape[1:], lambda i: (i // BLOCKS, 0, 0), pipeline_mode=pl.Buffered(1)
        )

    def like(array):
        return jax.ShapeDtypeStruct(array.shape[1:], low)

    sequence = jax.ShapeDtypeStruct((length, width), low)
    pieces = 2 * len(POSITIONS) - 1
    ahead = AHEAD * (shards // GROUP - 1)
    slots = 7 * 7 + 2 + 2 * ahead

    def landing(array):
        return jax.ShapeDtypeStruct((ahead, array.shape[1] // shards, array.shape[2]), low)

    return pl.pallas_call(
        functools.partial(expert_kernel, shards),
        grid=(2 * BLOCKS,),
        out_shape=[
            sequence,
            sequence,
            jax.ShapeDtypeStruct((length, 128), low),
            like(full_in),
            like(full_out),
            like(full_in),
            like(full_out),
            landing(full_in),
            landing(full_out),
        ],
        in_specs=[
            pl.BlockSpec((block, width), lambda i: (i % BLOCKS, 0)),
            pl.BlockSpec((block, width), lambda i: (i % BLOCKS, 0)),
            pl.BlockSpec((1, block, 1), lambda i: (i // BLOCKS, i % BLOCKS, 0)),
            weights(full_in),
            weights(full_out),
        ],
        out_specs=anywhere(9),
        scratch_shapes=[pltpu.VMEM((pieces, length, width // 3), low)] * 6
        + [
            pltpu.VMEM((pieces, length, 128), low),
            pltpu.VMEM(full_in.shape[1:], jnp.float32),
            pltpu.VMEM(full_out.shape[1:], jnp.float32),
            pltpu.VMEM(full_in.shape[1:], low),
            pltpu.VMEM(full_out.shape[1:], low),
            pltpu.VMEM((block, width), low),
            pltpu.SemaphoreType.DMA((slots,)),
            pltpu.SemaphoreType.DMA((slots,)),
            pltpu.SemaphoreType.DMA((12,)),
        ],
        compiler_params=pltpu.CompilerParams(
            collective_id=2,
            has_side_effects=True,
            vmem_limit_bytes=EXPERT_VMEM_BYTES,
            dimension_semantics=("arbitrary",),
        ),
        name="experts",
    )(rows, back, gate, full_in, full_out)


def turned_back(tile, tables):
    cosine, sine_up, sine_down = tables
    return (
        tile * cosine - pltpu.roll(tile, 96, 1) * sine_up - pltpu.roll(tile, 32, 1) * sine_down
    )


def close_kernel(shards, reps, *refs):
    (branch, attention, acts, lse, allowed, normed, x, grad_mid, gain, small) = refs[:10]
    tables = [ref[...] for ref in refs[10:13]]
    qkv_w, out_w, g_in, g_down, far_in, far_down = refs[13:19]
    qkv_sum, out_sum, small_sum, in_sum, down_sum, tokens_grad, qkv_part, out_part = refs[19:27]
    levels = 4 + len(far_bits(shards))
    dense = refs[27 : 27 + 6 * (levels + 1)]
    refs = refs[27 + 6 * (levels + 1) :]
    tiny, in_land, down_land, in_own, down_own = refs[:5]
    qkv_held, out_held, stage, acts_grad, heads_grad, small_held = refs[5:11]
    send, recv, local = refs[11:]
    low = jnp.bfloat16
    me = here()
    sems = (send, recv)
    far = far_bits(shards)
    partners = [moved(me, item) for item in subsets((Y_BIT, Z_BIT) + far)[1:]]
    meet(neighbours(me, (X_BIT, C_BIT)) + partners)
    count, local_count = Counter(), Counter()
    sends = []
    tail = []
    loads = []
    for source, held in ((out_w, out_held), (qkv_w, qkv_held)):
        load = pltpu.make_async_copy(source, held, local.at[local_count.next()])
        load.start()
        loads.append(load)
    columns_of = []
    groups = []
    tools = (me, sems, local, count, local_count, sends)
    for which, (source, target) in enumerate(((qkv_part, qkv_sum), (out_part, out_sum))):
        group = []
        height = source.shape[-2] // len(SUM_TURNED)
        width = source.shape[-1] // reps
        for number, order in enumerate(SUM_TURNED):
            buffers = dense[(3 * which + number) * (levels + 1) :][: levels + 1]
            rows = pl.ds(number * height, height)
            total = BlockSum(
                (C_BIT,) + order + far, source, rows, width, buffers[0], buffers[1:], tools
            )

            def goal(place, bits=(), target=target, rows=rows, width=width):
                return target.at[rows, pl.ds(pl.multiple_of(place[0] * width, 128), width)]

            group.append(total)
            columns_of.append((total, goal))
        groups.append(group)
    tiny_order = (Y_BIT, Z_BIT) + far
    rows_each = small_held.shape[0] // shards

    def tiny_piece(place):
        return small_held.at[pl.ds(pl.multiple_of(place[1] * rows_each, 16), rows_each)]

    tiny_flow = (tiny_order, tiny_piece, tiny, 16)

    def sum_run(flows):
        return sum_steps(flows, me, sems, local, count, local_count, sends)

    def last_steps():
        for total, goal in columns_of:
            store = pltpu.make_async_copy(total.result(), goal(me), local.at[local_count.next()])
            store.start()
            tail.append(store)
        columns = [
            ((X_BIT, C_BIT), lambda place, total=total: total.result(), goal, only_self)
            for total, goal in columns_of
        ]
        yield from gather_steps(columns, me, sems, count, sends)
        base = halving_slots(len(tiny_order))
        current = 0
        for bit in (X_BIT, C_BIT):
            slot = count.next()
            landed = tiny.at[base]
            copy = start_copy(tiny.at[current], landed, sems, slot, moved(me, (bit,)))
            copy.wait()
            add_into(tiny.at[base + 1], tiny.at[current], landed, 16)
            current = base + 1
            base += 2
            yield
        store = pltpu.make_async_copy(tiny.at[current], small_sum, local.at[local_count.next()])
        store.start()
        tail.append(store)

    arrays = (
        (g_in, far_in, in_land, in_own, in_sum),
        (g_down, far_down, down_land, down_own, down_sum),
    )
    waves = WAVES
    ahead = [near + item for near in WAVES[:AHEAD] for item in subsets(far)[1:]]

    def expert_steps():
        waiting = [[] for _ in waves]

        def send_wave(number, items):
            for item in items:
                place = moved(me, waves[number] + item)
                for source, arrived, landed, _, _ in arrays:
                    bits = waves[number] + item
                    if bits and bits not in ahead:
                        slot = count.next()
                        sends.append(
                            start_copy(source.at[place[1]], landed.at[me[1]], sems, slot, place)
                        )
                        wait = pltpu.make_async_remote_copy(
                            src_ref=landed.at[place[1]],
                            dst_ref=landed.at[place[1]],
                            send_sem=send.at[slot],
                            recv_sem=recv.at[slot],
                            device_id=place,
                            device_id_type=MESH,
                        ).wait_recv
                    else:
                        origin = arrived.at[ahead.index(bits)] if bits else source.at[me[1]]
                        load = pltpu.make_async_copy(
                            origin, landed.at[place[1]], local.at[local_count.next()]
                        )
                        load.start()
                        wait = load.wait
                    waiting[number].append(wait)

        away = subsets(far)[1:]
        for number in range(len(waves)):
            send_wave(number, ((),))
        for number in range(len(waves)):
            send_wave(number, away)
        yield
        relays = []
        for number, near in enumerate(waves):
            for wait in waiting[number]:
                wait()
            place = moved(me, near)
            expert = place[1] % GROUP
            for _, _, landed, held, target in arrays:
                total = landed.at[place[1]]
                for item in subsets(far)[1:]:
                    part = landed.at[moved(place, item)[1]]
                    add_into(held.at[number], total, part, part.shape[0])
                    total = held.at[number]

                def goal(where, bits=(), target=target, expert=expert):
                    return target.at[where[0] * GROUP + expert]

                store = pltpu.make_async_copy(total, goal(me), local.at[local_count.next()])
                store.start()
                tail.append(store)
                flow = ((X_BIT, C_BIT), lambda where, total=total: total, goal, only_self)
                relay = gather_steps([flow], me, sems, count, sends)
                relays.append(relay)
                next(relay)
            yield
        for relay in relays:
            for _ in relay:
                yield

    def weight_grad(rows, grads, part):
        width = grads.shape[1]
        rows_each = part.shape[-2]
        shard_bits = part.ndim - 2
        stores = []
        for number in range(rows.shape[1] // PIECE):
            if number >= 2:
                for store in stores[number - 2]:
                    store.wait()
            held = stage.at[number % 2, :, pl.ds(0, width)]
            piece = rows[:, number * PIECE : (number + 1) * PIECE]
            held[...] = dot(piece, grads[...], ((0,), (0,))).astype(low)
            stores.append([])
            for inner in range(PIECE // rows_each):
                index = number * (PIECE // rows_each) + inner
                spot = tuple((index >> bit) % 2 for bit in reversed(range(shard_bits)))
                store = pltpu.make_async_copy(
                    held.at[pl.ds(inner * rows_each, rows_each)],
                    part.at[spot],
                    local.at[local_count.next()],
                )
                store.start()
                stores[-1].append(store)
        for store in stores[-2] + stores[-1]:
            store.wait()

    def advance(run, steps):
        for _ in range(steps):
            if next(run, "end") == "end":
                return

    experts = expert_steps()
    next(experts)
    weight_grad(attention, branch, out_part)
    out_run = block_steps(groups[1])
    next(out_run)
    loads[0].wait()
    heads_grad[...] = dot(branch[...], out_held[...], ((1,), (1,))).astype(low)

    lane = lax.broadcasted_iota(jnp.int32, (1, 128), 1)
    sides = [(lane < HD).astype(jnp.float32), (lane >= HD).astype(jnp.float32)]
    sides_low = [side.astype(low) for side in sides]
    scale = HD ** (-0.5)
    group = HEADS // KV_HEADS

    def doubled(tile):
        tile = tile.astype(jnp.float32)
        other = pltpu.roll(tile, HD, 1)
        return [
            (tile * sides[0] + other * sides[1]).astype(low),
            (other * sides[0] + tile * sides[1]).astype(low),
        ]

    for pair in range(KV_HEADS // 2):
        keys = doubled(acts[:, QD + 128 * pair : QD + 128 * (pair + 1)])
        values = doubled(acts[:, QD + KVD + 128 * pair : QD + KVD + 128 * (pair + 1)])
        query_grads = [None] * group
        key_tile = value_tile = None
        for half in range(2):
            key_total = value_total = None
            for number in range(group):
                head = (2 * pair + half) * group + number
                tile, side = head // 2, head % 2
                columns = slice(128 * tile, 128 * (tile + 1))
                query = acts[:, columns] * sides_low[side]
                grad_out = heads_grad[:, columns] * sides_low[side]
                scores = dot(query, keys[half], ((1,), (1,))) * scale
                scores = jnp.where(allowed[...] > 0.5, scores, masked_score)
                probs = jnp.exp(scores - lse[:, head : head + 1])
                grad_probs = dot(grad_out, values[half], ((1,), (1,)))
                inner = jnp.sum(grad_probs * probs, axis=1, keepdims=True)
                grad_scores = (probs * (grad_probs - inner)).astype(low)
                value_part = dot(probs.astype(low), grad_out, ((0,), (0,)))
                key_part = dot(grad_scores, query, ((0,), (0,)))
                query_part = dot(grad_scores, keys[half]) * sides[side]
                local_tile = tile - group * pair
                if query_grads[local_tile] is None:
                    query_grads[local_tile] = query_part
                else:
                    query_grads[local_tile] += query_part
                key_total = key_part if key_total is None else key_total + key_part
                value_total = value_part if value_total is None else value_total + value_part
            key_total = (key_total + pltpu.roll(key_total, HD, 1)) * sides[half]
            value_total = (value_total + pltpu.roll(value_total, HD, 1)) * sides[half]
            key_tile = key_total if key_tile is None else key_tile + key_total
            value_tile = value_total if value_tile is None else value_tile + value_total
        for number in range(group):
            tile = group * pair + number
            acts_grad[:, 128 * tile : 128 * (tile + 1)] = turned_back(
                query_grads[number] * scale, tables
            ).astype(low)
        acts_grad[:, QD + 128 * pair : QD + 128 * (pair + 1)] = turned_back(
            key_tile * scale, tables
        ).astype(low)
        acts_grad[:, QD + KVD + 128 * pair : QD + KVD + 128 * (pair + 1)] = value_tile.astype(low)
        advance(out_run, OUT_STEPS[pair])
        advance(experts, EARLY[pair])

    weight_grad(normed, acts_grad, qkv_part)
    qkv_run = block_steps(groups[0])
    next(qkv_run)
    loads[1].wait()
    grad_normed = dot(acts_grad[...], qkv_held[...], ((1,), (1,)))
    value = x[...].astype(jnp.float32)
    spread = lax.rsqrt(jnp.mean(value * value, axis=-1, keepdims=True) + norm_eps)
    normal = value * spread
    inner = grad_normed * gain[...]
    tokens_grad[...] = grad_mid[...] + spread * (
        inner - normal * jnp.mean(inner * normal, axis=-1, keepdims=True)
    )
    gain_grad = lax.dot_general(
        grad_normed * normal,
        jnp.ones((value.shape[0], 128), jnp.float32),
        (((0,), (0,)), ((), ())),
        precision=HIGH,
        preferred_element_type=jnp.float32,
    )
    column = lax.broadcasted_iota(jnp.int32, gain_grad.shape, 1)
    small_held[...] = jnp.where(
        column == E, gain_grad, small[...].astype(jnp.float32)
    ).astype(low)
    third = sum_run([tiny_flow])
    next(third)

    mixed = [(qkv_run, 1), (out_run, 1), (experts, 1), (third, 1)]
    alive = [run for run, _ in mixed]
    while alive:
        for run, turns in mixed:
            for _ in range(turns):
                if run in alive and next(run, "end") == "end":
                    alive.remove(run)
    for _ in last_steps():
        pass
    for copy in sends:
        copy.wait_send()
    for copy in tail:
        copy.wait()


def close_call(near, weights, experts, shards, reps):
    branch, acts, small = near[0], near[2], near[9]
    qkv_w, out_w = weights
    g_in, g_down = experts[:2]
    far = far_bits(shards)
    size = 4 + len(far)
    low = jnp.bfloat16
    length = branch.shape[0]

    def part(array):
        return array.shape[0] // shards, array.shape[1]

    def dense_buffer(array):
        rows, columns = part(array)
        shapes = [(2,) * (size - 1)] + [(2,) * (size - 1 - level) for level in range(size)]
        return [pltpu.VMEM(shape + (rows // 3, columns // reps), low) for shape in shapes] * 3

    def by_bits(array):
        return jax.ShapeDtypeStruct((2,) * (size - 2) + part(array), low)

    small_rows = small.shape[0] // shards
    tiny_pieces = halving_slots(2 + len(far)) + 4
    slots = 7 * (2**size - 1) + 2 * shards + 14 * 3 + 4
    vmem = pl.BlockSpec(memory_space=pltpu.VMEM)
    return pl.pallas_call(
        functools.partial(close_kernel, shards, reps),
        out_shape=[
            jax.ShapeDtypeStruct(part(qkv_w), low),
            jax.ShapeDtypeStruct(part(out_w), low),
            jax.ShapeDtypeStruct((small_rows, 128), low),
        ]
        + [
            jax.ShapeDtypeStruct((reps * GROUP,) + array.shape[1:], low) for array in (g_in, g_down)
        ]
        + [
            jax.ShapeDtypeStruct((length, D), jnp.float32),
            by_bits(qkv_w),
            by_bits(out_w),
        ],
        in_specs=[vmem] * len(near) + anywhere(6),
        out_specs=anywhere(5) + [vmem] + anywhere(2),
        scratch_shapes=dense_buffer(qkv_w)
        + dense_buffer(out_w)
        + [
            pltpu.VMEM((tiny_pieces, small_rows, 128), low),
            pltpu.VMEM(g_in.shape, low),
            pltpu.VMEM(g_down.shape, low),
            pltpu.VMEM((GROUP,) + g_in.shape[1:], low),
            pltpu.VMEM((GROUP,) + g_down.shape[1:], low),
            pltpu.VMEM(qkv_w.shape, low),
            pltpu.VMEM(out_w.shape, low),
            pltpu.VMEM((2, PIECE, qkv_w.shape[1]), low),
            pltpu.VMEM(acts.shape, low),
            pltpu.VMEM(branch.shape, low),
            pltpu.VMEM(small.shape, low),
            pltpu.SemaphoreType.DMA((slots,)),
            pltpu.SemaphoreType.DMA((slots,)),
            pltpu.SemaphoreType.DMA((7 * 2 ** (size - 1) + 64,)),
        ],
        compiler_params=pltpu.CompilerParams(
            collective_id=3, has_side_effects=True, vmem_limit_bytes=EXPERT_VMEM_BYTES
        ),
        name="close_sums",
    )(*near, *weights, *experts)


def on_device(
    shards,
    reps,
    tokens,
    segments,
    routes,
    cotangent,
    wqkv,
    wqkv_first,
    wqkv_second,
    wo,
    wo_first,
    wo_second,
    router,
    router_first,
    router_second,
    w_in,
    w_in_first,
    w_in_second,
    w_out,
    w_out_first,
    w_out_second,
    gains,
    gains_first,
    gains_second,
):
    length, width = tokens.shape
    group = HEADS // KV_HEADS
    segs = segments[0]
    rep, shard = here()
    low = jnp.bfloat16

    def cut(array):
        return array.astype(low).reshape((shards, array.shape[0] // shards) + array.shape[1:])

    small = jnp.concatenate(
        [router, gains.T, jnp.zeros((router.shape[0], 128 - E - 2), jnp.float32)], axis=1
    ).astype(low)
    mine_in = lax.dynamic_slice_in_dim(w_in, rep * GROUP, GROUP, 0).astype(low)
    mine_out = lax.dynamic_slice_in_dim(w_out, rep * GROUP, GROUP, 0).astype(low)
    qkv_w, out_w, small_w, full_in, full_out, cot_all = open_call(
        wqkv.astype(low), wo.astype(low), small, mine_in, mine_out, cotangent, shards, reps
    )
    qkv_w = qkv_w.reshape(D, -1)
    out_w = out_w.reshape(QD, D)
    small_w = small_w.reshape(D, 128)
    router_w = small_w[:, :E]
    gain_f = small_w[:, E : E + 2].astype(jnp.float32).T

    x = tokens.astype(jnp.float32)
    normed = rms_norm(x, gain_f[0]).astype(low)
    qkv = jnp.dot(normed, qkv_w, preferred_element_type=jnp.float32)
    query = (
        rotary(qkv[:, :QD].reshape(length, HEADS, HD))
        .astype(low)
        .reshape(length, KV_HEADS, group, HD)
    )
    keys = rotary(qkv[:, QD : QD + KVD].reshape(length, KV_HEADS, HD)).astype(low)
    values = qkv[:, QD + KVD :].reshape(length, KV_HEADS, HD).astype(low)
    attended, lses = attend_forward(query, keys, values, segs)
    attention = attended.reshape(length, QD)
    branch = jnp.dot(attention, out_w, preferred_element_type=jnp.float32)
    mid = x + branch
    normed2 = rms_norm(mid, gain_f[1]).astype(low)
    logits = jnp.dot(normed2, router_w, preferred_element_type=jnp.float32)
    picks = (routes[:, :, None] == jnp.arange(E, dtype=jnp.int32)[None, None, :]).any(axis=1)
    gates = jax.nn.softmax(jnp.where(picks, logits, -jnp.inf), axis=-1)

    rows, gates_all = spread_call(normed2, gates.T)
    gate = jnp.stack(
        [
            lax.dynamic_index_in_dim(gates_all, flip(rep, 0) * GROUP + shard % GROUP, 1, False),
            lax.dynamic_index_in_dim(gates_all, rep * GROUP + shard % GROUP, 1, False),
        ]
    ).reshape(2, -1, 1)
    moe, grad_normed2, marks, _, _, grad_in, grad_down, far_in, far_down = expert_call(
        rows, cot_all, gate, full_in.reshape(2, D, 2 * H), full_out.reshape(2, H, D), shards
    )
    marks = marks.astype(jnp.float32)
    grad_gates = marks[:, :E] + marks[:, E : 2 * E]
    mixed = (mid + moe.astype(jnp.float32)).astype(low)

    grad_logits = gates * (grad_gates - jnp.sum(grad_gates * gates, axis=-1, keepdims=True))
    grad_router = jnp.dot(normed2.astype(jnp.float32).T, grad_logits, precision=HIGH)
    grad_normed2 = grad_normed2.astype(jnp.float32) + jnp.dot(
        grad_logits, router_w.astype(jnp.float32).T, precision=HIGH
    )
    cot = cotangent.astype(jnp.float32)
    grad_mid_norm, grad_gain2 = norm_back(mid, gain_f[1], grad_normed2)
    grad_mid = cot + grad_mid_norm
    grad_branch = grad_mid.astype(low)
    grad_small = jnp.concatenate(
        [
            grad_router,
            jnp.zeros((D, 1), jnp.float32),
            grad_gain2[:, None],
            jnp.zeros((D, 128 - E - 2), jnp.float32),
        ],
        axis=1,
    ).astype(low)
    acts = jnp.concatenate(
        [query.reshape(length, QD), keys.reshape(length, KVD), values.reshape(length, KVD)], axis=1
    )
    lse_columns = jnp.pad(lses.reshape(HEADS, length).T, ((0, 0), (0, 128 - HEADS)))
    places = jnp.arange(length, dtype=jnp.int32)
    allowed = (places[:, None] >= places[None, :]) & (segs[:, None] == segs[None, :])
    cosine, sine, _ = angle_tables(length, HD)
    cosine, sine = cosine[:, 0], sine[:, 0]
    blank = jnp.zeros_like(sine)
    grad_qkv_w, grad_out_w, grad_small, grad_in_all, grad_down_all, tokens_grad, _, _ = close_call(
        (
            grad_branch,
            attention,
            acts,
            lse_columns,
            allowed.astype(jnp.float32),
            normed,
            tokens,
            grad_mid,
            gain_f[:1],
            grad_small,
            jnp.concatenate([cosine] * 4, axis=1),
            jnp.concatenate([-sine, blank] * 2, axis=1),
            jnp.concatenate([blank, sine] * 2, axis=1),
        ),
        (qkv_w, out_w),
        (cut(grad_in), cut(grad_down), far_in, far_down),
        shards,
        reps,
    )
    grad_small = grad_small.astype(jnp.float32)
    grad_router = grad_small[:, :E]
    grad_gains = grad_small[:, E : E + 2].T
    qkv_m, qkv_v, qkv_new = adamw(
        wqkv, wqkv_first, wqkv_second, grad_qkv_w.astype(jnp.float32), 3.0 * D ** (-0.5), decay_rate
    )
    out_m, out_v, out_new = adamw(
        wo, wo_first, wo_second, grad_out_w.astype(jnp.float32), 3.0 * (QD // 64) ** (-0.5), decay_rate
    )
    rout_m, rout_v, rout_new = adamw(
        router, router_first, router_second, grad_router, 1.5 * D ** (-0.5), decay_rate
    )
    in_m, in_v, in_new = adamw(
        w_in, w_in_first, w_in_second, grad_in_all.astype(jnp.float32), 3.0 * D ** (-0.5), decay_rate
    )
    down_m, down_v, down_new = adamw(
        w_out,
        w_out_first,
        w_out_second,
        grad_down_all.astype(jnp.float32),
        3.0 * (H // 16) ** (-0.5),
        decay_rate,
    )
    gain_m, gain_v, gain_new = adamw(gains, gains_first, gains_second, grad_gains, 0.6, 0.0)
    return (
        mixed,
        tokens_grad,
        qkv_m,
        qkv_v,
        qkv_new,
        out_m,
        out_v,
        out_new,
        rout_m,
        rout_v,
        rout_new,
        in_m,
        in_v,
        in_new,
        down_m,
        down_v,
        down_new,
        gain_m,
        gain_v,
        gain_new,
    )


def solution(mesh):
    in_specs = (
        P(("rep", "shard"), None),
        P(("rep", "shard"), None),
        P(("rep", "shard"), None),
        P(("rep", "shard"), None),
        P("shard", None),
        P("shard", None),
        P("shard", None),
        P("shard", None),
        P("shard", None),
        P("shard", None),
        P("shard", None),
        P("shard", None),
        P("shard", None),
        P(None, "shard", None),
        P(None, "shard", None),
        P(None, "shard", None),
        P(None, "shard", None),
        P(None, "shard", None),
        P(None, "shard", None),
        P(None, "shard"),
        P(None, "shard"),
        P(None, "shard"),
    )
    out_specs = (
        P(("rep", "shard"), None),
        P(("rep", "shard"), None),
        P("shard", None),
        P("shard", None),
        P("shard", None),
        P("shard", None),
        P("shard", None),
        P("shard", None),
        P("shard", None),
        P("shard", None),
        P("shard", None),
        P(None, "shard", None),
        P(None, "shard", None),
        P(None, "shard", None),
        P(None, "shard", None),
        P(None, "shard", None),
        P(None, "shard", None),
        P(None, "shard"),
        P(None, "shard"),
        P(None, "shard"),
    )
    return jax.shard_map(
        functools.partial(on_device, mesh.shape["shard"], mesh.shape["rep"]), mesh=mesh, in_specs=in_specs, out_specs=out_specs, check_vma=False
    )
```
